32 devices in a mesh: dp: 16 (over z, y, core), section: 2 (over x).
Axes of the slice: x: 2, y: 2, z: 4, core: 2. Of those that a mesh axis runs over, the one named last changes fastest.
Arguments:
- tokens: bfloat16 [16, 1024, 768], P('dp'), may hold values from -6 to 6
- cotangent: bfloat16 [16, 1024, 768], P('dp'), may hold values from -6 to 6
- norm_gains: bfloat16 [2, 2, 768], P('section'), may hold values from 0.5 to 1.5
- norm_shifts: bfloat16 [2, 2, 768], P('section'), may hold values from -1.75 to 1.75
- in_weight: bfloat16 [2, 768, 2304], P('section'), may hold values from -0.21875 to 0.21875
- in_bias: bfloat16 [2, 3, 768], P('section'), may hold values from -1.75 to 1.75
- short_taps: bfloat16 [2, 3, 3, 768], P('section'), may hold values from -3.5 to 3.5
- long_filter: bfloat16 [2, 2, 1024, 768], P('section'), may hold values from -1.1 to 1.1
- skip_gains: bfloat16 [2, 2, 768], P('section'), may hold values from -3 to 3
- out_weight: bfloat16 [2, 768, 768], P('section'), may hold values from -0.21875 to 0.21875
- out_bias: bfloat16 [2, 768], P('section'), may hold values from -1.75 to 1.75
- up_weight: bfloat16 [2, 768, 3072], P('section'), may hold values from -0.21875 to 0.21875
- up_bias: bfloat16 [2, 3072], P('section'), may hold values from -1.75 to 1.75
- down_weight: bfloat16 [2, 3072, 768], P('section'), may hold values from -0.109375 to 0.109375
- down_bias: bfloat16 [2, 768], P('section'), may hold values from -1.75 to 1.75
Outputs:
- stream_out: bfloat16 [16, 1024, 768], P('dp', 'section')
- grad_tokens: float32 [16, 1024, 768], P('dp', 'section')
- grad_norm_gains: float32 [2, 2, 768], P('section', None, 'dp')
- grad_norm_shifts: float32 [2, 2, 768], P('section', None, 'dp')
- grad_in_weight: float32 [2, 768, 2304], P('section', 'dp')
- grad_in_bias: float32 [2, 3, 768], P('section', None, 'dp')
- grad_short_taps: float32 [2, 3, 3, 768], P('section', None, None, 'dp')
- grad_long_filter: float32 [2, 2, 1024, 768], P('section', None, 'dp')
- grad_skip_gains: float32 [2, 2, 768], P('section', None, 'dp')
- grad_out_weight: float32 [2, 768, 768], P('section', 'dp')
- grad_out_bias: float32 [2, 768], P('section', 'dp')
- grad_up_weight: float32 [2, 768, 3072], P('section', 'dp')
- grad_up_bias: float32 [2, 3072], P('section', 'dp')
- grad_down_weight: float32 [2, 3072, 768], P('section', None, 'dp')
- grad_down_bias: float32 [2, 768], P('section', 'dp')
The draws below stay inside these ranges and needn't reach their ends.
All inputs are finite; a program needn't handle non-finite values.
Results may differ from the reference program's by a relative error of at most 0.025.
Values may be sent and summed in bfloat16 or wider, within the bound.
A program may use at most 576 MiB of HBM per device.

```python
import jax
import jax.numpy as jnp
from jax import lax

D = 768
FF = 3072
SEQ = 1024
LAYERS = 2
SEQS = 16


def draw_long_filter(key, part):
    key = jax.random.fold_in(key, 11)
    rate_key, noise_key = jax.random.split(key)
    slow_rate = 0.5 / SEQ
    fast_rate = 1.0 / 30.0
    rates = jnp.exp(jax.random.uniform(rate_key, (LAYERS, 2, 1, D), jnp.float32, jnp.log(slow_rate), jnp.log(fast_rate)))
    noise = jax.random.truncated_normal(noise_key, -4.0, 4.0, (LAYERS, 2, SEQ, D), jnp.float32)
    lags = jnp.arange(SEQ, dtype=jnp.float32).reshape(1, 1, SEQ, 1)
    return (noise * jnp.sqrt(2.0 * rates) * jnp.exp(-rates * lags)).astype(jnp.bfloat16)


def block_scale(stream_key, shape, pieces, smallest, high):
    level, own = 1.0, jax.random.fold_in(stream_key, 6)
    for position, blocks in pieces:
        steps = jnp.exp(jax.random.uniform(jax.random.fold_in(own, position), (blocks,), jnp.float32, smallest / len(pieces), high / len(pieces)))
        level = level * jnp.repeat(steps, shape[position] // blocks).reshape([-1 if axis == position else 1 for axis in range(len(shape))])
    return level


def scatter_about(key, shape, width, limit, cuts=(), kind=jnp.bfloat16):
    drawn = width * jax.random.normal(key, shape, jnp.float32)
    if cuts:
        drawn = drawn * block_scale(key, shape, cuts, -0.22, 0.18)
    return jnp.clip(drawn, -limit, limit).astype(kind)


def setup_inputs(seed: int = 0) -> dict:
    keys = jax.random.split(jax.random.key(seed), 16)
    return {
        "tokens": scatter_about(keys[0], (SEQS, SEQ, D), 1.0, 6.0, ((0, 16),)),
        "cotangent": scatter_about(keys[1], (SEQS, SEQ, D), 1.0, 6.0, ((0, 16),)),
        "norm_gains": jnp.clip(1.0 + 0.1 * jax.random.normal(keys[2], (LAYERS, 2, D), jnp.float32), 0.5, 1.5).astype(jnp.bfloat16),
        "norm_shifts": scatter_about(keys[3], (LAYERS, 2, D), 0.3, 1.75, ((0, 2),)),
        "in_weight": scatter_about(keys[4], (LAYERS, D, 3 * D), D ** -0.5, 0.21875, ((0, 2),)),
        "in_bias": scatter_about(keys[5], (LAYERS, 3, D), 0.3, 1.75, ((0, 2),)),
        "short_taps": scatter_about(keys[6], (LAYERS, 3, 3, D), 0.6, 3.5, ((0, 2),)),
        "long_filter": draw_long_filter(jax.random.fold_in(keys[15], 71), 0),
        "skip_gains": scatter_about(keys[8], (LAYERS, 2, D), 0.5, 3.0, ((0, 2),)),
        "out_weight": scatter_about(keys[9], (LAYERS, D, D), D ** -0.5, 0.21875, ((0, 2),)),
        "out_bias": scatter_about(keys[10], (LAYERS, D), 0.3, 1.75, ((0, 2),)),
        "up_weight": scatter_about(keys[11], (LAYERS, D, FF), D ** -0.5, 0.21875, ((0, 2),)),
        "up_bias": scatter_about(keys[12], (LAYERS, FF), 0.3, 1.75, ((0, 2),)),
        "down_weight": scatter_about(keys[13], (LAYERS, FF, D), FF ** -0.5, 0.109375, ((0, 2),)),
        "down_bias": scatter_about(keys[14], (LAYERS, D), 0.3, 1.75, ((0, 2),)),
    }


@jax.custom_vjp
def low(v):
    return lax.optimization_barrier(v.astype(jnp.bfloat16)).astype(jnp.float32)

@jax.custom_vjp
def low_back(v):
    return v

def low_keep(v):
    return (low(v), None)

def low_pass(kept, grad):
    return (grad,)

def back_keep(v):
    return (v, None)

def back_low(kept, grad):
    return (low(grad),)
low.defvjp(low_keep, low_pass)
low_back.defvjp(back_keep, back_low)
eps = 1e-05
highest = lax.Precision.HIGHEST

def norm_affine(rows, gain_row, shift_row):
    average = lax.optimization_barrier(jnp.mean(rows, axis=-1, keepdims=True))
    centered = rows - average
    variance = lax.optimization_barrier(jnp.mean(centered * centered, axis=-1, keepdims=True))
    return centered * lax.rsqrt(variance + eps) * gain_row + shift_row

def long_conv(signal, response):
    points = 2 * signal.shape[0]
    spectrum = jnp.fft.rfft(signal, n=points, axis=0) * jnp.fft.rfft(response, n=points, axis=0)
    return jnp.fft.irfft(spectrum, n=points, axis=0)[:signal.shape[0]]

def precise_dot(first_op, second_op):
    return jnp.dot(first_op, second_op, precision=highest)

def hyena_layer(residual, layer_weights, is_first):
    gain_rows, shift_rows, weight_in, bias_in, taps_all, responses, skip_rows, weight_out, bias_out, weight_up, bias_up, weight_down, bias_down = layer_weights
    total_rows = residual.shape[0]
    if not is_first:
        residual = low_back(low(residual))
    normed = low(norm_affine(residual, gain_rows[0], shift_rows[0]))
    projected = low_back(precise_dot(normed, weight_in) + bias_in.reshape(-1))
    padded = jnp.concatenate([jnp.zeros((2, projected.shape[1]), projected.dtype), projected], axis=0)
    taps_flat = taps_all.reshape(3, -1)
    short_filter_apply = taps_flat[0] * projected + taps_flat[1] * padded[1:total_rows + 1] + taps_flat[2] * padded[:total_rows]
    relay_state, gate_leading, gate_trailing = jnp.split(short_filter_apply, 3, axis=1)
    input_leading = relay_state * gate_leading
    leading_section = long_conv(input_leading, responses[0]) + skip_rows[0] * input_leading
    input_trailing = leading_section * gate_trailing
    trailing_section = long_conv(input_trailing, responses[1]) + skip_rows[1] * input_trailing
    branch = low_back(precise_dot(low(trailing_section), weight_out) + bias_out)
    residual_mid = residual + branch
    normed_two = low(norm_affine(residual_mid, gain_rows[1], shift_rows[1]))
    hidden = low_back(precise_dot(normed_two, weight_up) + bias_up)
    activation = low(jax.nn.gelu(hidden, approximate=False))
    mlp_out = low_back(precise_dot(activation, weight_down) + bias_down)
    return residual_mid + mlp_out

def forward(token_rows, weights):
    residual = token_rows
    for layer_no in range(LAYERS):
        layer_weights = tuple((stacked[layer_no] for stacked in weights))
        residual = hyena_layer(residual, layer_weights, layer_no == 0)
    return residual

def reference(tokens, cotangent, norm_gains, norm_shifts, in_weight, in_bias, short_taps, long_filter, skip_gains, out_weight, out_bias, up_weight, up_bias, down_weight, down_bias):
    weights = tuple((stacked.astype(jnp.float32) for stacked in (norm_gains, norm_shifts, in_weight, in_bias, short_taps, long_filter, skip_gains, out_weight, out_bias, up_weight, up_bias, down_weight, down_bias)))
    zero_grads = tuple((jnp.zeros_like(stacked) for stacked in weights))

    def per_sequence(totals, sequence_item):
        token_rows, cot_rows = sequence_item
        result, pullback = jax.vjp(forward, token_rows.astype(jnp.float32), weights)
        grad_rows, grad_weights = pullback(cot_rows.astype(jnp.float32))
        totals = tuple((running + fresh for running, fresh in zip(totals, grad_weights)))
        return (totals, (result.astype(jnp.bfloat16), grad_rows))
    totals, (outputs, grad_tokens) = lax.scan(per_sequence, zero_grads, (tokens, cotangent))
    grad_gains, grad_shifts, grad_in_weight, grad_in_bias, grad_taps, grad_filter, grad_skips, grad_out_weight, grad_out_bias, grad_up_weight, grad_up_bias, grad_down_weight, grad_down_bias = totals
    return (outputs, grad_tokens, grad_gains, grad_shifts, grad_in_weight, grad_in_bias, grad_taps, grad_filter, grad_skips, grad_out_weight, grad_out_bias, grad_up_weight, grad_up_bias, grad_down_weight, grad_down_bias)
```

```python
import functools
import math

import jax
import jax.numpy as jnp
import ml_dtypes
import numpy as np
from jax import lax
from jax.experimental import pallas as pl
from jax.experimental.pallas import tpu as pltpu
from jax.sharding import PartitionSpec as P

CH = 256
FT = 512
CARRY = 8
f32, bf16 = jnp.float32, jnp.bfloat16
VMEM_LIMIT = 60 * 1024 * 1024
ANY = pl.BlockSpec(memory_space=pl.ANY)
SMEM = pl.BlockSpec(memory_space=pltpu.SMEM)
VM = pl.BlockSpec(memory_space=pltpu.VMEM)

GAIN, SHIFT, INB, TAP, SKIP, OUTB, DOWNB, UPB = 0, 2, 4, 7, 16, 18, 19, 20


def tables():
    order = np.concatenate([np.arange(0, CH, 2), np.arange(1, CH, 2)])
    angle = np.pi * ((2 * order[:, None] + 1) * np.arange(CH)[None] % (4 * CH)) / (2 * CH)
    cos, sin = np.cos(angle), np.sin(angle)
    sign = np.where(order % 2 == 0, 1.0, -1.0)[:, None]
    spread = np.concatenate([cos, -sin], 0)
    turned = np.concatenate([sign * sin, sign * cos], 0)
    as_low = lambda t: jnp.asarray(t.astype(ml_dtypes.bfloat16))
    return as_low(spread), as_low(spread.T / CH), as_low(np.concatenate([turned, spread], 1))


def dot(x, y):
    return jnp.dot(x, y, preferred_element_type=f32)


def dot_nt(x, y):
    return lax.dot_general(x, y, (((1,), (1,)), ((), ())), preferred_element_type=f32)


def rows_at(index, size):
    return pl.ds(pl.multiple_of(index * size, size), size)


def for_rows(total, size, step):
    def run(i, carry):
        step(pl.multiple_of(i * size, size))
        return carry

    lax.fori_loop(0, total // size, run, 0)


def normalize(rows):
    average = jnp.mean(rows, axis=-1, keepdims=True)
    centered = rows - average
    scale = lax.rsqrt(jnp.mean(centered * centered, axis=-1, keepdims=True) + 1e-05)
    return centered * scale, scale


def norm_back(z, gain, unit, scale):
    w = z * gain
    return (
        w - jnp.mean(w, axis=-1, keepdims=True) - unit * jnp.mean(w * unit, axis=-1, keepdims=True)
    ) * scale


def gelu_pair(u):
    t = 1.0 / (1.0 + (0.3275911 * math.sqrt(0.5)) * jnp.abs(u))
    series = t * (
        0.5 * 0.254829592
        + t * (0.5 * -0.284496736 + t * (0.5 * 1.421413741 + t * (0.5 * -1.453152027 + t * (0.5 * 1.061405429))))
    )
    bell = jnp.exp(-0.5 * (u * u))
    tail = series * bell
    phi_sum = jnp.where(u >= 0, 1.0 - tail, tail)
    return u * phi_sum, phi_sum + u * (bell * (1.0 / math.sqrt(2.0 * math.pi)))


def mix_spectra(left, right, out, low, high, left_of, conj):
    width = out.shape[1] // 2

    def tile(i, carry):
        r = pl.multiple_of(i * 16, 16)
        for half in range(2):
            cols = slice(half * width, (half + 1) * width)

            def term(j, acc):
                k = left_of(j)
                ar = left[k, pl.ds(r, 16), cols].astype(f32)
                ai = left[k, pl.ds(CH + r, 16), cols].astype(f32)
                br = right[j, pl.ds(r, 16), cols].astype(f32)
                bi = right[j, pl.ds(CH + r, 16), cols].astype(f32)
                if conj:
                    return acc[0] + (ar * br + ai * bi), acc[1] + (ar * bi - ai * br)
                return acc[0] + (ar * br - ai * bi), acc[1] + (ar * bi + ai * br)

            zero = jnp.zeros((16, width), f32)
            real, imag = lax.fori_loop(low, high, term, (zero, zero))
            out[pl.ds(r, 16), cols] = real.astype(out.dtype)
            out[pl.ds(CH + r, 16), cols] = imag.astype(out.dtype)
        return carry

    lax.fori_loop(0, CH // 16, tile, 0)


def forward_kernel(pieces, n_state, info, par, *refs):
    (tokens, arrived, filt, win, wout, wup, wdown, spread_h, back_h, pair_h) = refs[:10]
    refs = refs[10 + n_state :]
    out_h, aS, hS, pS, y1S, ybS, mS, nS, eS, dS, s1S, s2S, k1S, k2S, tailS = refs[:15]
    (
        hb, ab, winb, woutb, wupb, wdownb, spread, back, pair, wn1, wn2, k1, k2, s1, s2,
        pb, plow, g2b, sf, sb, yspec, y1b, y1low, yb, mb, nb, ub, eb, db, ob, outb, sem, osem,
    ) = refs[15:]
    seg, active, first = info[0], info[1], info[2]
    D = hb.shape[1]
    FF = wupb.shape[1]
    here = rows_at(seg, CH)

    def cp(src, dst, k):
        return pltpu.make_async_copy(src, dst, sem.at[k])

    def put(src, dst, k):
        c = pltpu.make_async_copy(src, dst, osem.at[k])
        c.start()
        return c

    @pl.when(active == 1)
    def _():
        @pl.when(first == 1)
        def _():
            cp(tokens.at[here], hb, 0).start()

        @pl.when(first == 0)
        def _():
            cp(arrived, hb, 0).start()

        cp(win, winb, 1).start()
        cp(pair_h, pair, 2).start()

        @pl.when(seg == 0)
        def _():
            cp(filt.at[0, pl.ds(0, CH)], wn1.at[pl.ds(CH, CH)], 3).start()
            cp(filt.at[1, pl.ds(0, CH)], wn2.at[pl.ds(CH, CH)], 4).start()
            wn1[pl.ds(0, CH), :] = jnp.zeros((CH, D), bf16)
            wn2[pl.ds(0, CH), :] = jnp.zeros((CH, D), bf16)
            pb[pl.ds(0, CARRY), :] = jnp.zeros((CARRY, 3 * D), f32)

        @pl.when(seg > 0)
        def _():
            before = pl.ds(pl.multiple_of((seg - 1) * CH, CH), 2 * CH)
            cp(filt.at[0, before], wn1, 3).start()
            cp(filt.at[1, before], wn2, 4).start()
            cp(tailS, pb.at[pl.ds(0, CARRY)], 5).start()

        cp(spread_h, spread, 6).start()
        cp(back_h, back, 7).start()
        cp(arrived, hb, 0).wait()
        back_h_put = put(hb, hS.at[here], 0)

        def ln1(r):
            unit, _ = normalize(hb[pl.ds(r, 64), :].astype(f32))
            ab[pl.ds(r, 64), :] = (unit * par[GAIN : GAIN + 1, :] + par[SHIFT : SHIFT + 1, :]).astype(bf16)

        for_rows(CH, 64, ln1)
        a_put = put(ab, aS.at[here], 1)
        cp(win, winb, 1).wait()
        for j in range(pieces - 1):

            @pl.when(j < seg)
            def _(j=j):
                for k, (src, dst) in enumerate(((k1S, k1), (s1S, s1), (k2S, k2), (s2S, s2))):
                    cp(src.at[j], dst.at[j], 8 + 4 * j + k).start()

        base = 8 + 4 * pieces
        cp(wout, woutb, base).start()
        cp(wup, wupb, base + 1).start()
        for b in range(3):
            cols = slice(b * D, (b + 1) * D)
            pb[pl.ds(CARRY, CH), cols] = dot(ab[...], winb[:, cols]) + par[INB + b : INB + b + 1, :]
        cp(wdown, wdownb, base + 2).start()

        @pl.when(seg > 0)
        def _():
            cp(tailS, pb.at[pl.ds(0, CARRY)], 5).wait()

        def short(r):
            got = []
            for b in range(3):
                cols = slice(b * D, (b + 1) * D)
                rows = pb[pl.ds(r, 32 + CARRY), cols]
                now = rows[CARRY:]
                plow[pl.ds(r, 32), cols] = now.astype(bf16)
                t = [par[TAP + 3 * i + b : TAP + 3 * i + b + 1, :] for i in range(3)]
                got.append(t[0] * now + t[1] * rows[CARRY - 1 : -1] + t[2] * rows[CARRY - 2 : -2])
            g2b[pl.ds(r, 32), :] = got[2]
            lead = got[0] * got[1]
            sf[pl.ds(r, 32), :] = lead
            sb[pl.ds(r, 32), :] = lead.astype(bf16)

        for_rows(CH, 32, short)
        p_put = put(plow, pS.at[here], 2)
        tail_put = put(pb.at[pl.ds(CH, CARRY)], tailS, 3)
        cp(pair_h, pair, 2).wait()
        cp(spread_h, spread, 6).wait()
        cp(back_h, back, 7).wait()
        cp(filt.at[0, pl.ds(0, CH)], wn1.at[pl.ds(CH, CH)], 3).wait()
        cp(filt.at[1, pl.ds(0, CH)], wn2.at[pl.ds(CH, CH)], 4).wait()

        @pl.when(seg > 0)
        def _():
            cp(filt.at[0, pl.ds(0, CH)], wn1.at[pl.ds(CH, CH)], 3).wait()
            cp(filt.at[1, pl.ds(0, CH)], wn2.at[pl.ds(CH, CH)], 4).wait()

        for j in range(pieces - 1):

            @pl.when(j < seg)
            def _(j=j):
                for k, (src, dst) in enumerate(((k1S, k1), (s1S, s1), (k2S, k2), (s2S, s2))):
                    cp(src.at[j], dst.at[j], 8 + 4 * j + k).wait()

        k1[seg] = dot(pair[...], wn1[...]).astype(bf16)
        k2[seg] = dot(pair[...], wn2[...]).astype(bf16)
        puts = [put(k1.at[seg], k1S.at[seg], 4), put(k2.at[seg], k2S.at[seg], 5)]
        s1[seg] = dot(spread[...], sb[...]).astype(bf16)
        puts.append(put(s1.at[seg], s1S.at[seg], 6))
        mix_spectra(k1, s1, yspec, 0, seg + 1, lambda j: seg - j, False)
        y1b[...] = dot(back[...], yspec[...])

        def second(r):
            rows = pl.ds(r, 64)
            y = y1b[rows, :] + par[SKIP : SKIP + 1, :] * sf[rows, :]
            y1low[rows, :] = y.astype(bf16)
            trail = y * g2b[rows, :]
            sf[rows, :] = trail
            sb[rows, :] = trail.astype(bf16)

        for_rows(CH, 64, second)
        puts.append(put(y1low, y1S.at[here], 7))
        s2[seg] = dot(spread[...], sb[...]).astype(bf16)
        puts.append(put(s2.at[seg], s2S.at[seg], 8))
        mix_spectra(k2, s2, yspec, 0, seg + 1, lambda j: seg - j, False)
        yb[...] = (dot(back[...], yspec[...]) + par[SKIP + 1 : SKIP + 2, :] * sf[...]).astype(bf16)
        puts.append(put(yb, ybS.at[here], 9))
        cp(wout, woutb, base).wait()
        mb[...] = dot(yb[...], woutb[...])

        def ln2(r):
            rows = pl.ds(r, 64)
            mid = hb[rows, :].astype(f32) + (mb[rows, :] + par[OUTB : OUTB + 1, :])
            mb[rows, :] = mid
            unit, _ = normalize(mid)
            nb[rows, :] = (unit * par[GAIN + 1 : GAIN + 2, :] + par[SHIFT + 1 : SHIFT + 2, :]).astype(bf16)
            ob[rows, :] = mid + par[DOWNB : DOWNB + 1, :]

        for_rows(CH, 64, ln2)
        puts.append(put(mb, mS.at[here], 10))
        puts.append(put(nb, nS.at[here], 11))
        cp(wup, wupb, base + 1).wait()
        cp(wdown, wdownb, base + 2).wait()
        tiles = FF // FT

        def up(k):
            return dot(nb[...], wupb[:, k * FT : (k + 1) * FT])

        def act(k):
            u = ub[k % 2]
            per_row = D // FT if D % FT == 0 else 0
            u = u + bias_up(k)
            e, d = gelu_pair(u)
            eb[:, k * FT : (k + 1) * FT] = e.astype(bf16)
            db[:, k * FT : (k + 1) * FT] = d.astype(bf16)

        def bias_up(k):
            parts, at = [], k * FT
            while at < (k + 1) * FT:
                row, col = at // D, at % D
                wide = min(D - col, (k + 1) * FT - at)
                parts.append(par[UPB + row : UPB + row + 1, col : col + wide])
                at += wide
            return parts[0] if len(parts) == 1 else jnp.concatenate(parts, axis=1)

        def down(k):
            ob[...] += dot(eb[:, k * FT : (k + 1) * FT], wdownb[k * FT : (k + 1) * FT, :])

        ub[0] = up(0)
        for k in range(tiles):
            if k + 1 < tiles:
                ub[(k + 1) % 2] = up(k + 1)
            act(k)
            if k >= 1:
                down(k - 1)
        down(tiles - 1)
        puts.append(put(eb, eS.at[here], 12))
        puts.append(put(db, dS.at[here], 13))
        outb[...] = ob[...].astype(bf16)
        puts.append(put(outb, out_h, 14))
        for c in [back_h_put, a_put, p_put, tail_put] + puts:
            c.wait()


def forward_call(info, par, tokens, arrived, filt, win, wout, wup, wdown, tabs, state):
    T, D = tokens.shape
    FF = wup.shape[1]
    pieces = T // CH
    spec3 = (pieces, 2 * CH, D)
    shapes = [
        ((CH, D), bf16),
        ((T, D), bf16), ((T, D), bf16), ((T, 3 * D), bf16), ((T, D), bf16), ((T, D), bf16), ((T, D), f32),
        ((T, D), bf16), ((T, FF), bf16), ((T, FF), bf16),
        (spec3, bf16), (spec3, bf16), (spec3, bf16), (spec3, bf16),
        ((CARRY, 3 * D), f32),
    ]
    out_shape = [jax.ShapeDtypeStruct(*s) for s in shapes]
    n_state = 0 if state is None else len(shapes) - 1
    V = pltpu.VMEM
    scratch = [
        V((CH, D), bf16), V((CH, D), bf16), V(win.shape, bf16), V(wout.shape, bf16), V(wup.shape, bf16),
        V(wdown.shape, bf16), V((2 * CH, CH), bf16), V((CH, 2 * CH), bf16), V((2 * CH, 2 * CH), bf16),
        V((2 * CH, D), bf16), V((2 * CH, D), bf16), V(spec3, bf16), V(spec3, bf16), V(spec3, bf16), V(spec3, bf16),
        V((CARRY + CH, 3 * D), f32), V((CH, 3 * D), bf16), V((CH, D), f32), V((CH, D), f32), V((CH, D), bf16),
        V((2 * CH, D), bf16), V((CH, D), f32), V((CH, D), bf16), V((CH, D), bf16), V((CH, D), f32), V((CH, D), bf16),
        V((2, CH, FT), f32), V((CH, FF), bf16), V((CH, FF), bf16), V((CH, D), f32), V((CH, D), bf16),
        pltpu.SemaphoreType.DMA((8 + 4 * pieces + 3,)),
        pltpu.SemaphoreType.DMA((15,)),
    ]
    return pl.pallas_call(
        functools.partial(forward_kernel, pieces, n_state),
        out_shape=out_shape,
        in_specs=[SMEM, VM] + [ANY] * (10 + n_state),
        out_specs=[ANY] * len(shapes),
        scratch_shapes=scratch,
        input_output_aliases={12 + i: 1 + i for i in range(n_state)},
        compiler_params=pltpu.CompilerParams(vmem_limit_bytes=VMEM_LIMIT),
        cost_estimate=pl.CostEstimate(flops=2 * CH * (4 * D * D + 2 * D * FF), bytes_accessed=30 << 20, transcendentals=0),
        name="forward_chunk",
    )(info, par, tokens, arrived, filt, win, wout, wup, wdown, *tabs, *(state or ()))


def fold_rows(x):
    return jnp.sum(x.reshape(x.shape[0] // 8, 8, x.shape[1]), axis=0)


def pieces_of(at, wide, D):
    spans, off = [], 0
    while off < wide:
        row, col = (at + off) // D, (at + off) % D
        size = min(D - col, wide - off)
        spans.append((row, col, off, size))
        off += size
    return spans


def backward_kernel(pieces, n_state, info, par, *refs):
    (cots, arrived, win, wout, wup, wdown, spread_h, back_h, hS, pS, y1S, mS, dS, k1S, k2S) = refs[:15]
    refs = refs[15 + n_state :]
    out_h, outf_h, gdS, guS, goS, gpS, g1S, g2S, headS, smallS = refs[:10]
    (
        gdb, winb, woutb, wupb, wdownb, spread, back, k1, k2, g1, g2, db, hb, mb, pb, y1b,
        tb, gub, gnb, gmb, gob, gyb, gylow, gsb, zspec, gy1b, gqb, gpb, outb, outfb, small, sem, osem,
    ) = refs[10:]
    seg, active, last = info[0], info[1], info[2]
    D = hb.shape[1]
    FF = wupb.shape[1]
    here = rows_at(seg, CH)

    def cp(src, dst, k):
        return pltpu.make_async_copy(src, dst, sem.at[k])

    def put(src, dst, k):
        c = pltpu.make_async_copy(src, dst, osem.at[k])
        c.start()
        return c

    def add_small(k, x, cols=slice(None)):
        small[k, :, cols] += fold_rows(x)

    @pl.when(active == 1)
    def _():
        fresh = seg == pieces - 1

        @pl.when(last == 1)
        def _():
            cp(cots.at[here], gdb, 0).start()

        @pl.when(last == 0)
        def _():
            cp(arrived, gdb, 0).start()

        cp(wdown, wdownb, 1).start()
        cp(dS.at[here], db, 2).start()
        cp(wup, wupb, 3).start()
        cp(mS.at[here], mb, 4).start()

        @pl.when(fresh)
        def _():
            small[...] = jnp.zeros(small.shape, f32)
            gqb[pl.ds(CH, CARRY), :] = jnp.zeros((CARRY, 3 * D), f32)

        @pl.when(jnp.logical_not(fresh))
        def _():
            cp(smallS, small, 5).start()
            cp(headS, gqb.at[pl.ds(CH, CARRY)], 6).start()

        cp(arrived, gdb, 0).wait()
        puts = [put(gdb, gdS.at[here], 0)]

        @pl.when(jnp.logical_not(fresh))
        def _():
            cp(smallS, small, 5).wait()
            cp(headS, gqb.at[pl.ds(CH, CARRY)], 6).wait()

        cp(wdown, wdownb, 1).wait()
        cp(dS.at[here], db, 2).wait()
        cp(wout, woutb, 7).start()
        cp(spread_h, spread, 8).start()
        cp(back_h, back, 9).start()
        for j in range(pieces):

            @pl.when(j > seg)
            def _(j=j):
                cp(g2S.at[j], g2.at[j], 16 + 4 * j).start()
                cp(g1S.at[j], g1.at[j], 16 + 4 * j + 1).start()

            @pl.when(j < pieces - seg)
            def _(j=j):
                cp(k2S.at[j], k2.at[j], 16 + 4 * j + 2).start()
                cp(k1S.at[j], k1.at[j], 16 + 4 * j + 3).start()

        @pl.when(seg == 0)
        def _():
            pb[pl.ds(0, 16), :] = jnp.zeros((16, 3 * D), bf16)
            cp(pS.at[pl.ds(0, CH)], pb.at[pl.ds(16, CH)], 10).start()

        @pl.when(seg > 0)
        def _():
            cp(pS.at[pl.ds(pl.multiple_of(seg * CH - 16, 16), CH + 16)], pb, 10).start()

        cp(y1S.at[here], y1b, 11).start()
        cp(win, winb, 12).start()
        cp(hS.at[here], hb, 13).start()
        tiles = FF // FT

        def down(k):
            return dot_nt(gdb[...], wdownb[k * FT : (k + 1) * FT, :])

        def act(k):
            cols = slice(k * FT, (k + 1) * FT)
            gu = (db[:, cols].astype(f32) * tb[k % 2]).astype(bf16)
            gub[:, cols] = gu
            total = fold_rows(gu.astype(f32))
            for row, col, off, size in pieces_of(k * FT, FT, D):
                small[UPB + row, :, col : col + size] += total[:, off : off + size]

        def up(k):
            part = dot_nt(gub[:, k * FT : (k + 1) * FT], wupb[:, k * FT : (k + 1) * FT])
            if k == 0:
                gnb[...] = part
            else:
                gnb[...] += part

        tb[0] = down(0)
        cp(wup, wupb, 3).wait()
        for k in range(tiles):
            if k + 1 < tiles:
                tb[(k + 1) % 2] = down(k + 1)
            act(k)
            if k >= 1:
                up(k - 1)
        up(tiles - 1)
        puts.append(put(gub, guS.at[here], 1))
        cp(mS.at[here], mb, 4).wait()

        def ln2(r):
            rows = pl.ds(r, 32)
            unit, scale = normalize(mb[rows, :])
            z = gnb[rows, :]
            gd = gdb[rows, :].astype(f32)
            gm = gd + norm_back(z, par[GAIN + 1 : GAIN + 2, :], unit, scale)
            gmb[rows, :] = gm
            go = gm.astype(bf16)
            gob[rows, :] = go
            add_small(GAIN + 1, z * unit)
            add_small(SHIFT + 1, z)
            add_small(OUTB, go.astype(f32))
            add_small(DOWNB, gd)

        for_rows(CH, 32, ln2)
        puts.append(put(gob, goS.at[here], 2))
        cp(wout, woutb, 7).wait()
        gy = dot_nt(gob[...], woutb[...])
        gyb[...] = gy
        gylow[...] = gy.astype(bf16)
        cp(spread_h, spread, 8).wait()
        cp(back_h, back, 9).wait()
        g2[seg] = dot(spread[...], gylow[...]).astype(bf16)
        puts.append(put(g2.at[seg], g2S.at[seg], 3))
        for j in range(pieces):

            @pl.when(j > seg)
            def _(j=j):
                cp(g2S.at[j], g2.at[j], 16 + 4 * j).wait()
                cp(g1S.at[j], g1.at[j], 16 + 4 * j + 1).wait()

            @pl.when(j < pieces - seg)
            def _(j=j):
                cp(k2S.at[j], k2.at[j], 16 + 4 * j + 2).wait()
                cp(k1S.at[j], k1.at[j], 16 + 4 * j + 3).wait()

        mix_spectra(k2, g2, zspec, seg, pieces, lambda j: j - seg, True)
        gsb[...] = dot(back[...], zspec[...])

        @pl.when(seg == 0)
        def _():
            cp(pS.at[pl.ds(0, CH)], pb.at[pl.ds(16, CH)], 10).wait()

        @pl.when(seg > 0)
        def _():
            cp(pS.at[pl.ds(0, CH + 16)], pb, 10).wait()

        cp(y1S.at[here], y1b, 11).wait()

        def branch(r, b):
            rows = pb[pl.ds(r, 48), b * D : (b + 1) * D].astype(f32)
            late = [rows[16 - i : 48 - i] for i in range(3)]
            t = [par[TAP + 3 * i + b : TAP + 3 * i + b + 1, :] for i in range(3)]
            return t[0] * late[0] + t[1] * late[1] + t[2] * late[2], late

        def keep(r, b, grad, late):
            gqb[pl.ds(r, 32), b * D : (b + 1) * D] = grad
            for i in range(3):
                add_small(TAP + 3 * i + b, grad * late[i])

        def second(r):
            rows = pl.ds(r, 32)
            gate, late = branch(r, 2)
            y1 = y1b[rows, :].astype(f32)
            gy2 = gyb[rows, :]
            gs2 = gsb[rows, :] + par[SKIP + 1 : SKIP + 2, :] * gy2
            gy1 = gs2 * gate
            gy1b[rows, :] = gy1
            gylow[rows, :] = gy1.astype(bf16)
            add_small(SKIP + 1, gy2 * (y1 * gate))
            keep(r, 2, gs2 * y1, late)

        for_rows(CH, 32, second)
        g1[seg] = dot(spread[...], gylow[...]).astype(bf16)
        puts.append(put(g1.at[seg], g1S.at[seg], 4))
        mix_spectra(k1, g1, zspec, seg, pieces, lambda j: j - seg, True)
        gsb[...] = dot(back[...], zspec[...])

        def first(r):
            rows = pl.ds(r, 32)
            relay, late_relay = branch(r, 0)
            gate, late_gate = branch(r, 1)
            gy1 = gy1b[rows, :]
            gs1 = gsb[rows, :] + par[SKIP : SKIP + 1, :] * gy1
            add_small(SKIP, gy1 * (relay * gate))
            keep(r, 0, gs1 * gate, late_relay)
            keep(r, 1, gs1 * relay, late_gate)

        for_rows(CH, 32, first)
        puts.append(put(gqb.at[pl.ds(0, CARRY)], headS, 5))

        def short(r):
            for b in range(3):
                cols = slice(b * D, (b + 1) * D)
                rows = gqb[pl.ds(r, 32 + CARRY), cols]
                t = [par[TAP + 3 * i + b : TAP + 3 * i + b + 1, :] for i in range(3)]
                gp = (t[0] * rows[:32] + t[1] * rows[1:33] + t[2] * rows[2:34]).astype(bf16)
                gpb[pl.ds(r, 32), cols] = gp
                add_small(INB + b, gp.astype(f32))

        for_rows(CH, 32, short)
        puts.append(put(gpb, gpS.at[here], 6))
        cp(win, winb, 12).wait()
        gnb[...] = dot_nt(gpb[...], winb[...])
        cp(hS.at[here], hb, 13).wait()

        def ln1(r):
            rows = pl.ds(r, 32)
            unit, scale = normalize(hb[rows, :].astype(f32))
            z = gnb[rows, :]
            gh = gmb[rows, :] + norm_back(z, par[GAIN : GAIN + 1, :], unit, scale)
            outfb[rows, :] = gh
            outb[rows, :] = gh.astype(bf16)
            add_small(GAIN, z * unit)
            add_small(SHIFT, z)

        for_rows(CH, 32, ln1)
        puts.append(put(outb, out_h, 7))
        puts.append(put(outfb, outf_h, 8))
        puts.append(put(small, smallS, 9))
        for c in puts:
            c.wait()


def backward_call(info, par, cots, arrived, win, wout, wup, wdown, tabs, kept, state):
    T, D = cots.shape
    FF = wup.shape[1]
    pieces = T // CH
    spec3 = (pieces, 2 * CH, D)
    small = (UPB + FF // D, 8, D)
    shapes = [
        ((CH, D), bf16), ((CH, D), f32),
        ((T, D), bf16), ((T, FF), bf16), ((T, D), bf16), ((T, 3 * D), bf16),
        (spec3, bf16), (spec3, bf16), ((CARRY, 3 * D), f32), (small, f32),
    ]
    out_shape = [jax.ShapeDtypeStruct(*s) for s in shapes]
    n_state = 0 if state is None else len(shapes) - 2
    V = pltpu.VMEM
    scratch = [
        V((CH, D), bf16), V(win.shape, bf16), V(wout.shape, bf16), V(wup.shape, bf16), V(wdown.shape, bf16),
        V((2 * CH, CH), bf16), V((CH, 2 * CH), bf16), V(spec3, bf16), V(spec3, bf16), V(spec3, bf16), V(spec3, bf16),
        V((CH, FF), bf16), V((CH, D), bf16), V((CH, D), f32), V((CH + 16, 3 * D), bf16), V((CH, D), bf16),
        V((2, CH, FT), f32), V((CH, FF), bf16), V((CH, D), f32), V((CH, D), f32), V((CH, D), bf16),
        V((CH, D), f32), V((CH, D), bf16), V((CH, D), f32), V((2 * CH, D), bf16), V((CH, D), f32),
        V((CH + CARRY, 3 * D), f32), V((CH, 3 * D), bf16), V((CH, D), bf16), V((CH, D), f32), V(small, f32),
        pltpu.SemaphoreType.DMA((16 + 4 * pieces,)),
        pltpu.SemaphoreType.DMA((10,)),
    ]
    return pl.pallas_call(
        functools.partial(backward_kernel, pieces, n_state),
        out_shape=out_shape,
        in_specs=[SMEM, VM] + [ANY] * (15 + n_state),
        out_specs=[ANY] * len(shapes),
        scratch_shapes=scratch,
        input_output_aliases={17 + i: 2 + i for i in range(n_state)},
        compiler_params=pltpu.CompilerParams(vmem_limit_bytes=VMEM_LIMIT),
        cost_estimate=pl.CostEstimate(flops=2 * CH * (4 * D * D + 2 * D * FF), bytes_accessed=30 << 20, transcendentals=0),
        name="backward_chunk",
    )(info, par, cots, arrived, win, wout, wup, wdown, tabs[0], tabs[1], *kept, *(state or ()))


def filter_kernel(pieces, s, g, back, turned, out, q):
    width = s.shape[2] // 2

    for d in range(pieces):

        def tile(i, carry, d=d):
            r = pl.multiple_of(i * 16, 16)
            for half in range(2):
                cols = slice(half * width, (half + 1) * width)
                real = jnp.zeros((16, width), f32)
                imag = jnp.zeros((16, width), f32)
                for k in range(d, pieces):
                    ar = s[k - d, pl.ds(r, 16), cols].astype(f32)
                    ai = s[k - d, pl.ds(CH + r, 16), cols].astype(f32)
                    br = g[k, pl.ds(r, 16), cols].astype(f32)
                    bi = g[k, pl.ds(CH + r, 16), cols].astype(f32)
                    real = real + (ar * br + ai * bi)
                    imag = imag + (ar * bi - ai * br)
                q[d, pl.ds(r, 16), cols] = real.astype(bf16)
                q[d, pl.ds(CH + r, 16), cols] = imag.astype(bf16)
            return carry

        lax.fori_loop(0, CH // 16, tile, 0)
    for d in range(pieces):
        rows = dot(back[...], q[d])
        if d + 1 < pieces:
            rows += dot(turned[...], q[d + 1])
        out[pl.ds(d * CH, CH), :] = rows.astype(bf16)


def filter_call(s, g, tabs):
    pieces, _, D = s.shape
    turned = (tabs[2][:, :CH].astype(f32) / CH).astype(bf16).T
    return pl.pallas_call(
        functools.partial(filter_kernel, pieces),
        out_shape=jax.ShapeDtypeStruct((pieces * CH, D), bf16),
        in_specs=[VM] * 4,
        out_specs=VM,
        scratch_shapes=[pltpu.VMEM(s.shape, bf16)],
        compiler_params=pltpu.CompilerParams(vmem_limit_bytes=VMEM_LIMIT),
        name="filter_grad",
    )(s, g, tabs[1], turned)


def dot_rows(x, y):
    return lax.dot_general(x, y, (((0,), (0,)), ((), ())), preferred_element_type=f32).astype(bf16)


def rows_of(chunks, low, high):
    parts, at = [], low
    while at < high:
        k, off = at // CH, at % CH
        size = min(CH - off, high - at)
        parts.append(chunks[k][off : off + size])
        at += size
    return parts[0] if len(parts) == 1 else jnp.concatenate(parts, axis=0)


def spread_rows(chunks, source, total, count, rank):
    share = total // count
    mine = None
    for r in range(count):
        rows = rows_of(chunks, r * share, (r + 1) * share)
        if r != source:
            rows = lax.ppermute(rows.astype(bf16), "section", [(source, r)]).astype(rows.dtype)
        mine = rows if mine is None else jnp.where(rank == r, rows, mine)
    return mine


def body(
    tokens, cotangent, norm_gains, norm_shifts, in_weight, in_bias, short_taps, long_filter, skip_gains,
    out_weight, out_bias, up_weight, up_bias, down_weight, down_bias,
):
    count = lax.axis_size("section")
    ranks = lax.axis_size("dp")
    rank = lax.axis_index("section")
    tok, cot = tokens[0], cotangent[0]
    T, D = tok.shape
    FF = up_weight.shape[2]
    pieces = T // CH
    steps = pieces + 2 * (count - 1)
    tabs = tables()
    as_rows = lambda x: x[0].astype(f32).reshape(-1, D)
    par = jnp.concatenate(
        [as_rows(x) for x in (norm_gains, norm_shifts, in_bias, short_taps, skip_gains, out_bias, down_bias, up_bias)], 0
    )
    win, wout, wup, wdown, filt = in_weight[0], out_weight[0], up_weight[0], down_weight[0], long_filter[0]

    outs, state, sent = [], None, []
    for t in range(steps):
        seg = t - 2 * rank
        active = (seg >= 0) & (seg < pieces)
        info = jnp.stack([jnp.clip(seg, 0, pieces - 1), active.astype(jnp.int32), (rank == 0).astype(jnp.int32)])
        arrived = sent[t - 2] if t >= 2 else tok[:CH]
        got = forward_call(info.astype(jnp.int32), par, tok, arrived, filt, win, wout, wup, wdown, tabs, state)
        outs.append(got[0])
        state = got[1:]
        if t + 2 < steps:
            sent.append(lax.ppermute(got[0], "section", [(i, i + 1) for i in range(count - 1)]))
    aS, hS, pS, y1S, ybS, mS, nS, eS, dS, s1S, s2S, k1S, k2S, _ = state
    kept = (hS, pS, y1S, mS, dS, k1S, k2S)
    stream = spread_rows(outs[2 * (count - 1) :], count - 1, T, count, rank)

    grads, state, sent = [], None, []
    for t in range(steps):
        seg = pieces - 1 - (t - 2 * (count - 1 - rank))
        active = (seg >= 0) & (seg < pieces)
        info = jnp.stack([jnp.clip(seg, 0, pieces - 1), active.astype(jnp.int32), (rank == count - 1).astype(jnp.int32)])
        arrived = sent[t - 2] if t >= 2 else cot[:CH]
        got = backward_call(info.astype(jnp.int32), par, cot, arrived, win, wout, wup, wdown, tabs, kept, state)
        grads.append(got[1])
        state = got[2:]
        if t + 2 < steps:
            sent.append(lax.ppermute(got[0], "section", [(i + 1, i) for i in range(count - 1)]))
    gdS, guS, goS, gpS, g1S, g2S, _, small = state
    token_grad = spread_rows(grads[2 * (count - 1) :][::-1], 0, T, count, rank)

    slab = jnp.concatenate([dot_rows(gdS, eS), dot_rows(nS, guS), dot_rows(ybS, goS), dot_rows(aS, gpS)], axis=1)
    taps = jnp.concatenate([filter_call(s1S, g1S, tabs), filter_call(s2S, g2S, tabs)], axis=1)
    small = jnp.sum(small, axis=1)
    per = D // ranks
    mini = jnp.concatenate(
        [small[:UPB].reshape(UPB, ranks, per).transpose(1, 0, 2).reshape(ranks, -1), small[UPB:].reshape(ranks, -1)], axis=1
    )
    scatter = lambda x: lax.psum_scatter(x, "dp", scatter_dimension=0, tiled=True).astype(f32)
    slab, taps, mini = scatter(slab), scatter(taps), scatter(mini)[0]
    head = mini[: UPB * per].reshape(UPB, per)
    return (
        stream[None],
        token_grad[None],
        head[GAIN : GAIN + 2][None],
        head[SHIFT : SHIFT + 2][None],
        slab[:, 2 * FF + D :][None],
        head[INB : INB + 3][None],
        head[TAP : TAP + 9].reshape(1, 3, 3, per),
        taps.reshape(-1, 2, D).transpose(1, 0, 2)[None],
        head[SKIP : SKIP + 2][None],
        slab[:, 2 * FF : 2 * FF + D][None],
        head[OUTB][None],
        slab[:, FF : 2 * FF][None],
        mini[UPB * per :][None],
        slab[:, :FF].T[None],
        head[DOWNB][None],
    )


def solution(mesh):
    whole = P("dp", None, None)
    split = lambda n: P("section", *([None] * n))
    return jax.shard_map(
        body,
        mesh=mesh,
        in_specs=(
            whole, whole, split(2), split(2), split(2), split(2), split(3), split(3), split(2), split(2), split(1),
            split(2), split(1), split(2), split(1),
        ),
        out_specs=(
            P("dp", "section", None),
            P("dp", "section", None),
            P("section", None, "dp"),
            P("section", None, "dp"),
            P("section", "dp", None),
            P("section", None, "dp"),
            P("section", None, None, "dp"),
            P("section", None, "dp", None),
            P("section", None, "dp"),
            P("section", "dp", None),
            P("section", "dp"),
            P("section", "dp", None),
            P("section", "dp"),
            P("section", None, "dp"),
            P("section", "dp"),
        ),
        check_vma=False,
    )
```

```python
import functools
import math

import jax
import jax.numpy as jnp
import ml_dtypes
import numpy as np
from jax import lax
from jax.experimental import pallas as pl
from jax.experimental.pallas import tpu as pltpu
from jax.sharding import PartitionSpec as P

CH = 256
FT = 512
CARRY = 8
f32, bf16 = jnp.float32, jnp.bfloat16
VMEM_LIMIT = 60 * 1024 * 1024
ANY = pl.BlockSpec(memory_space=pl.ANY)
SMEM = pl.BlockSpec(memory_space=pltpu.SMEM)
VM = pl.BlockSpec(memory_space=pltpu.VMEM)

GAIN, SHIFT, INB, TAP, SKIP, OUTB, DOWNB, UPB = 0, 2, 4, 7, 16, 18, 19, 20


def tables():
    order = np.concatenate([np.arange(0, CH, 2), np.arange(1, CH, 2)])
    angle = np.pi * ((2 * order[:, None] + 1) * np.arange(CH)[None] % (4 * CH)) / (2 * CH)
    cos, sin = np.cos(angle), np.sin(angle)
    sign = np.where(order % 2 == 0, 1.0, -1.0)[:, None]
    spread = np.concatenate([cos, -sin], 0)
    turned = np.concatenate([sign * sin, sign * cos], 0)
    as_low = lambda t: jnp.asarray(t.astype(ml_dtypes.bfloat16))
    return as_low(spread), as_low(spread.T / CH), as_low(np.concatenate([turned, spread], 1))


def dot(x, y):
    return jnp.dot(x, y, preferred_element_type=f32)


def dot_nt(x, y):
    return lax.dot_general(x, y, (((1,), (1,)), ((), ())), preferred_element_type=f32)


def rows_at(index, size):
    return pl.ds(pl.multiple_of(index * size, size), size)


def for_rows(total, size, step):
    def run(i, carry):
        step(pl.multiple_of(i * size, size))
        return carry

    lax.fori_loop(0, total // size, run, 0)


def normalize(rows):
    average = jnp.mean(rows, axis=-1, keepdims=True)
    centered = rows - average
    scale = lax.rsqrt(jnp.mean(centered * centered, axis=-1, keepdims=True) + 1e-05)
    return centered * scale, scale


def norm_back(z, gain, unit, scale):
    w = z * gain
    return (
        w - jnp.mean(w, axis=-1, keepdims=True) - unit * jnp.mean(w * unit, axis=-1, keepdims=True)
    ) * scale


def gelu_pair(u):
    t = 1.0 / (1.0 + (0.3275911 * math.sqrt(0.5)) * jnp.abs(u))
    series = t * (
        0.5 * 0.254829592
        + t * (0.5 * -0.284496736 + t * (0.5 * 1.421413741 + t * (0.5 * -1.453152027 + t * (0.5 * 1.061405429))))
    )
    bell = jnp.exp(-0.5 * (u * u))
    tail = series * bell
    phi_sum = jnp.where(u >= 0, 1.0 - tail, tail)
    return u * phi_sum, phi_sum + u * (bell * (1.0 / math.sqrt(2.0 * math.pi)))


def mix_spectra(left, right, out, low, high, left_of, conj):
    width = out.shape[1] // 2

    def tile(i, carry):
        r = pl.multiple_of(i * 16, 16)
        for half in range(2):
            cols = slice(half * width, (half + 1) * width)

            def term(j, acc):
                k = left_of(j)
                ar = left[k, pl.ds(r, 16), cols].astype(f32)
                ai = left[k, pl.ds(CH + r, 16), cols].astype(f32)
                br = right[j, pl.ds(r, 16), cols].astype(f32)
                bi = right[j, pl.ds(CH + r, 16), cols].astype(f32)
                if conj:
                    return acc[0] + (ar * br + ai * bi), acc[1] + (ar * bi - ai * br)
                return acc[0] + (ar * br - ai * bi), acc[1] + (ar * bi + ai * br)

            zero = jnp.zeros((16, width), f32)
            real, imag = lax.fori_loop(low, high, term, (zero, zero))
            out[pl.ds(r, 16), cols] = real.astype(out.dtype)
            out[pl.ds(CH + r, 16), cols] = imag.astype(out.dtype)
        return carry

    lax.fori_loop(0, CH // 16, tile, 0)


def forward_kernel(pieces, n_state, info, par, *refs):
    (tokens, arrived, filt, win, wout, wup, wdown, spread_h, back_h, pair_h) = refs[:10]
    refs = refs[10 + n_state :]
    out_h, aS, hS, pS, y1S, ybS, mS, nS, eS, dS, s1S, s2S, k1S, k2S, tailS = refs[:15]
    (
        hb, ab, winb, woutb, wupb, wdownb, spread, back, pair, wn1, wn2, k1, k2, s1, s2,
        pb, plow, g2b, sf, sb, yspec, y1b, y1low, yb, mb, nb, ub, eb, db, ob, outb, sem, osem,
    ) = refs[15:]
    seg, active, first = info[0], info[1], info[2]
    D = hb.shape[1]
    FF = wupb.shape[1]
    here = rows_at(seg, CH)

    def cp(src, dst, k):
        return pltpu.make_async_copy(src, dst, sem.at[k])

    def put(src, dst, k):
        c = pltpu.make_async_copy(src, dst, osem.at[k])
        c.start()
        return c

    @pl.when(active == 1)
    def _():
        @pl.when(first == 1)
        def _():
            cp(tokens.at[here], hb, 0).start()

        @pl.when(first == 0)
        def _():
            cp(arrived, hb, 0).start()

        cp(win, winb, 1).start()
        cp(pair_h, pair, 2).start()

        @pl.when(seg == 0)
        def _():
            cp(filt.at[0, pl.ds(0, CH)], wn1.at[pl.ds(CH, CH)], 3).start()
            cp(filt.at[1, pl.ds(0, CH)], wn2.at[pl.ds(CH, CH)], 4).start()
            wn1[pl.ds(0, CH), :] = jnp.zeros((CH, D), bf16)
            wn2[pl.ds(0, CH), :] = jnp.zeros((CH, D), bf16)
            pb[pl.ds(0, CARRY), :] = jnp.zeros((CARRY, 3 * D), f32)

        @pl.when(seg > 0)
        def _():
            before = pl.ds(pl.multiple_of((seg - 1) * CH, CH), 2 * CH)
            cp(filt.at[0, before], wn1, 3).start()
            cp(filt.at[1, before], wn2, 4).start()
            cp(tailS, pb.at[pl.ds(0, CARRY)], 5).start()

        cp(spread_h, spread, 6).start()
        cp(back_h, back, 7).start()
        cp(arrived, hb, 0).wait()
        back_h_put = put(hb, hS.at[here], 0)

        def ln1(r):
            unit, _ = normalize(hb[pl.ds(r, 64), :].astype(f32))
            ab[pl.ds(r, 64), :] = (unit * par[GAIN : GAIN + 1, :] + par[SHIFT : SHIFT + 1, :]).astype(bf16)

        for_rows(CH, 64, ln1)
        a_put = put(ab, aS.at[here], 1)
        cp(win, winb, 1).wait()
        for j in range(pieces - 1):

            @pl.when(j < seg)
            def _(j=j):
                for k, (src, dst) in enumerate(((k1S, k1), (s1S, s1), (k2S, k2), (s2S, s2))):
                    cp(src.at[j], dst.at[j], 8 + 4 * j + k).start()

        base = 8 + 4 * pieces
        cp(wout, woutb, base).start()
        cp(wup, wupb, base + 1).start()
        for b in range(3):
            cols = slice(b * D, (b + 1) * D)
            pb[pl.ds(CARRY, CH), cols] = dot(ab[...], winb[:, cols]) + par[INB + b : INB + b + 1, :]
        cp(wdown, wdownb, base + 2).start()

        @pl.when(seg > 0)
        def _():
            cp(tailS, pb.at[pl.ds(0, CARRY)], 5).wait()

        def short(r):
            got = []
            for b in range(3):
                cols = slice(b * D, (b + 1) * D)
                rows = pb[pl.ds(r, 32 + CARRY), cols]
                now = rows[CARRY:]
                plow[pl.ds(r, 32), cols] = now.astype(bf16)
                t = [par[TAP + 3 * i + b : TAP + 3 * i + b + 1, :] for i in range(3)]
                got.append(t[0] * now + t[1] * rows[CARRY - 1 : -1] + t[2] * rows[CARRY - 2 : -2])
            g2b[pl.ds(r, 32), :] = got[2]
            lead = got[0] * got[1]
            sf[pl.ds(r, 32), :] = lead
            sb[pl.ds(r, 32), :] = lead.astype(bf16)

        for_rows(CH, 32, short)
        p_put = put(plow, pS.at[here], 2)
        tail_put = put(pb.at[pl.ds(CH, CARRY)], tailS, 3)
        cp(pair_h, pair, 2).wait()
        cp(spread_h, spread, 6).wait()
        cp(back_h, back, 7).wait()
        cp(filt.at[0, pl.ds(0, CH)], wn1.at[pl.ds(CH, CH)], 3).wait()
        cp(filt.at[1, pl.ds(0, CH)], wn2.at[pl.ds(CH, CH)], 4).wait()

        @pl.when(seg > 0)
        def _():
            cp(filt.at[0, pl.ds(0, CH)], wn1.at[pl.ds(CH, CH)], 3).wait()
            cp(filt.at[1, pl.ds(0, CH)], wn2.at[pl.ds(CH, CH)], 4).wait()

        for j in range(pieces - 1):

            @pl.when(j < seg)
            def _(j=j):
                for k, (src, dst) in enumerate(((k1S, k1), (s1S, s1), (k2S, k2), (s2S, s2))):
                    cp(src.at[j], dst.at[j], 8 + 4 * j + k).wait()

        k1[seg] = dot(pair[...], wn1[...]).astype(bf16)
        k2[seg] = dot(pair[...], wn2[...]).astype(bf16)
        puts = [put(k1.at[seg], k1S.at[seg], 4), put(k2.at[seg], k2S.at[seg], 5)]
        s1[seg] = dot(spread[...], sb[...]).astype(bf16)
        puts.append(put(s1.at[seg], s1S.at[seg], 6))
        mix_spectra(k1, s1, yspec, 0, seg + 1, lambda j: seg - j, False)
        y1b[...] = dot(back[...], yspec[...])

        def second(r):
            rows = pl.ds(r, 64)
            y = y1b[rows, :] + par[SKIP : SKIP + 1, :] * sf[rows, :]
            y1low[rows, :] = y.astype(bf16)
            trail = y * g2b[rows, :]
            sf[rows, :] = trail
            sb[rows, :] = trail.astype(bf16)

        for_rows(CH, 64, second)
        puts.append(put(y1low, y1S.at[here], 7))
        s2[seg] = dot(spread[...], sb[...]).astype(bf16)
        puts.append(put(s2.at[seg], s2S.at[seg], 8))
        mix_spectra(k2, s2, yspec, 0, seg + 1, lambda j: seg - j, False)
        yb[...] = (dot(back[...], yspec[...]) + par[SKIP + 1 : SKIP + 2, :] * sf[...]).astype(bf16)
        puts.append(put(yb, ybS.at[here], 9))
        cp(wout, woutb, base).wait()
        mb[...] = dot(yb[...], woutb[...])

        def ln2(r):
            rows = pl.ds(r, 64)
            mid = hb[rows, :].astype(f32) + (mb[rows, :] + par[OUTB : OUTB + 1, :])
            mb[rows, :] = mid
            unit, _ = normalize(mid)
            nb[rows, :] = (unit * par[GAIN + 1 : GAIN + 2, :] + par[SHIFT + 1 : SHIFT + 2, :]).astype(bf16)
            ob[rows, :] = mid + par[DOWNB : DOWNB + 1, :]

        for_rows(CH, 64, ln2)
        puts.append(put(mb, mS.at[here], 10))
        puts.append(put(nb, nS.at[here], 11))
        cp(wup, wupb, base + 1).wait()
        cp(wdown, wdownb, base + 2).wait()
        tiles = FF // FT

        def up(k):
            return dot(nb[...], wupb[:, k * FT : (k + 1) * FT])

        def act(k):
            u = ub[k % 2]
            per_row = D // FT if D % FT == 0 else 0
            u = u + bias_up(k)
            e, d = gelu_pair(u)
            eb[:, k * FT : (k + 1) * FT] = e.astype(bf16)
            db[:, k * FT : (k + 1) * FT] = d.astype(bf16)

        def bias_up(k):
            parts, at = [], k * FT
            while at < (k + 1) * FT:
                row, col = at // D, at % D
                wide = min(D - col, (k + 1) * FT - at)
                parts.append(par[UPB + row : UPB + row + 1, col : col + wide])
                at += wide
            return parts[0] if len(parts) == 1 else jnp.concatenate(parts, axis=1)

        def down(k):
            ob[...] += dot(eb[:, k * FT : (k + 1) * FT], wdownb[k * FT : (k + 1) * FT, :])

        ub[0] = up(0)
        for k in range(tiles):
            if k + 1 < tiles:
                ub[(k + 1) % 2] = up(k + 1)
            act(k)
            if k >= 1:
                down(k - 1)
        down(tiles - 1)
        puts.append(put(eb, eS.at[here], 12))
        puts.append(put(db, dS.at[here], 13))
        outb[...] = ob[...].astype(bf16)
        puts.append(put(outb, out_h, 14))
        for c in [back_h_put, a_put, p_put, tail_put] + puts:
            c.wait()


def forward_call(info, par, tokens, arrived, filt, win, wout, wup, wdown, tabs, state):
    T, D = tokens.shape
    FF = wup.shape[1]
    pieces = T // CH
    spec3 = (pieces, 2 * CH, D)
    shapes = [
        ((CH, D), bf16),
        ((T, D), bf16), ((T, D), bf16), ((T, 3 * D), bf16), ((T, D), bf16), ((T, D), bf16), ((T, D), f32),
        ((T, D), bf16), ((T, FF), bf16), ((T, FF), bf16),
        (spec3, bf16), (spec3, bf16), (spec3, bf16), (spec3, bf16),
        ((CARRY, 3 * D), f32),
    ]
    out_shape = [jax.ShapeDtypeStruct(*s) for s in shapes]
    n_state = 0 if state is None else len(shapes) - 1
    V = pltpu.VMEM
    scratch = [
        V((CH, D), bf16), V((CH, D), bf16), V(win.shape, bf16), V(wout.shape, bf16), V(wup.shape, bf16),
        V(wdown.shape, bf16), V((2 * CH, CH), bf16), V((CH, 2 * CH), bf16), V((2 * CH, 2 * CH), bf16),
        V((2 * CH, D), bf16), V((2 * CH, D), bf16), V(spec3, bf16), V(spec3, bf16), V(spec3, bf16), V(spec3, bf16),
        V((CARRY + CH, 3 * D), f32), V((CH, 3 * D), bf16), V((CH, D), f32), V((CH, D), f32), V((CH, D), bf16),
        V((2 * CH, D), bf16), V((CH, D), f32), V((CH, D), bf16), V((CH, D), bf16), V((CH, D), f32), V((CH, D), bf16),
        V((2, CH, FT), f32), V((CH, FF), bf16), V((CH, FF), bf16), V((CH, D), f32), V((CH, D), bf16),
        pltpu.SemaphoreType.DMA((8 + 4 * pieces + 3,)),
        pltpu.SemaphoreType.DMA((15,)),
    ]
    return pl.pallas_call(
        functools.partial(forward_kernel, pieces, n_state),
        out_shape=out_shape,
        in_specs=[SMEM, VM] + [ANY] * (10 + n_state),
        out_specs=[ANY] * len(shapes),
        scratch_shapes=scratch,
        input_output_aliases={12 + i: 1 + i for i in range(n_state)},
        compiler_params=pltpu.CompilerParams(vmem_limit_bytes=VMEM_LIMIT),
        cost_estimate=pl.CostEstimate(flops=2 * CH * (4 * D * D + 2 * D * FF), bytes_accessed=30 << 20, transcendentals=0),
        name="forward_chunk",
    )(info, par, tokens, arrived, filt, win, wout, wup, wdown, *tabs, *(state or ()))


def fold_rows(x):
    return jnp.sum(x.reshape(x.shape[0] // 8, 8, x.shape[1]), axis=0)


def pieces_of(at, wide, D):
    spans, off = [], 0
    while off < wide:
        row, col = (at + off) // D, (at + off) % D
        size = min(D - col, wide - off)
        spans.append((row, col, off, size))
        off += size
    return spans


def backward_kernel(pieces, n_state, info, par, *refs):
    (cots, arrived, win, wout, wup, wdown, spread_h, back_h, hS, pS, y1S, mS, dS, k1S, k2S) = refs[:15]
    refs = refs[15 + n_state :]
    out_h, outf_h, gdS, guS, goS, gpS, g1S, g2S, headS, smallS = refs[:10]
    (
        gdb, winb, woutb, wupb, wdownb, spread, back, k1, k2, g1, g2, db, hb, mb, pb, y1b,
        tb, gub, gnb, gmb, gob, gyb, gylow, gsb, zspec, gy1b, gqb, gpb, outb, outfb, small, sem, osem,
    ) = refs[10:]
    seg, active, last = info[0], info[1], info[2]
    D = hb.shape[1]
    FF = wupb.shape[1]
    here = rows_at(seg, CH)

    def cp(src, dst, k):
        return pltpu.make_async_copy(src, dst, sem.at[k])

    def put(src, dst, k):
        c = pltpu.make_async_copy(src, dst, osem.at[k])
        c.start()
        return c

    def add_small(k, x, cols=slice(None)):
        small[k, :, cols] += fold_rows(x)

    @pl.when(active == 1)
    def _():
        fresh = seg == pieces - 1

        @pl.when(last == 1)
        def _():
            cp(cots.at[here], gdb, 0).start()

        @pl.when(last == 0)
        def _():
            cp(arrived, gdb, 0).start()

        cp(wdown, wdownb, 1).start()
        cp(dS.at[here], db, 2).start()
        cp(wup, wupb, 3).start()
        cp(mS.at[here], mb, 4).start()

        @pl.when(fresh)
        def _():
            small[...] = jnp.zeros(small.shape, f32)
            gqb[pl.ds(CH, CARRY), :] = jnp.zeros((CARRY, 3 * D), f32)

        @pl.when(jnp.logical_not(fresh))
        def _():
            cp(smallS, small, 5).start()
            cp(headS, gqb.at[pl.ds(CH, CARRY)], 6).start()

        cp(arrived, gdb, 0).wait()
        puts = [put(gdb, gdS.at[here], 0)]

        @pl.when(jnp.logical_not(fresh))
        def _():
            cp(smallS, small, 5).wait()
            cp(headS, gqb.at[pl.ds(CH, CARRY)], 6).wait()

        cp(wdown, wdownb, 1).wait()
        cp(dS.at[here], db, 2).wait()
        cp(wout, woutb, 7).start()
        cp(spread_h, spread, 8).start()
        cp(back_h, back, 9).start()
        for j in range(pieces):

            @pl.when(j > seg)
            def _(j=j):
                cp(g2S.at[j], g2.at[j], 16 + 4 * j).start()
                cp(g1S.at[j], g1.at[j], 16 + 4 * j + 1).start()

            @pl.when(j < pieces - seg)
            def _(j=j):
                cp(k2S.at[j], k2.at[j], 16 + 4 * j + 2).start()
                cp(k1S.at[j], k1.at[j], 16 + 4 * j + 3).start()

        @pl.when(seg == 0)
        def _():
            pb[pl.ds(0, 16), :] = jnp.zeros((16, 3 * D), bf16)
            cp(pS.at[pl.ds(0, CH)], pb.at[pl.ds(16, CH)], 10).start()

        @pl.when(seg > 0)
        def _():
            cp(pS.at[pl.ds(pl.multiple_of(seg * CH - 16, 16), CH + 16)], pb, 10).start()

        cp(y1S.at[here], y1b, 11).start()
        cp(win, winb, 12).start()
        cp(hS.at[here], hb, 13).start()
        tiles = FF // FT

        def down(k):
            return dot_nt(gdb[...], wdownb[k * FT : (k + 1) * FT, :])

        def act(k):
            cols = slice(k * FT, (k + 1) * FT)
            gu = (db[:, cols].astype(f32) * tb[k % 2]).astype(bf16)
            gub[:, cols] = gu
            total = fold_rows(gu.astype(f32))
            for row, col, off, size in pieces_of(k * FT, FT, D):
                small[UPB + row, :, col : col + size] += total[:, off : off + size]

        def up(k):
            part = dot_nt(gub[:, k * FT : (k + 1) * FT], wupb[:, k * FT : (k + 1) * FT])
            if k == 0:
                gnb[...] = part
            else:
                gnb[...] += part

        tb[0] = down(0)
        cp(wup, wupb, 3).wait()
        for k in range(tiles):
            if k + 1 < tiles:
                tb[(k + 1) % 2] = down(k + 1)
            act(k)
            if k >= 1:
                up(k - 1)
        up(tiles - 1)
        puts.append(put(gub, guS.at[here], 1))
        cp(mS.at[here], mb, 4).wait()

        def ln2(r):
            rows = pl.ds(r, 32)
            unit, scale = normalize(mb[rows, :])
            z = gnb[rows, :]
            gd = gdb[rows, :].astype(f32)
            gm = gd + norm_back(z, par[GAIN + 1 : GAIN + 2, :], unit, scale)
            gmb[rows, :] = gm
            go = gm.astype(bf16)
            gob[rows, :] = go
            add_small(GAIN + 1, z * unit)
            add_small(SHIFT + 1, z)
            add_small(OUTB, go.astype(f32))
            add_small(DOWNB, gd)

        for_rows(CH, 32, ln2)
        puts.append(put(gob, goS.at[here], 2))
        cp(wout, woutb, 7).wait()
        gy = dot_nt(gob[...], woutb[...])
        gyb[...] = gy
        gylow[...] = gy.astype(bf16)
        cp(spread_h, spread, 8).wait()
        cp(back_h, back, 9).wait()
        g2[seg] = dot(spread[...], gylow[...]).astype(bf16)
        puts.append(put(g2.at[seg], g2S.at[seg], 3))
        for j in range(pieces):

            @pl.when(j > seg)
            def _(j=j):
                cp(g2S.at[j], g2.at[j], 16 + 4 * j).wait()
                cp(g1S.at[j], g1.at[j], 16 + 4 * j + 1).wait()

            @pl.when(j < pieces - seg)
            def _(j=j):
                cp(k2S.at[j], k2.at[j], 16 + 4 * j + 2).wait()
                cp(k1S.at[j], k1.at[j], 16 + 4 * j + 3).wait()

        mix_spectra(k2, g2, zspec, seg, pieces, lambda j: j - seg, True)
        gsb[...] = dot(back[...], zspec[...])

        @pl.when(seg == 0)
        def _():
            cp(pS.at[pl.ds(0, CH)], pb.at[pl.ds(16, CH)], 10).wait()

        @pl.when(seg > 0)
        def _():
            cp(pS.at[pl.ds(0, CH + 16)], pb, 10).wait()

        cp(y1S.at[here], y1b, 11).wait()

        def branch(r, b):
            rows = pb[pl.ds(r, 48), b * D : (b + 1) * D].astype(f32)
            late = [rows[16 - i : 48 - i] for i in range(3)]
            t = [par[TAP + 3 * i + b : TAP + 3 * i + b + 1, :] for i in range(3)]
            return t[0] * late[0] + t[1] * late[1] + t[2] * late[2], late

        def keep(r, b, grad, late):
            gqb[pl.ds(r, 32), b * D : (b + 1) * D] = grad
            for i in range(3):
                add_small(TAP + 3 * i + b, grad * late[i])

        def second(r):
            rows = pl.ds(r, 32)
            gate, late = branch(r, 2)
            y1 = y1b[rows, :].astype(f32)
            gy2 = gyb[rows, :]
            gs2 = gsb[rows, :] + par[SKIP + 1 : SKIP + 2, :] * gy2
            gy1 = gs2 * gate
            gy1b[rows, :] = gy1
            gylow[rows, :] = gy1.astype(bf16)
            add_small(SKIP + 1, gy2 * (y1 * gate))
            keep(r, 2, gs2 * y1, late)

        for_rows(CH, 32, second)
        g1[seg] = dot(spread[...], gylow[...]).astype(bf16)
        puts.append(put(g1.at[seg], g1S.at[seg], 4))
        mix_spectra(k1, g1, zspec, seg, pieces, lambda j: j - seg, True)
        gsb[...] = dot(back[...], zspec[...])

        def first(r):
            rows = pl.ds(r, 32)
            relay, late_relay = branch(r, 0)
            gate, late_gate = branch(r, 1)
            gy1 = gy1b[rows, :]
            gs1 = gsb[rows, :] + par[SKIP : SKIP + 1, :] * gy1
            add_small(SKIP, gy1 * (relay * gate))
            keep(r, 0, gs1 * gate, late_relay)
            keep(r, 1, gs1 * relay, late_gate)

        for_rows(CH, 32, first)
        puts.append(put(gqb.at[pl.ds(0, CARRY)], headS, 5))

        def short(r):
            for b in range(3):
                cols = slice(b * D, (b + 1) * D)
                rows = gqb[pl.ds(r, 32 + CARRY), cols]
                t = [par[TAP + 3 * i + b : TAP + 3 * i + b + 1, :] for i in range(3)]
                gp = (t[0] * rows[:32] + t[1] * rows[1:33] + t[2] * rows[2:34]).astype(bf16)
                gpb[pl.ds(r, 32), cols] = gp
                add_small(INB + b, gp.astype(f32))

        for_rows(CH, 32, short)
        puts.append(put(gpb, gpS.at[here], 6))
        cp(win, winb, 12).wait()
        gnb[...] = dot_nt(gpb[...], winb[...])
        cp(hS.at[here], hb, 13).wait()

        def ln1(r):
            rows = pl.ds(r, 32)
            unit, scale = normalize(hb[rows, :].astype(f32))
            z = gnb[rows, :]
            gh = gmb[rows, :] + norm_back(z, par[GAIN : GAIN + 1, :], unit, scale)
            outfb[rows, :] = gh
            outb[rows, :] = gh.astype(bf16)
            add_small(GAIN, z * unit)
            add_small(SHIFT, z)

        for_rows(CH, 32, ln1)
        puts.append(put(outb, out_h, 7))
        puts.append(put(outfb, outf_h, 8))
        puts.append(put(small, smallS, 9))
        for c in puts:
            c.wait()


def backward_call(info, par, cots, arrived, win, wout, wup, wdown, tabs, kept, state):
    T, D = cots.shape
    FF = wup.shape[1]
    pieces = T // CH
    spec3 = (pieces, 2 * CH, D)
    small = (UPB + FF // D, 8, D)
    shapes = [
        ((CH, D), bf16), ((CH, D), f32),
        ((T, D), bf16), ((T, FF), bf16), ((T, D), bf16), ((T, 3 * D), bf16),
        (spec3, bf16), (spec3, bf16), ((CARRY, 3 * D), f32), (small, f32),
    ]
    out_shape = [jax.ShapeDtypeStruct(*s) for s in shapes]
    n_state = 0 if state is None else len(shapes) - 2
    V = pltpu.VMEM
    scratch = [
        V((CH, D), bf16), V(win.shape, bf16), V(wout.shape, bf16), V(wup.shape, bf16), V(wdown.shape, bf16),
        V((2 * CH, CH), bf16), V((CH, 2 * CH), bf16), V(spec3, bf16), V(spec3, bf16), V(spec3, bf16), V(spec3, bf16),
        V((CH, FF), bf16), V((CH, D), bf16), V((CH, D), f32), V((CH + 16, 3 * D), bf16), V((CH, D), bf16),
        V((2, CH, FT), f32), V((CH, FF), bf16), V((CH, D), f32), V((CH, D), f32), V((CH, D), bf16),
        V((CH, D), f32), V((CH, D), bf16), V((CH, D), f32), V((2 * CH, D), bf16), V((CH, D), f32),
        V((CH + CARRY, 3 * D), f32), V((CH, 3 * D), bf16), V((CH, D), bf16), V((CH, D), f32), V(small, f32),
        pltpu.SemaphoreType.DMA((16 + 4 * pieces,)),
        pltpu.SemaphoreType.DMA((10,)),
    ]
    return pl.pallas_call(
        functools.partial(backward_kernel, pieces, n_state),
        out_shape=out_shape,
        in_specs=[SMEM, VM] + [ANY] * (15 + n_state),
        out_specs=[ANY] * len(shapes),
        scratch_shapes=scratch,
        input_output_aliases={17 + i: 2 + i for i in range(n_state)},
        compiler_params=pltpu.CompilerParams(vmem_limit_bytes=VMEM_LIMIT),
        cost_estimate=pl.CostEstimate(flops=2 * CH * (4 * D * D + 2 * D * FF), bytes_accessed=30 << 20, transcendentals=0),
        name="backward_chunk",
    )(info, par, cots, arrived, win, wout, wup, wdown, tabs[0], tabs[1], *kept, *(state or ()))


def filter_kernel(pieces, s, g, back, turned, out, q):
    width = s.shape[2] // 2

    for d in range(pieces):

        def tile(i, carry, d=d):
            r = pl.multiple_of(i * 16, 16)
            for half in range(2):
                cols = slice(half * width, (half + 1) * width)
                real = jnp.zeros((16, width), f32)
                imag = jnp.zeros((16, width), f32)
                for k in range(d, pieces):
                    ar = s[k - d, pl.ds(r, 16), cols].astype(f32)
                    ai = s[k - d, pl.ds(CH + r, 16), cols].astype(f32)
                    br = g[k, pl.ds(r, 16), cols].astype(f32)
                    bi = g[k, pl.ds(CH + r, 16), cols].astype(f32)
                    real = real + (ar * br + ai * bi)
                    imag = imag + (ar * bi - ai * br)
                q[d, pl.ds(r, 16), cols] = real.astype(bf16)
                q[d, pl.ds(CH + r, 16), cols] = imag.astype(bf16)
            return carry

        lax.fori_loop(0, CH // 16, tile, 0)
    for d in range(pieces):
        rows = dot(back[...], q[d])
        if d + 1 < pieces:
            rows += dot(turned[...], q[d + 1])
        out[pl.ds(d * CH, CH), :] = rows.astype(bf16)


def filter_call(s, g, tabs):
    pieces, _, D = s.shape
    turned = (tabs[2][:, :CH].astype(f32) / CH).astype(bf16).T
    return pl.pallas_call(
        functools.partial(filter_kernel, pieces),
        out_shape=jax.ShapeDtypeStruct((pieces * CH, D), bf16),
        in_specs=[VM] * 4,
        out_specs=VM,
        scratch_shapes=[pltpu.VMEM(s.shape, bf16)],
        compiler_params=pltpu.CompilerParams(vmem_limit_bytes=VMEM_LIMIT),
        name="filter_grad",
    )(s, g, tabs[1], turned)


def exchange_kernel(
    pieces, small_in, back_h, turned_h, gdS, eS, nS, guS, ybS, goS, aS, gpS, s1S, g1S, s2S, g2S,
    downT, upO, outO, inO, filtO, smallO,
    x, r1, r2, rr, rl, gb, lb, lt, sb, qb, back, turned, ob, mine, got, lsem, osem, csem, ysem, rsem, fsem, msem,
):
    D = lb.shape[2]
    me = lax.axis_index("dp")
    c, y, z = me % 2, (me // 2) % 2, me // 4
    Z = r2.shape[1]
    groups = lt.shape[2]
    n_blocks = 3 * groups + 2
    at = lambda i: {"dp": i}
    core_id, y_id = me + 1 - 2 * c, me + 2 - 4 * y
    mates = (core_id, y_id, me + 4 - 8 * (z % 2), me + 8 - 16 * (z // 2))
    inner = (z == 1) | (z == 2)

    barrier = pltpu.get_barrier_semaphore()
    for mate in mates:
        pl.semaphore_signal(barrier, inc=1, device_id=at(mate), device_id_type=pl.DeviceIdType.MESH)

    @pl.when(inner)
    def _():
        other = me + 12 - 8 * z
        pl.semaphore_signal(barrier, inc=1, device_id=at(other), device_id_type=pl.DeviceIdType.MESH)

    @pl.when(inner)
    def _():
        pl.semaphore_wait(barrier, len(mates) + 1)

    @pl.when(jnp.logical_not(inner))
    def _():
        pl.semaphore_wait(barrier, len(mates))

    def remote(src, dst, send, recv, mate):
        return pltpu.make_async_remote_copy(
            src_ref=src, dst_ref=dst, send_sem=send, recv_sem=recv, device_id=at(mate),
            device_id_type=pl.DeviceIdType.MESH,
        )

    def load(src, dst, k):
        return pltpu.make_async_copy(src, dst, lsem.at[k])

    rights = ((eS,), (guS,), (goS, gpS))
    lefts = ((gdS,), (nS,), (ybS, aS))

    def loads(m):
        found, off = [], 0
        for k, src in enumerate(rights[m]):
            wide = src.shape[1]
            found.append(load(src, gb.at[m % 2, :, pl.ds(off, wide)], 4 * m + k))
            off += wide
        for k, src in enumerate(lefts[m]):
            found.append(load(src, lb.at[k], 4 * m + 2 + k))
        return found

    def spectra(f):
        src = ((s1S, g1S), (s2S, g2S))[f]
        return [load(src[k], sb.at[k], 12 + 2 * f + k) for k in range(2)]

    def turn(m):
        for k in range(len(lefts[m])):

            def part(i, carry, k=k):
                rows = pl.multiple_of(i * 128, 128)
                piece = jnp.transpose(lb[k, pl.ds(rows, 128), :])
                lt[k, :, :, :, pl.ds(rows, 128)] = piece.reshape(lt.shape[1:4] + (128,))
                return carry

            lax.fori_loop(0, lb.shape[1] // 128, part, 0)

    def product(m, g, slot):
        def part(i, carry):
            k = jnp.minimum(i, 1) if m == 2 else 0
            left = lt[k, :, g].reshape(16 * lt.shape[1], lt.shape[4])
            cols = pl.ds(pl.multiple_of(i * D, D), D)
            value = dot(left, gb[m % 2, :, cols]).astype(bf16)
            x[slot, :, :, :, pl.ds(pl.multiple_of(i * 16, 16), 16), :] = value.reshape(x.shape[1:4] + (16, D))
            return carry

        lax.fori_loop(0, 4, part, 0)

    def filters(f, slot):
        def mix(d, carry):
            mix_spectra(sb.at[0], sb.at[1], qb.at[d], d, pieces, lambda j: j - d, True)
            return carry

        lax.fori_loop(0, pieces, mix, 0)
        qb[pieces] = jnp.zeros(qb.shape[1:], bf16)

        def part(d, carry):
            rows = dot(back[...], qb[d]) + dot(turned[...], qb[d + 1])
            x[slot, d] = rows.astype(bf16).reshape(x.shape[2:])
            return carry

        lax.fori_loop(0, pieces, part, 0)

    def core_copy(b, slot):
        return remote(x.at[slot, :, :, 1 - c], r1.at[b], csem.at[0, b], csem.at[1, b], core_id)

    def y_copy(b):
        return remote(r1.at[b, :, 1 - y], r2.at[b], ysem.at[0, b], ysem.at[1, b], y_id)

    def right_copy(b, d, src):
        return remote(src, rr.at[b, d - 1], rsem.at[0, b, d - 1], rsem.at[1, b, d - 1], me + 4)

    def left_copy(b, d, src):
        return remote(src, rl.at[b, d], fsem.at[0, b, d], fsem.at[1, b, d], me - 4)

    def add(p, q):
        return (p.astype(f32) + q.astype(f32)).astype(bf16)

    def after_core(b):
        slot = b % x.shape[0]
        core_copy(b, slot).wait()

        def part(i, carry):
            for j in range(2):
                r1[b, i, j] = add(r1[b, i, j], x[slot, i, j, c])
            return carry

        lax.fori_loop(0, Z, part, 0)
        y_copy(b).start()

    def after_y(b):
        y_copy(b).wait()

        def part(i, carry):
            r2[b, i] = add(r2[b, i], r1[b, i, y])
            return carry

        lax.fori_loop(0, Z, part, 0)

    def hop(b, h):
        @pl.when(z == h)
        def _():
            for d in range(Z - 1, h, -1):
                if h > 0:
                    right_copy(b, d, r2.at[b, d]).wait_recv()
                    rr[b, d - 1] = add(rr[b, d - 1], r2[b, d])
                right_copy(b, d, r2.at[b, d] if h == 0 else rr.at[b, d - 1]).start()

        @pl.when(z == Z - 1 - h)
        def _():
            for d in range(Z - 1 - h):
                if h > 0:
                    left_copy(b, d, r2.at[b, d]).wait_recv()
                    rl[b, d] = add(rl[b, d], r2[b, d])
                left_copy(b, d, r2.at[b, d] if h == 0 else rl.at[b, d]).start()

    def out_copies(b, slot):
        kind, a, g = order[b]
        src = ob.at[slot]
        if kind == "filter":
            return [pltpu.make_async_copy(src, filtO.at[a], osem.at[4 * slot])]
        found = []
        rows = pl.ds(g * 16, 16)
        for k in range(4):
            if a < 2:
                dst = (downT, upO)[a].at[rows, pl.ds(k * D, D)]
            elif k == 0:
                dst = outO.at[rows]
            else:
                dst = inO.at[rows, pl.ds((k - 1) * D, D)]
            found.append(pltpu.make_async_copy(src.at[pl.ds(16 * k, 16)], dst, osem.at[4 * slot + k]))
        return found

    def finish(b):
        slot = b % 2
        if b >= 2:
            for copy in out_copies(b - 2, slot):
                copy.wait()
        for p in range(Z):

            @pl.when(z == p)
            def _(p=p):
                total = r2[b, p].astype(f32)
                if p > 0:
                    right_copy(b, p, r2.at[b, p]).wait_recv()
                    total += rr[b, p - 1].astype(f32)
                if p < Z - 1:
                    left_copy(b, p, r2.at[b, p]).wait_recv()
                    total += rl[b, p].astype(f32)
                ob[slot] = total
                for d in range(p + 1, Z):
                    right_copy(b, d, r2.at[b, d]).wait_send()
                for d in range(p):
                    left_copy(b, d, r2.at[b, d]).wait_send()

        for copy in out_copies(b, slot):
            copy.start()

    def mini_copy(k):
        return remote(mine.at[k], got.at[k], msem.at[0, k], msem.at[1, k], mates[k])

    order = [("product", 0, g) for g in range(groups)] + [("filter", 0, 0)]
    order += [("product", 1, g) for g in range(groups)] + [("filter", 1, 0)]
    order += [("product", 2, g) for g in range(groups)]

    for copy in loads(0):
        copy.start()
    tables_in = [load(back_h, back, 16), load(turned_h, turned, 17)]
    tables_in[0].start()
    tables_in[1].start()
    for copy in spectra(0):
        copy.start()
    mine[0] = jnp.sum(small_in[...], axis=1)
    mini_copy(0).start()

    for i in range(n_blocks + 6):
        if 0 <= i - 1 < n_blocks:
            after_core(i - 1)
        if 0 <= i - 2 < n_blocks:
            after_y(i - 2)
            hop(i - 2, 0)
        if 0 <= i - 3 < n_blocks:
            hop(i - 3, 1)
        if 0 <= i - 4 < n_blocks:
            hop(i - 4, 2)
        if 0 <= i - 5 < n_blocks:
            finish(i - 5)
        if i < n_blocks:
            kind, a, g = order[i]
            slot = i % x.shape[0]
            if kind == "product":
                if g == 0:
                    for copy in loads(a):
                        copy.wait()
                    turn(a)
                    if a + 1 < 3:
                        for copy in loads(a + 1):
                            copy.start()
                product(a, g, slot)
            else:
                if a == 0:
                    tables_in[0].wait()
                    tables_in[1].wait()
                for copy in spectra(a):
                    copy.wait()
                filters(a, slot)
                if a == 0:
                    for copy in spectra(1):
                        copy.start()
            core_copy(i, slot).start()
        if 2 <= i < 6:
            k = i - 2
            mini_copy(k).wait()
            total = mine[k] + got[k]
            if k < 3:
                mine[k + 1] = total
                mini_copy(k + 1).start()
            else:
                smallO[...] = total
    for b in (n_blocks - 2, n_blocks - 1):
        for copy in out_copies(b, b % 2):
            copy.wait()


def exchange_call(small, tabs, gdS, eS, nS, guS, ybS, goS, aS, gpS, s1S, g1S, s2S, g2S, ranks):
    T, D = aS.shape
    FF = eS.shape[1]
    pieces = T // CH
    per = D // ranks
    groups = per // 16
    blocks = 3 * groups + 2
    Z, Y, rows = 4, 2, T // ranks
    turned = (tabs[2][:, :CH].astype(f32) / CH).astype(bf16).T
    V, S = pltpu.VMEM, pltpu.SemaphoreType.DMA
    shard = (rows, D)
    scratch = [
        V((3, Z, Y, 2) + shard, bf16),
        V((blocks, Z, Y) + shard, bf16),
        V((blocks, Z) + shard, bf16),
        V((blocks, Z - 1) + shard, bf16),
        V((blocks, Z - 1) + shard, bf16),
        V((2, T, FF), bf16),
        V((2, T, D), bf16),
        V((2, ranks, groups, 16, T), bf16),
        V((2,) + s1S.shape, bf16),
        V((pieces + 1, 2 * CH, D), bf16),
        V((CH, 2 * CH), bf16),
        V((CH, 2 * CH), bf16),
        V((2,) + shard, f32),
        V((4, small.shape[0], D), f32),
        V((4, small.shape[0], D), f32),
        S((18,)), S((8,)), S((2, blocks)), S((2, blocks)), S((2, blocks, Z - 1)), S((2, blocks, Z - 1)), S((2, 4)),
    ]
    out_shape = [
        jax.ShapeDtypeStruct(s, f32)
        for s in ((per, FF), (per, FF), (per, D), (per, 3 * D), (2, rows, D), (small.shape[0], D))
    ]
    return pl.pallas_call(
        functools.partial(exchange_kernel, pieces),
        out_shape=out_shape,
        in_specs=[VM] + [ANY] * 14,
        out_specs=[ANY] * 5 + [VM],
        scratch_shapes=scratch,
        compiler_params=pltpu.CompilerParams(vmem_limit_bytes=VMEM_LIMIT, collective_id=0, has_side_effects=True),
        cost_estimate=pl.CostEstimate(flops=2 * T * 12 * D * D, bytes_accessed=40 << 20, transcendentals=0),
        name="exchange",
    )(small, tabs[1], turned, gdS, eS, nS, guS, ybS, goS, aS, gpS, s1S, g1S, s2S, g2S)


def dot_rows(x, y):
    return lax.dot_general(x, y, (((0,), (0,)), ((), ())), preferred_element_type=f32).astype(bf16)


def rows_of(chunks, low, high):
    parts, at = [], low
    while at < high:
        k, off = at // CH, at % CH
        size = min(CH - off, high - at)
        parts.append(chunks[k][off : off + size])
        at += size
    return parts[0] if len(parts) == 1 else jnp.concatenate(parts, axis=0)


def spread_rows(chunks, source, total, count, rank):
    share = total // count
    mine = None
    for r in range(count):
        rows = rows_of(chunks, r * share, (r + 1) * share)
        if r != source:
            rows = lax.ppermute(rows.astype(bf16), "section", [(source, r)]).astype(rows.dtype)
        mine = rows if mine is None else jnp.where(rank == r, rows, mine)
    return mine


def body(
    tokens, cotangent, norm_gains, norm_shifts, in_weight, in_bias, short_taps, long_filter, skip_gains,
    out_weight, out_bias, up_weight, up_bias, down_weight, down_bias,
):
    count = lax.axis_size("section")
    ranks = lax.axis_size("dp")
    rank = lax.axis_index("section")
    tok, cot = tokens[0], cotangent[0]
    T, D = tok.shape
    FF = up_weight.shape[2]
    pieces = T // CH
    steps = pieces + 2 * (count - 1)
    tabs = tables()
    as_rows = lambda x: x[0].astype(f32).reshape(-1, D)
    par = jnp.concatenate(
        [as_rows(x) for x in (norm_gains, norm_shifts, in_bias, short_taps, skip_gains, out_bias, down_bias, up_bias)], 0
    )
    win, wout, wup, wdown, filt = in_weight[0], out_weight[0], up_weight[0], down_weight[0], long_filter[0]

    outs, state, sent = [], None, []
    for t in range(steps):
        seg = t - 2 * rank
        active = (seg >= 0) & (seg < pieces)
        info = jnp.stack([jnp.clip(seg, 0, pieces - 1), active.astype(jnp.int32), (rank == 0).astype(jnp.int32)])
        arrived = sent[t - 2] if t >= 2 else tok[:CH]
        got = forward_call(info.astype(jnp.int32), par, tok, arrived, filt, win, wout, wup, wdown, tabs, state)
        outs.append(got[0])
        state = got[1:]
        if t + 2 < steps:
            sent.append(lax.ppermute(got[0], "section", [(i, i + 1) for i in range(count - 1)]))
    aS, hS, pS, y1S, ybS, mS, nS, eS, dS, s1S, s2S, k1S, k2S, _ = state
    kept = (hS, pS, y1S, mS, dS, k1S, k2S)
    stream = spread_rows(outs[2 * (count - 1) :], count - 1, T, count, rank)

    grads, state, sent = [], None, []
    for t in range(steps):
        seg = pieces - 1 - (t - 2 * (count - 1 - rank))
        active = (seg >= 0) & (seg < pieces)
        info = jnp.stack([jnp.clip(seg, 0, pieces - 1), active.astype(jnp.int32), (rank == count - 1).astype(jnp.int32)])
        arrived = sent[t - 2] if t >= 2 else cot[:CH]
        got = backward_call(info.astype(jnp.int32), par, cot, arrived, win, wout, wup, wdown, tabs, kept, state)
        grads.append(got[1])
        state = got[2:]
        if t + 2 < steps:
            sent.append(lax.ppermute(got[0], "section", [(i + 1, i) for i in range(count - 1)]))
    gdS, guS, goS, gpS, g1S, g2S, _, small = state
    token_grad = spread_rows(grads[2 * (count - 1) :][::-1], 0, T, count, rank)

    if ranks == 16 and D % (16 * ranks) == 0 and T == 64 * ranks and FF == 4 * D and pieces == 4:
        downT, up, out, inn, taps, small = exchange_call(
            small, tabs, gdS, eS, nS, guS, ybS, goS, aS, gpS, s1S, g1S, s2S, g2S, ranks
        )
        spot = lax.axis_index("dp")
        per = D // ranks
        head = lax.dynamic_slice_in_dim(small[:UPB], spot * per, per, 1)
        up_bias_grad = lax.dynamic_slice_in_dim(small[UPB:].reshape(-1), spot * (FF // ranks), FF // ranks, 0)
    else:
        slab = jnp.concatenate([dot_rows(gdS, eS), dot_rows(nS, guS), dot_rows(ybS, goS), dot_rows(aS, gpS)], axis=1)
        taps = jnp.concatenate([filter_call(s1S, g1S, tabs), filter_call(s2S, g2S, tabs)], axis=1)
        small = jnp.sum(small, axis=1)
        per = D // ranks
        mini = jnp.concatenate(
            [small[:UPB].reshape(UPB, ranks, per).transpose(1, 0, 2).reshape(ranks, -1), small[UPB:].reshape(ranks, -1)], axis=1
        )
        scatter = lambda x: lax.psum_scatter(x, "dp", scatter_dimension=0, tiled=True).astype(f32)
        slab, taps, mini = scatter(slab), scatter(taps), scatter(mini)[0]
        head = mini[: UPB * per].reshape(UPB, per)
        up_bias_grad = mini[UPB * per :]
        taps = taps.reshape(-1, 2, D).transpose(1, 0, 2)
        downT, up, out, inn = (slab[:, i:j] for i, j in ((0, FF), (FF, 2 * FF), (2 * FF, 2 * FF + D), (2 * FF + D, None)))
    return (
        stream[None],
        token_grad[None],
        head[GAIN : GAIN + 2][None],
        head[SHIFT : SHIFT + 2][None],
        inn[None],
        head[INB : INB + 3][None],
        head[TAP : TAP + 9].reshape(1, 3, 3, per),
        taps[None],
        head[SKIP : SKIP + 2][None],
        out[None],
        head[OUTB][None],
        up[None],
        up_bias_grad[None],
        downT.T[None],
        head[DOWNB][None],
    )


def solution(mesh):
    whole = P("dp", None, None)
    split = lambda n: P("section", *([None] * n))
    return jax.shard_map(
        body,
        mesh=mesh,
        in_specs=(
            whole, whole, split(2), split(2), split(2), split(2), split(3), split(3), split(2), split(2), split(1),
            split(2), split(1), split(2), split(1),
        ),
        out_specs=(
            P("dp", "section", None),
            P("dp", "section", None),
            P("section", None, "dp"),
            P("section", None, "dp"),
            P("section", "dp", None),
            P("section", None, "dp"),
            P("section", None, None, "dp"),
            P("section", None, "dp", None),
            P("section", None, "dp"),
            P("section", "dp", None),
            P("section", "dp"),
            P("section", "dp", None),
            P("section", "dp"),
            P("section", None, "dp"),
            P("section", "dp"),
        ),
        check_vma=False,
    )
```

```python
import functools
import math

import jax
import jax.numpy as jnp
import ml_dtypes
import numpy as np
from jax import lax
from jax.experimental import pallas as pl
from jax.experimental.pallas import tpu as pltpu
from jax.sharding import PartitionSpec as P

CH = 256
FT = 512
CARRY = 8
f32, bf16 = jnp.float32, jnp.bfloat16
VMEM_LIMIT = 60 * 1024 * 1024
ANY = pl.BlockSpec(memory_space=pl.ANY)
SMEM = pl.BlockSpec(memory_space=pltpu.SMEM)
VM = pl.BlockSpec(memory_space=pltpu.VMEM)

GAIN, SHIFT, INB, TAP, SKIP, OUTB, DOWNB, UPB = 0, 2, 4, 7, 16, 18, 19, 20


def tables():
    order = np.concatenate([np.arange(0, CH, 2), np.arange(1, CH, 2)])
    angle = np.pi * ((2 * order[:, None] + 1) * np.arange(CH)[None] % (4 * CH)) / (2 * CH)
    cos, sin = np.cos(angle), np.sin(angle)
    sign = np.where(order % 2 == 0, 1.0, -1.0)[:, None]
    spread = np.concatenate([cos, -sin], 0)
    turned = np.concatenate([sign * sin, sign * cos], 0)
    as_low = lambda t: jnp.asarray(t.astype(ml_dtypes.bfloat16))
    return as_low(spread), as_low(spread.T / CH), as_low(np.concatenate([turned, spread], 1))


def dot(x, y):
    return jnp.dot(x, y, preferred_element_type=f32)


def dot_nt(x, y):
    return lax.dot_general(x, y, (((1,), (1,)), ((), ())), preferred_element_type=f32)


def rows_at(index, size):
    return pl.ds(pl.multiple_of(index * size, size), size)


def for_rows(total, size, step):
    def run(i, carry):
        step(pl.multiple_of(i * size, size))
        return carry

    lax.fori_loop(0, total // size, run, 0)


def normalize(rows):
    average = jnp.mean(rows, axis=-1, keepdims=True)
    centered = rows - average
    scale = lax.rsqrt(jnp.mean(centered * centered, axis=-1, keepdims=True) + 1e-05)
    return centered * scale, scale


def norm_back(z, gain, unit, scale):
    w = z * gain
    return (
        w - jnp.mean(w, axis=-1, keepdims=True) - unit * jnp.mean(w * unit, axis=-1, keepdims=True)
    ) * scale


def gelu_pair(u):
    t = 1.0 / (1.0 + (0.3275911 * math.sqrt(0.5)) * jnp.abs(u))
    series = t * (
        0.5 * 0.254829592
        + t * (0.5 * -0.284496736 + t * (0.5 * 1.421413741 + t * (0.5 * -1.453152027 + t * (0.5 * 1.061405429))))
    )
    bell = jnp.exp(-0.5 * (u * u))
    tail = series * bell
    phi_sum = jnp.where(u >= 0, 1.0 - tail, tail)
    return u * phi_sum, phi_sum + u * (bell * (1.0 / math.sqrt(2.0 * math.pi)))


def mix_spectra(left, right, out, low, high, left_of, conj):
    width = out.shape[1] // 2

    def tile(i, carry):
        r = pl.multiple_of(i * 16, 16)
        for half in range(2):
            cols = slice(half * width, (half + 1) * width)

            def term(j, acc):
                k = left_of(j)
                ar = left[k, pl.ds(r, 16), cols].astype(f32)
                ai = left[k, pl.ds(CH + r, 16), cols].astype(f32)
                br = right[j, pl.ds(r, 16), cols].astype(f32)
                bi = right[j, pl.ds(CH + r, 16), cols].astype(f32)
                if conj:
                    return acc[0] + (ar * br + ai * bi), acc[1] + (ar * bi - ai * br)
                return acc[0] + (ar * br - ai * bi), acc[1] + (ar * bi + ai * br)

            zero = jnp.zeros((16, width), f32)
            real, imag = lax.fori_loop(low, high, term, (zero, zero))
            out[pl.ds(r, 16), cols] = real.astype(out.dtype)
            out[pl.ds(CH + r, 16), cols] = imag.astype(out.dtype)
        return carry

    lax.fori_loop(0, CH // 16, tile, 0)


def fold_rows(x):
    return jnp.sum(x.reshape(x.shape[0] // 8, 8, x.shape[1]), axis=0)


def pieces_of(at, wide, D):
    spans, off = [], 0
    while off < wide:
        row, col = (at + off) // D, (at + off) % D
        size = min(D - col, wide - off)
        spans.append((row, col, off, size))
        off += size
    return spans


def pass_kernel(
    sections, pieces, par, tokens, cots, filt, win, wout, wup, wdown, spread_h, back_h, pair_h,
    stream, gtok, aS, ybS, nS, eS, s1S, s2S, gdS, guS, goS, gpS, g1S, g2S, smallO,
    inf, inb, gin, winb, woutb, wupb, wdownb, spread, back, pair, k1, k2, sp1, sp2, pall, y1all, mall, dall,
    ab, lead, leadlow, spec, wide, gate2, mid, nb, tile2, hid, outb, outfb, gnb, gqb, gpb, small,
    wsem, osem, fsem, bsem, ssem, gsem,
):
    rank = lax.axis_index("section")
    first, final = rank == 0, rank == sections - 1
    D, FF = woutb.shape[0], wupb.shape[1]
    tiles = FF // FT
    T = pieces * CH
    share = T // sections
    sub = min(CH, share)
    at = lambda r: {"section": r}

    def when(condition):
        return pl.when(condition)

    def remote(src, dst, send, recv, r):
        return pltpu.make_async_remote_copy(
            src_ref=src, dst_ref=dst, send_sem=send, recv_sem=recv, device_id=at(r), device_id_type=pl.DeviceIdType.MESH
        )

    def local(src, dst, sem):
        return pltpu.make_async_copy(src, dst, sem)

    loads = [
        local(win, winb, wsem.at[0]),
        local(wout, woutb, wsem.at[1]),
        local(wup, wupb, wsem.at[2]),
        local(wdown, wdownb, wsem.at[3]),
        local(spread_h, spread, wsem.at[4]),
        local(back_h, back, wsem.at[5]),
        local(pair_h, pair, wsem.at[6]),
    ]
    fill = [local(filt.at[f, pl.ds(0, CH)], sp.at[0, pl.ds(CH, CH)], wsem.at[7 + f]) for f, sp in enumerate((sp1, sp2))]
    for seg in range(1, pieces):
        window = pl.ds((seg - 1) * CH, 2 * CH)
        fill += [local(filt.at[f, window], sp.at[seg], wsem.at[7 + 2 * seg + f]) for f, sp in enumerate((sp1, sp2))]

    def own_chunk(src, dst, seg, sems):
        return local(src.at[rows_at(seg, CH)], dst.at[seg], sems.at[1, seg])

    def relay(src, dst, seg, sems, r):
        return remote(src, dst.at[seg], sems.at[0, seg], sems.at[1, seg], r)

    @when(first)
    def _():
        for seg in range(pieces):
            own_chunk(tokens, inf, seg, fsem).start()

    loads[0].start()
    for copy in fill:
        copy.start()
    for k in (6, 4, 5, 1, 2, 3):
        loads[k].start()

    @when(final)
    def _():
        for seg in range(pieces):
            own_chunk(cots, inb, seg, bsem).start()

    barrier = pltpu.get_barrier_semaphore()
    for r in range(sections):

        @when(rank != r)
        def _(r=r):
            pl.semaphore_signal(barrier, inc=1, device_id=at(r), device_id_type=pl.DeviceIdType.MESH)

    pl.semaphore_wait(barrier, sections - 1)

    pall[pl.ds(0, 16), :] = jnp.zeros((16, 3 * D), bf16)
    for sp in (sp1, sp2):
        sp[0, pl.ds(0, CH), :] = jnp.zeros((CH, D), bf16)
    small[...] = jnp.zeros(small.shape, f32)
    gqb[pl.ds(CH, CARRY), :] = jnp.zeros((CARRY, 3 * D), f32)

    def filter_spectra(seg):
        k1[seg] = dot(pair[...], sp1[seg]).astype(bf16)
        k2[seg] = dot(pair[...], sp2[seg]).astype(bf16)

    @when(jnp.logical_not(first))
    def _():
        for copy in fill:
            copy.wait()
        loads[6].wait()

        def run(seg, carry):
            filter_spectra(seg)
            return carry

        lax.fori_loop(0, pieces, run, 0)

    def out_parts(seg, src, dst, sems, to_self):
        found = []
        for j in range(CH // sub):
            row = seg * CH + j * sub
            r, off = row // share, row % share
            found.append((r, off, src.at[pl.ds(j * sub, sub)], sems.at[0, seg * (CH // sub) + j], off // sub))
        return found

    def put(src, dst, k):
        return local(src, dst, osem.at[k])

    def forward_chunk(seg, carry):
        here = rows_at(seg, CH)
        base = pl.multiple_of(seg * CH, CH)
        hb = inf.at[seg]
        slot = 0
        later = seg > 0

        def before(copy):
            @when(later)
            def _():
                copy.wait()

        puts = [
            put(ab, aS.at[here], 0), put(sp1.at[seg], s1S.at[seg], 1), put(sp2.at[seg], s2S.at[seg], 2),
            put(leadlow, ybS.at[here], 3), put(nb, nS.at[here], 4), put(hid, eS.at[here], 5),
        ]

        @when(first)
        def _():
            own_chunk(tokens, inf, seg, fsem).wait()

        @when(jnp.logical_not(first))
        def _():
            relay(outb.at[slot], inf, seg, fsem, rank).wait_recv()

        before(puts[0])

        def ln1(r):
            unit, _ = normalize(hb[pl.ds(r, 64), :].astype(f32))
            ab[pl.ds(r, 64), :] = (unit * par[GAIN : GAIN + 1, :] + par[SHIFT : SHIFT + 1, :]).astype(bf16)

        for_rows(CH, 64, ln1)
        puts[0].start()

        @when(seg == 0)
        def _():
            loads[0].wait()

        for b in range(3):
            cols = slice(b * D, (b + 1) * D)
            value = dot(ab[...], winb[:, cols]) + par[INB + b : INB + b + 1, :]
            pall[pl.ds(pl.multiple_of(base + 16, 16), CH), cols] = value.astype(bf16)

        before(puts[3])

        def short(r):
            got = [branch(base + r, b)[0] for b in range(3)]
            gate2[pl.ds(r, 32), :] = got[2]
            s = got[0] * got[1]
            lead[pl.ds(r, 32), :] = s
            leadlow[pl.ds(r, 32), :] = s.astype(bf16)

        for_rows(CH, 32, short)

        @when(first)
        def _():
            @when(seg == 0)
            def _():
                for copy in fill:
                    copy.wait()
                loads[6].wait()

            filter_spectra(seg)

        @when(seg == 0)
        def _():
            loads[4].wait()
            loads[5].wait()

        sp1[seg] = dot(spread[...], leadlow[...]).astype(bf16)
        puts[1].start()
        mix_spectra(k1, sp1, spec, 0, seg + 1, lambda j: seg - j, False)
        wide[...] = dot(back[...], spec[...])

        def second(r):
            rows = pl.ds(r, 64)
            y = wide[rows, :] + par[SKIP : SKIP + 1, :] * lead[rows, :]
            y1all[seg, rows, :] = y.astype(bf16)
            trail = y * gate2[rows, :]
            lead[rows, :] = trail
            leadlow[rows, :] = trail.astype(bf16)

        for_rows(CH, 64, second)
        sp2[seg] = dot(spread[...], leadlow[...]).astype(bf16)
        puts[2].start()
        mix_spectra(k2, sp2, spec, 0, seg + 1, lambda j: seg - j, False)
        leadlow[...] = (dot(back[...], spec[...]) + par[SKIP + 1 : SKIP + 2, :] * lead[...]).astype(bf16)
        puts[3].start()

        @when(seg == 0)
        def _():
            loads[1].wait()

        wide[...] = dot(leadlow[...], woutb[...])
        before(puts[4])

        def ln2(r):
            rows = pl.ds(r, 64)
            m = hb[rows, :].astype(f32) + (wide[rows, :] + par[OUTB : OUTB + 1, :])
            mall[seg, rows, :] = m.astype(bf16)
            unit, _ = normalize(m)
            nb[rows, :] = (unit * par[GAIN + 1 : GAIN + 2, :] + par[SHIFT + 1 : SHIFT + 2, :]).astype(bf16)
            mid[rows, :] = m + par[DOWNB : DOWNB + 1, :]

        for_rows(CH, 64, ln2)
        puts[4].start()

        @when(seg == 0)
        def _():
            loads[2].wait()
            loads[3].wait()

        before(puts[5])

        def up(k):
            return dot(nb[...], wupb[:, k * FT : (k + 1) * FT])

        def act(k):
            spans = pieces_of(k * FT, FT, D)
            bias = [par[UPB + row : UPB + row + 1, col : col + size] for row, col, _, size in spans]
            bias = bias[0] if len(bias) == 1 else jnp.concatenate(bias, axis=1)
            e, d = gelu_pair(tile2[k % 2] + bias)
            hid[:, k * FT : (k + 1) * FT] = e.astype(bf16)
            dall[seg, :, k * FT : (k + 1) * FT] = d.astype(bf16)

        def down(k):
            mid[...] += dot(hid[:, k * FT : (k + 1) * FT], wdownb[k * FT : (k + 1) * FT, :])

        tile2[0] = up(0)
        for k in range(tiles):
            if k + 1 < tiles:
                tile2[(k + 1) % 2] = up(k + 1)
            act(k)
            if k >= 1:
                down(k - 1)
        down(tiles - 1)
        puts[5].start()

        @when(later)
        def _():
            finish_out(seg - 1, slot)

        outb[slot] = mid[...].astype(bf16)

        @when(jnp.logical_not(final))
        def _():
            relay(outb.at[slot], inf, seg, fsem, rank + 1).start()

        @when(final)
        def _():
            for r, off, src, sem, k in out_parts(seg, outb.at[slot], stream, ssem, None):

                @when(r != rank)
                def _():
                    remote(src, stream.at[pl.ds(pl.multiple_of(off, sub), sub)], sem, ssem.at[1, k], r).start()

                @when(r == rank)
                def _():
                    local(src, stream.at[pl.ds(pl.multiple_of(off, sub), sub)], sem).start()

        return carry

    def finish_out(seg, slot):
        @when(jnp.logical_not(final))
        def _():
            relay(outb.at[slot], inf, seg, fsem, rank + 1).wait_send()

        @when(final)
        def _():
            for r, off, src, sem, k in out_parts(seg, outb.at[slot], stream, ssem, None):

                @when(r != rank)
                def _():
                    remote(src, stream.at[pl.ds(pl.multiple_of(off, sub), sub)], sem, ssem.at[1, k], r).wait_send()

                @when(r == rank)
                def _():
                    local(src, stream.at[pl.ds(pl.multiple_of(off, sub), sub)], sem).wait()

    def branch(start, b):
        rows = pall[pl.ds(pl.multiple_of(start, 16), 48), b * D : (b + 1) * D].astype(f32)
        late = [rows[16 - i : 48 - i] for i in range(3)]
        t = [par[TAP + 3 * i + b : TAP + 3 * i + b + 1, :] for i in range(3)]
        return t[0] * late[0] + t[1] * late[1] + t[2] * late[2], late

    lax.fori_loop(0, pieces, forward_chunk, 0)
    last = pieces - 1
    here = rows_at(last, CH)
    for copy in (
        put(ab, aS.at[here], 0), put(sp1.at[last], s1S.at[last], 1), put(sp2.at[last], s2S.at[last], 2),
        put(leadlow, ybS.at[here], 3), put(nb, nS.at[here], 4), put(hid, eS.at[here], 5),
    ):
        copy.wait()
    for k in range(last):
        put(sp1.at[k], s1S.at[k], 1).wait()
        put(sp2.at[k], s2S.at[k], 2).wait()
    finish_out(last, 0)

    def add_small(k, x, cols=slice(None)):
        small[k, :, cols] += fold_rows(x)

    def backward_chunk(i, carry):
        seg = pieces - 1 - i
        here = rows_at(seg, CH)
        base = pl.multiple_of(seg * CH, CH)
        gdb, hb = inb.at[seg], inf.at[seg]
        slot = 0

        def before(copy):
            @when(i > 0)
            def _():
                copy.wait()

        puts = [
            put(gdb, gdS.at[here], 6), put(hid, guS.at[here], 7), put(nb, goS.at[here], 8), put(gpb, gpS.at[here], 9),
            put(sp2.at[seg], g2S.at[seg], 10), put(sp1.at[seg], g1S.at[seg], 11),
        ]

        @when(final)
        def _():
            own_chunk(cots, inb, seg, bsem).wait()

        @when(jnp.logical_not(final))
        def _():
            relay(outb.at[slot], inb, seg, bsem, rank).wait_recv()

        before(puts[0])
        puts[0].start()
        before(puts[1])

        def down(k):
            return dot_nt(gdb[...], wdownb[k * FT : (k + 1) * FT, :])

        def act(k):
            cols = slice(k * FT, (k + 1) * FT)
            gu = (dall[seg, :, cols].astype(f32) * tile2[k % 2]).astype(bf16)
            hid[:, cols] = gu
            total = fold_rows(gu.astype(f32))
            for row, col, off, size in pieces_of(k * FT, FT, D):
                small[UPB + row, :, col : col + size] += total[:, off : off + size]

        def up(k):
            part = dot_nt(hid[:, k * FT : (k + 1) * FT], wupb[:, k * FT : (k + 1) * FT])
            if k == 0:
                gnb[...] = part
            else:
                gnb[...] += part

        tile2[0] = down(0)
        for k in range(tiles):
            if k + 1 < tiles:
                tile2[(k + 1) % 2] = down(k + 1)
            act(k)
            if k >= 1:
                up(k - 1)
        up(tiles - 1)
        puts[1].start()
        before(puts[2])

        def ln2(r):
            rows = pl.ds(r, 32)
            unit, scale = normalize(mall[seg, rows, :].astype(f32))
            z = gnb[rows, :]
            gd = gdb[rows, :].astype(f32)
            gm = gd + norm_back(z, par[GAIN + 1 : GAIN + 2, :], unit, scale)
            mid[rows, :] = gm
            go = gm.astype(bf16)
            nb[rows, :] = go
            add_small(GAIN + 1, z * unit)
            add_small(SHIFT + 1, z)
            add_small(OUTB, go.astype(f32))
            add_small(DOWNB, gd)

        for_rows(CH, 32, ln2)
        puts[2].start()
        gy = dot_nt(nb[...], woutb[...])
        lead[...] = gy
        leadlow[...] = gy.astype(bf16)
        sp2[seg] = dot(spread[...], leadlow[...]).astype(bf16)
        puts[4].start()
        mix_spectra(k2, sp2, spec, seg, pieces, lambda j: j - seg, True)
        wide[...] = dot(back[...], spec[...])

        def keep(r, b, grad, late):
            gqb[pl.ds(r, 32), b * D : (b + 1) * D] = grad
            for tap in range(3):
                add_small(TAP + 3 * tap + b, grad * late[tap])

        def second(r):
            rows = pl.ds(r, 32)
            gate, late = branch(base + r, 2)
            y1 = y1all[seg, rows, :].astype(f32)
            gy2 = lead[rows, :]
            gs2 = wide[rows, :] + par[SKIP + 1 : SKIP + 2, :] * gy2
            gy1 = gs2 * gate
            gate2[rows, :] = gy1
            leadlow[rows, :] = gy1.astype(bf16)
            add_small(SKIP + 1, gy2 * (y1 * gate))
            keep(r, 2, gs2 * y1, late)

        for_rows(CH, 32, second)
        sp1[seg] = dot(spread[...], leadlow[...]).astype(bf16)
        puts[5].start()
        mix_spectra(k1, sp1, spec, seg, pieces, lambda j: j - seg, True)
        wide[...] = dot(back[...], spec[...])

        def lower(r):
            rows = pl.ds(r, 32)
            carrier, late_carrier = branch(base + r, 0)
            gate, late_gate = branch(base + r, 1)
            gy1 = gate2[rows, :]
            gs1 = wide[rows, :] + par[SKIP : SKIP + 1, :] * gy1
            add_small(SKIP, gy1 * (carrier * gate))
            keep(r, 0, gs1 * gate, late_carrier)
            keep(r, 1, gs1 * carrier, late_gate)

        for_rows(CH, 32, lower)
        before(puts[3])

        def short(r):
            for b in range(3):
                cols = slice(b * D, (b + 1) * D)
                rows = gqb[pl.ds(r, 32 + CARRY), cols]
                t = [par[TAP + 3 * tap + b : TAP + 3 * tap + b + 1, :] for tap in range(3)]
                gp = (t[0] * rows[:32] + t[1] * rows[1:33] + t[2] * rows[2:34]).astype(bf16)
                gpb[pl.ds(r, 32), cols] = gp
                add_small(INB + b, gp.astype(f32))

        for_rows(CH, 32, short)
        puts[3].start()
        gqb[pl.ds(CH, CARRY), :] = gqb[pl.ds(0, CARRY), :]
        gnb[...] = dot_nt(gpb[...], winb[...])

        @when(i > 0)
        def _():
            finish_grad(i - 1, slot)

        def ln1(r):
            rows = pl.ds(r, 32)
            unit, scale = normalize(hb[rows, :].astype(f32))
            z = gnb[rows, :]
            gh = mid[rows, :] + norm_back(z, par[GAIN : GAIN + 1, :], unit, scale)
            outfb[slot, rows, :] = gh
            outb[slot, rows, :] = gh.astype(bf16)
            add_small(GAIN, z * unit)
            add_small(SHIFT, z)

        for_rows(CH, 32, ln1)

        @when(jnp.logical_not(first))
        def _():
            relay(outb.at[slot], inb, seg, bsem, rank - 1).start()

        @when(first)
        def _():
            for r, off, src, sem, k in out_parts(seg, outb.at[slot], gtok, gsem, None):
                whole = outfb.at[slot, pl.ds(lax.rem(seg * CH + off, CH) if sub < CH else 0, sub)]

                @when(r != rank)
                def _():
                    remote(src, gin.at[k], sem, gsem.at[1, k], r).start()

                @when(r == rank)
                def _():
                    local(whole, gtok.at[pl.ds(pl.multiple_of(off, sub), sub)], sem).start()

        return carry

    def finish_grad(i, slot):
        seg = pieces - 1 - i

        @when(jnp.logical_not(first))
        def _():
            relay(outb.at[slot], inb, seg, bsem, rank - 1).wait_send()

        @when(first)
        def _():
            for r, off, src, sem, k in out_parts(seg, outb.at[slot], gtok, gsem, None):
                whole = outfb.at[slot, pl.ds(0, sub)]

                @when(r != rank)
                def _():
                    remote(src, gin.at[k], sem, gsem.at[1, k], r).wait_send()

                @when(r == rank)
                def _():
                    local(whole, gtok.at[pl.ds(pl.multiple_of(off, sub), sub)], sem).wait()

    lax.fori_loop(0, pieces, backward_chunk, 0)
    here = rows_at(0, CH)
    ends = [
        put(inb.at[0], gdS.at[here], 6), put(hid, guS.at[here], 7), put(nb, goS.at[here], 8), put(gpb, gpS.at[here], 9),
        put(sp2.at[0], g2S.at[0], 10), put(sp1.at[0], g1S.at[0], 11),
    ]
    for copy in ends:
        copy.wait()
    for k in range(last):
        ends[4].wait()
        ends[5].wait()
    total = put(small, smallO, 12)
    total.start()
    finish_grad(last, 0)
    parts = share // sub

    @when(jnp.logical_not(final))
    def _():
        for k in range(parts):
            remote(outb.at[0, pl.ds(0, sub)], stream.at[pl.ds(k * sub, sub)], ssem.at[0, 0], ssem.at[1, k], rank).wait_recv()

    @when(jnp.logical_not(first))
    def _():
        for k in range(parts):
            remote(outb.at[0, pl.ds(0, sub)], gin.at[k], gsem.at[0, 0], gsem.at[1, k], rank).wait_recv()
            outfb[0, pl.ds(0, sub), :] = gin[k].astype(f32)
            copy = local(outfb.at[0, pl.ds(0, sub)], gtok.at[pl.ds(k * sub, sub)], gsem.at[0, k])
            copy.start()
            copy.wait()

    total.wait()


def pass_call(par, tokens, cots, filt, win, wout, wup, wdown, tabs, sections):
    T, D = tokens.shape
    FF = wup.shape[1]
    pieces = T // CH
    share = T // sections
    sub = min(CH, share)
    spec3 = (pieces, 2 * CH, D)
    small = (UPB + FF // D, 8, D)
    shapes = [
        ((share, D), bf16), ((share, D), f32),
        ((T, D), bf16), ((T, D), bf16), ((T, D), bf16), ((T, FF), bf16), (spec3, bf16), (spec3, bf16),
        ((T, D), bf16), ((T, FF), bf16), ((T, D), bf16), ((T, 3 * D), bf16), (spec3, bf16), (spec3, bf16),
        (small, f32),
    ]
    V, S = pltpu.VMEM, pltpu.SemaphoreType.DMA
    chunk, chunks = (CH, D), (pieces, CH, D)
    scratch = [
        V(chunks, bf16), V(chunks, bf16), V((share // sub, sub, D), bf16),
        V(win.shape, bf16), V(wout.shape, bf16), V(wup.shape, bf16), V(wdown.shape, bf16),
        V((2 * CH, CH), bf16), V((CH, 2 * CH), bf16), V((2 * CH, 2 * CH), bf16),
        V(spec3, bf16), V(spec3, bf16), V(spec3, bf16), V(spec3, bf16),
        V((16 + T, 3 * D), bf16), V(chunks, bf16), V(chunks, bf16), V((pieces, CH, FF), bf16),
        V(chunk, bf16), V(chunk, f32), V(chunk, bf16), V((2 * CH, D), bf16), V(chunk, f32), V(chunk, f32), V(chunk, f32),
        V(chunk, bf16), V((2, CH, FT), f32), V((CH, FF), bf16), V((1,) + chunk, bf16), V((1,) + chunk, f32),
        V(chunk, f32), V((CH + CARRY, 3 * D), f32), V((CH, 3 * D), bf16), V(small, f32),
        S((7 + 2 * pieces,)), S((13,)), S((2, pieces)), S((2, pieces)), S((2, T // sub)), S((2, T // sub)),
    ]
    return pl.pallas_call(
        functools.partial(pass_kernel, sections, pieces),
        out_shape=[jax.ShapeDtypeStruct(*s) for s in shapes],
        in_specs=[VM] + [ANY] * 10,
        out_specs=[ANY] * len(shapes),
        scratch_shapes=scratch,
        compiler_params=pltpu.CompilerParams(vmem_limit_bytes=63 * 1024 * 1024, collective_id=1, has_side_effects=True),
        name="layer_pass",
    )(par, tokens, cots, filt, win, wout, wup, wdown, *tabs)


def filter_kernel(pieces, s, g, back, turned, out, q):
    width = s.shape[2] // 2

    for d in range(pieces):

        def tile(i, carry, d=d):
            r = pl.multiple_of(i * 16, 16)
            for half in range(2):
                cols = slice(half * width, (half + 1) * width)
                real = jnp.zeros((16, width), f32)
                imag = jnp.zeros((16, width), f32)
                for k in range(d, pieces):
                    ar = s[k - d, pl.ds(r, 16), cols].astype(f32)
                    ai = s[k - d, pl.ds(CH + r, 16), cols].astype(f32)
                    br = g[k, pl.ds(r, 16), cols].astype(f32)
                    bi = g[k, pl.ds(CH + r, 16), cols].astype(f32)
                    real = real + (ar * br + ai * bi)
                    imag = imag + (ar * bi - ai * br)
                q[d, pl.ds(r, 16), cols] = real.astype(bf16)
                q[d, pl.ds(CH + r, 16), cols] = imag.astype(bf16)
            return carry

        lax.fori_loop(0, CH // 16, tile, 0)
    for d in range(pieces):
        rows = dot(back[...], q[d])
        if d + 1 < pieces:
            rows += dot(turned[...], q[d + 1])
        out[pl.ds(d * CH, CH), :] = rows.astype(bf16)


def filter_call(s, g, tabs):
    pieces, _, D = s.shape
    turned = (tabs[2][:, :CH].astype(f32) / CH).astype(bf16).T
    return pl.pallas_call(
        functools.partial(filter_kernel, pieces),
        out_shape=jax.ShapeDtypeStruct((pieces * CH, D), bf16),
        in_specs=[VM] * 4,
        out_specs=VM,
        scratch_shapes=[pltpu.VMEM(s.shape, bf16)],
        compiler_params=pltpu.CompilerParams(vmem_limit_bytes=VMEM_LIMIT),
        name="filter_grad",
    )(s, g, tabs[1], turned)


def exchange_kernel(
    pieces, small_in, back_h, turned_h, gdS, eS, nS, guS, ybS, goS, aS, gpS, s1S, g1S, s2S, g2S,
    downT, upO, outO, inO, filtO, smallO,
    x, r1, r2, rr, rl, gb, lb, lt, sb, qb, back, turned, ob, mine, got, lsem, osem, csem, ysem, rsem, fsem, msem,
):
    D = lb.shape[2]
    me = lax.axis_index("dp")
    c, y, z = me % 2, (me // 2) % 2, me // 4
    Z = r2.shape[1]
    groups = lt.shape[2]
    n_blocks = 3 * groups + 2
    at = lambda i: {"dp": i}
    core_id, y_id = me + 1 - 2 * c, me + 2 - 4 * y
    mates = (core_id, y_id, me + 4 - 8 * (z % 2), me + 8 - 16 * (z // 2))
    inner = (z == 1) | (z == 2)

    barrier = pltpu.get_barrier_semaphore()
    for mate in mates:
        pl.semaphore_signal(barrier, inc=1, device_id=at(mate), device_id_type=pl.DeviceIdType.MESH)

    @pl.when(inner)
    def _():
        other = me + 12 - 8 * z
        pl.semaphore_signal(barrier, inc=1, device_id=at(other), device_id_type=pl.DeviceIdType.MESH)

    @pl.when(inner)
    def _():
        pl.semaphore_wait(barrier, len(mates) + 1)

    @pl.when(jnp.logical_not(inner))
    def _():
        pl.semaphore_wait(barrier, len(mates))

    def remote(src, dst, send, recv, mate):
        return pltpu.make_async_remote_copy(
            src_ref=src, dst_ref=dst, send_sem=send, recv_sem=recv, device_id=at(mate),
            device_id_type=pl.DeviceIdType.MESH,
        )

    def load(src, dst, k):
        return pltpu.make_async_copy(src, dst, lsem.at[k])

    rights = ((eS,), (guS,), (goS, gpS))
    lefts = ((gdS,), (nS,), (ybS, aS))

    def loads(m):
        found, off = [], 0
        for k, src in enumerate(rights[m]):
            wide = src.shape[1]
            found.append(load(src, gb.at[m % 2, :, pl.ds(off, wide)], 4 * m + k))
            off += wide
        for k, src in enumerate(lefts[m]):
            found.append(load(src, lb.at[k], 4 * m + 2 + k))
        return found

    def spectra(f):
        src = ((s1S, g1S), (s2S, g2S))[f]
        return [load(src[k], sb.at[k], 12 + 2 * f + k) for k in range(2)]

    def turn(m):
        for k in range(len(lefts[m])):

            def part(i, carry, k=k):
                rows = pl.multiple_of(i * 128, 128)
                piece = jnp.transpose(lb[k, pl.ds(rows, 128), :])
                lt[k, :, :, :, pl.ds(rows, 128)] = piece.reshape(lt.shape[1:4] + (128,))
                return carry

            lax.fori_loop(0, lb.shape[1] // 128, part, 0)

    def product(m, g, slot):
        def part(i, carry):
            k = jnp.minimum(i, 1) if m == 2 else 0
            left = lt[k, :, g].reshape(16 * lt.shape[1], lt.shape[4])
            cols = pl.ds(pl.multiple_of(i * D, D), D)
            value = dot(left, gb[m % 2, :, cols]).astype(bf16)
            x[slot, :, :, :, pl.ds(pl.multiple_of(i * 16, 16), 16), :] = value.reshape(x.shape[1:4] + (16, D))
            return carry

        lax.fori_loop(0, 4, part, 0)

    def filters(f, slot):
        def mix(d, carry):
            mix_spectra(sb.at[0], sb.at[1], qb.at[d], d, pieces, lambda j: j - d, True)
            return carry

        lax.fori_loop(0, pieces, mix, 0)
        qb[pieces] = jnp.zeros(qb.shape[1:], bf16)

        def part(d, carry):
            rows = dot(back[...], qb[d]) + dot(turned[...], qb[d + 1])
            x[slot, d] = rows.astype(bf16).reshape(x.shape[2:])
            return carry

        lax.fori_loop(0, pieces, part, 0)

    def core_copy(b, slot):
        return remote(x.at[slot, :, :, 1 - c], r1.at[b], csem.at[0, b], csem.at[1, b], core_id)

    def y_copy(b):
        return remote(r1.at[b, :, 1 - y], r2.at[b], ysem.at[0, b], ysem.at[1, b], y_id)

    def right_copy(b, d, src):
        return remote(src, rr.at[b, d - 1], rsem.at[0, b, d - 1], rsem.at[1, b, d - 1], me + 4)

    def left_copy(b, d, src):
        return remote(src, rl.at[b, d], fsem.at[0, b, d], fsem.at[1, b, d], me - 4)

    def add(p, q):
        return (p.astype(f32) + q.astype(f32)).astype(bf16)

    def after_core(b):
        slot = b % x.shape[0]
        core_copy(b, slot).wait()

        def part(i, carry):
            for j in range(2):
                r1[b, i, j] = add(r1[b, i, j], x[slot, i, j, c])
            return carry

        lax.fori_loop(0, Z, part, 0)
        y_copy(b).start()

    def after_y(b):
        y_copy(b).wait()

        def part(i, carry):
            r2[b, i] = add(r2[b, i], r1[b, i, y])
            return carry

        lax.fori_loop(0, Z, part, 0)

    def hop(b, h):
        @pl.when(z == h)
        def _():
            for d in range(Z - 1, h, -1):
                if h > 0:
                    right_copy(b, d, r2.at[b, d]).wait_recv()
                    rr[b, d - 1] = add(rr[b, d - 1], r2[b, d])
                right_copy(b, d, r2.at[b, d] if h == 0 else rr.at[b, d - 1]).start()

        @pl.when(z == Z - 1 - h)
        def _():
            for d in range(Z - 1 - h):
                if h > 0:
                    left_copy(b, d, r2.at[b, d]).wait_recv()
                    rl[b, d] = add(rl[b, d], r2[b, d])
                left_copy(b, d, r2.at[b, d] if h == 0 else rl.at[b, d]).start()

    def out_copies(b, slot):
        kind, a, g = order[b]
        src = ob.at[slot]
        if kind == "filter":
            return [pltpu.make_async_copy(src, filtO.at[a], osem.at[4 * slot])]
        found = []
        rows = pl.ds(g * 16, 16)
        for k in range(4):
            if a < 2:
                dst = (downT, upO)[a].at[rows, pl.ds(k * D, D)]
            elif k == 0:
                dst = outO.at[rows]
            else:
                dst = inO.at[rows, pl.ds((k - 1) * D, D)]
            found.append(pltpu.make_async_copy(src.at[pl.ds(16 * k, 16)], dst, osem.at[4 * slot + k]))
        return found

    def finish(b):
        slot = b % 2
        if b >= 2:
            for copy in out_copies(b - 2, slot):
                copy.wait()
        for p in range(Z):

            @pl.when(z == p)
            def _(p=p):
                total = r2[b, p].astype(f32)
                if p > 0:
                    right_copy(b, p, r2.at[b, p]).wait_recv()
                    total += rr[b, p - 1].astype(f32)
                if p < Z - 1:
                    left_copy(b, p, r2.at[b, p]).wait_recv()
                    total += rl[b, p].astype(f32)
                ob[slot] = total
                for d in range(p + 1, Z):
                    right_copy(b, d, r2.at[b, d]).wait_send()
                for d in range(p):
                    left_copy(b, d, r2.at[b, d]).wait_send()

        for copy in out_copies(b, slot):
            copy.start()

    def mini_copy(k):
        return remote(mine.at[k], got.at[k], msem.at[0, k], msem.at[1, k], mates[k])

    order = [("product", 0, g) for g in range(groups)] + [("filter", 0, 0)]
    order += [("product", 1, g) for g in range(groups)] + [("filter", 1, 0)]
    order += [("product", 2, g) for g in range(groups)]

    for copy in loads(0):
        copy.start()
    tables_in = [load(back_h, back, 16), load(turned_h, turned, 17)]
    tables_in[0].start()
    tables_in[1].start()
    for copy in spectra(0):
        copy.start()
    mine[0] = jnp.sum(small_in[...], axis=1)
    mini_copy(0).start()

    for i in range(n_blocks + 6):
        if 0 <= i - 1 < n_blocks:
            after_core(i - 1)
        if 0 <= i - 2 < n_blocks:
            after_y(i - 2)
            hop(i - 2, 0)
        if 0 <= i - 3 < n_blocks:
            hop(i - 3, 1)
        if 0 <= i - 4 < n_blocks:
            hop(i - 4, 2)
        if 0 <= i - 5 < n_blocks:
            finish(i - 5)
        if i < n_blocks:
            kind, a, g = order[i]
            slot = i % x.shape[0]
            if kind == "product":
                if g == 0:
                    for copy in loads(a):
                        copy.wait()
                    turn(a)
                    if a + 1 < 3:
                        for copy in loads(a + 1):
                            copy.start()
                product(a, g, slot)
            else:
                if a == 0:
                    tables_in[0].wait()
                    tables_in[1].wait()
                for copy in spectra(a):
                    copy.wait()
                filters(a, slot)
                if a == 0:
                    for copy in spectra(1):
                        copy.start()
            core_copy(i, slot).start()
        if 2 <= i < 6:
            k = i - 2
            mini_copy(k).wait()
            total = mine[k] + got[k]
            if k < 3:
                mine[k + 1] = total
                mini_copy(k + 1).start()
            else:
                smallO[...] = total
    for b in (n_blocks - 2, n_blocks - 1):
        for copy in out_copies(b, b % 2):
            copy.wait()


def exchange_call(small, tabs, gdS, eS, nS, guS, ybS, goS, aS, gpS, s1S, g1S, s2S, g2S, ranks):
    T, D = aS.shape
    FF = eS.shape[1]
    pieces = T // CH
    per = D // ranks
    groups = per // 16
    blocks = 3 * groups + 2
    Z, Y, rows = 4, 2, T // ranks
    turned = (tabs[2][:, :CH].astype(f32) / CH).astype(bf16).T
    V, S = pltpu.VMEM, pltpu.SemaphoreType.DMA
    shard = (rows, D)
    scratch = [
        V((3, Z, Y, 2) + shard, bf16),
        V((blocks, Z, Y) + shard, bf16),
        V((blocks, Z) + shard, bf16),
        V((blocks, Z - 1) + shard, bf16),
        V((blocks, Z - 1) + shard, bf16),
        V((2, T, FF), bf16),
        V((2, T, D), bf16),
        V((2, ranks, groups, 16, T), bf16),
        V((2,) + s1S.shape, bf16),
        V((pieces + 1, 2 * CH, D), bf16),
        V((CH, 2 * CH), bf16),
        V((CH, 2 * CH), bf16),
        V((2,) + shard, f32),
        V((4, small.shape[0], D), f32),
        V((4, small.shape[0], D), f32),
        S((18,)), S((8,)), S((2, blocks)), S((2, blocks)), S((2, blocks, Z - 1)), S((2, blocks, Z - 1)), S((2, 4)),
    ]
    out_shape = [
        jax.ShapeDtypeStruct(s, f32)
        for s in ((per, FF), (per, FF), (per, D), (per, 3 * D), (2, rows, D), (small.shape[0], D))
    ]
    return pl.pallas_call(
        functools.partial(exchange_kernel, pieces),
        out_shape=out_shape,
        in_specs=[VM] + [ANY] * 14,
        out_specs=[ANY] * 5 + [VM],
        scratch_shapes=scratch,
        compiler_params=pltpu.CompilerParams(vmem_limit_bytes=VMEM_LIMIT, collective_id=0, has_side_effects=True),
        cost_estimate=pl.CostEstimate(flops=2 * T * 12 * D * D, bytes_accessed=40 << 20, transcendentals=0),
        name="exchange",
    )(small, tabs[1], turned, gdS, eS, nS, guS, ybS, goS, aS, gpS, s1S, g1S, s2S, g2S)


def dot_rows(x, y):
    return lax.dot_general(x, y, (((0,), (0,)), ((), ())), preferred_element_type=f32).astype(bf16)


def body(
    tokens, cotangent, norm_gains, norm_shifts, in_weight, in_bias, short_taps, long_filter, skip_gains,
    out_weight, out_bias, up_weight, up_bias, down_weight, down_bias,
):
    count = lax.axis_size("section")
    ranks = lax.axis_size("dp")
    tok, cot = tokens[0], cotangent[0]
    T, D = tok.shape
    FF = up_weight.shape[2]
    pieces = T // CH
    tabs = tables()
    as_rows = lambda x: x[0].astype(f32).reshape(-1, D)
    par = jnp.concatenate(
        [as_rows(x) for x in (norm_gains, norm_shifts, in_bias, short_taps, skip_gains, out_bias, down_bias, up_bias)], 0
    )
    win, wout, wup, wdown, filt = in_weight[0], out_weight[0], up_weight[0], down_weight[0], long_filter[0]

    (stream, token_grad, aS, ybS, nS, eS, s1S, s2S, gdS, guS, goS, gpS, g1S, g2S, small) = pass_call(
        par, tok, cot, filt, win, wout, wup, wdown, tabs, count
    )
    if ranks == 16 and D % (16 * ranks) == 0 and T == 64 * ranks and FF == 4 * D and pieces == 4:
        downT, up, out, inn, taps, small = exchange_call(
            small, tabs, gdS, eS, nS, guS, ybS, goS, aS, gpS, s1S, g1S, s2S, g2S, ranks
        )
        spot = lax.axis_index("dp")
        per = D // ranks
        head = lax.dynamic_slice_in_dim(small[:UPB], spot * per, per, 1)
        up_bias_grad = lax.dynamic_slice_in_dim(small[UPB:].reshape(-1), spot * (FF // ranks), FF // ranks, 0)
    else:
        slab = jnp.concatenate([dot_rows(gdS, eS), dot_rows(nS, guS), dot_rows(ybS, goS), dot_rows(aS, gpS)], axis=1)
        taps = jnp.concatenate([filter_call(s1S, g1S, tabs), filter_call(s2S, g2S, tabs)], axis=1)
        small = jnp.sum(small, axis=1)
        per = D // ranks
        mini = jnp.concatenate(
            [small[:UPB].reshape(UPB, ranks, per).transpose(1, 0, 2).reshape(ranks, -1), small[UPB:].reshape(ranks, -1)], axis=1
        )
        scatter = lambda x: lax.psum_scatter(x, "dp", scatter_dimension=0, tiled=True).astype(f32)
        slab, taps, mini = scatter(slab), scatter(taps), scatter(mini)[0]
        head = mini[: UPB * per].reshape(UPB, per)
        up_bias_grad = mini[UPB * per :]
        taps = taps.reshape(-1, 2, D).transpose(1, 0, 2)
        downT, up, out, inn = (slab[:, i:j] for i, j in ((0, FF), (FF, 2 * FF), (2 * FF, 2 * FF + D), (2 * FF + D, None)))
    return (
        stream[None],
        token_grad[None],
        head[GAIN : GAIN + 2][None],
        head[SHIFT : SHIFT + 2][None],
        inn[None],
        head[INB : INB + 3][None],
        head[TAP : TAP + 9].reshape(1, 3, 3, per),
        taps[None],
        head[SKIP : SKIP + 2][None],
        out[None],
        head[OUTB][None],
        up[None],
        up_bias_grad[None],
        downT.T[None],
        head[DOWNB][None],
    )


def solution(mesh):
    whole = P("dp", None, None)
    split = lambda n: P("section", *([None] * n))
    return jax.shard_map(
        body,
        mesh=mesh,
        in_specs=(
            whole, whole, split(2), split(2), split(2), split(2), split(3), split(3), split(2), split(2), split(1),
            split(2), split(1), split(2), split(1),
        ),
        out_specs=(
            P("dp", "section", None),
            P("dp", "section", None),
            P("section", None, "dp"),
            P("section", None, "dp"),
            P("section", "dp", None),
            P("section", None, "dp"),
            P("section", None, None, "dp"),
            P("section", None, "dp", None),
            P("section", None, "dp"),
            P("section", "dp", None),
            P("section", "dp"),
            P("section", "dp", None),
            P("section", "dp"),
            P("section", None, "dp"),
            P("section", "dp"),
        ),
        check_vma=False,
    )
```

```python
import functools
import math

import jax
import jax.numpy as jnp
import ml_dtypes
import numpy as np
from jax import lax
from jax.experimental import pallas as pl
from jax.experimental.pallas import tpu as pltpu
from jax.sharding import PartitionSpec as P

CH = 256
FT = 512
CARRY = 8
f32, bf16 = jnp.float32, jnp.bfloat16
VMEM_LIMIT = 60 * 1024 * 1024
ANY = pl.BlockSpec(memory_space=pl.ANY)
SMEM = pl.BlockSpec(memory_space=pltpu.SMEM)
VM = pl.BlockSpec(memory_space=pltpu.VMEM)

GAIN, SHIFT, INB, TAP, SKIP, OUTB, DOWNB, UPB = 0, 2, 4, 7, 16, 18, 19, 20


def tables():
    order = np.concatenate([np.arange(0, CH, 2), np.arange(1, CH, 2)])
    angle = np.pi * ((2 * order[:, None] + 1) * np.arange(CH)[None] % (4 * CH)) / (2 * CH)
    cos, sin = np.cos(angle), np.sin(angle)
    sign = np.where(order % 2 == 0, 1.0, -1.0)[:, None]
    spread = np.concatenate([cos, -sin], 0)
    turned = np.concatenate([sign * sin, sign * cos], 0)
    as_low = lambda t: jnp.asarray(t.astype(ml_dtypes.bfloat16))
    return as_low(spread), as_low(spread.T / CH), as_low(np.concatenate([turned, spread], 1))


def dot(x, y):
    return jnp.dot(x, y, preferred_element_type=f32)


def dot_nt(x, y):
    return lax.dot_general(x, y, (((1,), (1,)), ((), ())), preferred_element_type=f32)


def rows_at(index, size):
    return pl.ds(pl.multiple_of(index * size, size), size)


def for_rows(total, size, step, unroll=1):
    def run(i, carry):
        step(pl.multiple_of(i * size, size))
        return carry

    lax.fori_loop(0, total // size, run, 0, unroll=unroll)


def normalize(rows):
    average = jnp.mean(rows, axis=-1, keepdims=True)
    centered = rows - average
    scale = lax.rsqrt(jnp.mean(centered * centered, axis=-1, keepdims=True) + 1e-05)
    return centered * scale, scale


def norm_back(z, gain, unit, scale):
    w = z * gain
    return (
        w - jnp.mean(w, axis=-1, keepdims=True) - unit * jnp.mean(w * unit, axis=-1, keepdims=True)
    ) * scale


def gelu_pair(u):
    t = 1.0 / (1.0 + (0.3275911 * math.sqrt(0.5)) * jnp.abs(u))
    series = t * (
        0.5 * 0.254829592
        + t * (0.5 * -0.284496736 + t * (0.5 * 1.421413741 + t * (0.5 * -1.453152027 + t * (0.5 * 1.061405429))))
    )
    bell = jnp.exp(-0.5 * (u * u))
    tail = series * bell
    phi_sum = jnp.where(u >= 0, 1.0 - tail, tail)
    return u * phi_sum, phi_sum + u * (bell * (1.0 / math.sqrt(2.0 * math.pi)))


def mix_spectra(left, right, out, terms, conj):
    width = out.shape[1] // 2

    def tile(step, carry):
        r = pl.multiple_of(step * 16, 16)
        for half in range(2):
            cols = slice(half * width, (half + 1) * width)
            real = imag = None
            for i, j in terms:
                ar = left[i, pl.ds(r, 16), cols].astype(f32)
                ai = left[i, pl.ds(CH + r, 16), cols].astype(f32)
                br = right[j, pl.ds(r, 16), cols].astype(f32)
                bi = right[j, pl.ds(CH + r, 16), cols].astype(f32)
                if conj:
                    pr, pi = ar * br + ai * bi, ar * bi - ai * br
                else:
                    pr, pi = ar * br - ai * bi, ar * bi + ai * br
                real, imag = (pr, pi) if real is None else (real + pr, imag + pi)
            out[pl.ds(r, 16), cols] = real.astype(out.dtype)
            out[pl.ds(CH + r, 16), cols] = imag.astype(out.dtype)
        return carry

    lax.fori_loop(0, CH // 16, tile, 0)


def mix_at(seg, pieces, left, right, out, conj):
    for s in range(pieces):
        terms = [(j - s, j) for j in range(s, pieces)] if conj else [(s - j, j) for j in range(s + 1)]

        @pl.when(seg == s)
        def _(terms=terms):
            mix_spectra(left, right, out, terms, conj)


def fold_rows(x):
    return jnp.sum(x.reshape(x.shape[0] // 8, 8, x.shape[1]), axis=0)


def pieces_of(at, wide, D):
    spans, off = [], 0
    while off < wide:
        row, col = (at + off) // D, (at + off) % D
        size = min(D - col, wide - off)
        spans.append((row, col, off, size))
        off += size
    return spans


def pass_kernel(
    sections, pieces, par, tokens, cots, filt, win, wout, wup, wdown, spread_h, back_h, pair_h,
    stream, gtok, aS, ybS, nS, eS, s1S, s2S, gdS, guS, goS, gpS, g1S, g2S, smallO,
    inf, inb, gin, winb, woutb, wupb, wdownb, spread, back, pair, k1, k2, sp1, sp2, pall, y1all, mall, dall,
    ab, lead, leadlow, spec, wide, gate2, mid, nb, tile2, hid, outb, outfb, gnb, gqb, gpb, small,
    wsem, osem, fsem, bsem, ssem, gsem,
):
    rank = lax.axis_index("section")
    first, final = rank == 0, rank == sections - 1
    D, FF = woutb.shape[0], wupb.shape[1]
    tiles = FF // FT
    T = pieces * CH
    share = T // sections
    sub = min(CH, share)
    at = lambda r: {"section": r}

    def when(condition):
        return pl.when(condition)

    def remote(src, dst, send, recv, r):
        return pltpu.make_async_remote_copy(
            src_ref=src, dst_ref=dst, send_sem=send, recv_sem=recv, device_id=at(r), device_id_type=pl.DeviceIdType.MESH
        )

    def local(src, dst, sem):
        return pltpu.make_async_copy(src, dst, sem)

    loads = [
        local(win, winb, wsem.at[0]),
        local(wout, woutb, wsem.at[1]),
        local(wup, wupb, wsem.at[2]),
        local(wdown, wdownb, wsem.at[3]),
        local(spread_h, spread, wsem.at[4]),
        local(back_h, back, wsem.at[5]),
        local(pair_h, pair, wsem.at[6]),
    ]
    fill = [local(filt.at[f, pl.ds(0, CH)], sp.at[0, pl.ds(CH, CH)], wsem.at[7 + f]) for f, sp in enumerate((sp1, sp2))]
    for seg in range(1, pieces):
        window = pl.ds((seg - 1) * CH, 2 * CH)
        fill += [local(filt.at[f, window], sp.at[seg], wsem.at[7 + 2 * seg + f]) for f, sp in enumerate((sp1, sp2))]

    def own_chunk(src, dst, seg, sems):
        return local(src.at[rows_at(seg, CH)], dst.at[seg], sems.at[1, seg])

    def relay(src, dst, seg, sems, r):
        return remote(src, dst.at[seg], sems.at[0, seg], sems.at[1, seg], r)

    @when(first)
    def _():
        for seg in range(pieces):
            own_chunk(tokens, inf, seg, fsem).start()

    loads[0].start()
    for copy in fill:
        copy.start()
    for k in (6, 4, 5, 1, 2, 3):
        loads[k].start()

    @when(final)
    def _():
        for seg in range(pieces):
            own_chunk(cots, inb, seg, bsem).start()

    barrier = pltpu.get_barrier_semaphore()
    for r in range(sections):

        @when(rank != r)
        def _(r=r):
            pl.semaphore_signal(barrier, inc=1, device_id=at(r), device_id_type=pl.DeviceIdType.MESH)

    if sections > 1:
        pl.semaphore_wait(barrier, sections - 1)

    pall[pl.ds(0, 16), :] = jnp.zeros((16, 3 * D), bf16)
    for sp in (sp1, sp2):
        sp[0, pl.ds(0, CH), :] = jnp.zeros((CH, D), bf16)
    small[...] = jnp.zeros(small.shape, f32)
    gqb[pl.ds(CH, CARRY), :] = jnp.zeros((CARRY, 3 * D), f32)

    def filter_spectra(seg):
        k1[seg] = dot(pair[...], sp1[seg]).astype(bf16)
        k2[seg] = dot(pair[...], sp2[seg]).astype(bf16)

    @when(jnp.logical_not(first))
    def _():
        for copy in fill:
            copy.wait()
        loads[6].wait()

        def run(seg, carry):
            filter_spectra(seg)
            return carry

        lax.fori_loop(0, pieces, run, 0)

    def out_parts(seg, src, dst, sems, to_self):
        found = []
        for j in range(CH // sub):
            row = seg * CH + j * sub
            r, off = row // share, row % share
            found.append((r, off, src.at[pl.ds(j * sub, sub)], sems.at[0, seg * (CH // sub) + j], off // sub))
        return found

    def put(src, dst, k):
        return local(src, dst, osem.at[k])

    def forward_chunk(seg, carry):
        here = rows_at(seg, CH)
        base = pl.multiple_of(seg * CH, CH)
        hb = inf.at[seg]
        slot = 0
        later = seg > 0

        def before(copy):
            @when(later)
            def _():
                copy.wait()

        puts = [
            put(ab, aS.at[here], 0), put(sp1.at[seg], s1S.at[seg], 1), put(sp2.at[seg], s2S.at[seg], 2),
            put(leadlow, ybS.at[here], 3), put(nb, nS.at[here], 4), put(hid, eS.at[here], 5),
        ]

        @when(first)
        def _():
            own_chunk(tokens, inf, seg, fsem).wait()

        @when(jnp.logical_not(first))
        def _():
            relay(outb.at[slot], inf, seg, fsem, rank).wait_recv()

        before(puts[0])

        def ln1(r):
            unit, _ = normalize(hb[pl.ds(r, 32), :].astype(f32))
            ab[pl.ds(r, 32), :] = (unit * par[GAIN : GAIN + 1, :] + par[SHIFT : SHIFT + 1, :]).astype(bf16)

        for_rows(CH, 32, ln1, 8)
        puts[0].start()

        @when(seg == 0)
        def _():
            loads[0].wait()

        for b in range(3):
            cols = slice(b * D, (b + 1) * D)
            value = dot(ab[...], winb[:, cols]) + par[INB + b : INB + b + 1, :]
            pall[pl.ds(pl.multiple_of(base + 16, 16), CH), cols] = value.astype(bf16)

        before(puts[3])

        def short(r):
            got = [branch(base + r, b)[0] for b in range(3)]
            gate2[pl.ds(r, 32), :] = got[2]
            s = got[0] * got[1]
            lead[pl.ds(r, 32), :] = s
            leadlow[pl.ds(r, 32), :] = s.astype(bf16)

        for_rows(CH, 32, short)

        @when(first)
        def _():
            @when(seg == 0)
            def _():
                for copy in fill:
                    copy.wait()
                loads[6].wait()

            filter_spectra(seg)

        @when(seg == 0)
        def _():
            loads[4].wait()
            loads[5].wait()

        sp1[seg] = dot(spread[...], leadlow[...]).astype(bf16)
        puts[1].start()
        mix_at(seg, pieces, k1, sp1, spec, False)
        wide[...] = dot(back[...], spec[...])

        def second(r):
            rows = pl.ds(r, 64)
            y = wide[rows, :] + par[SKIP : SKIP + 1, :] * lead[rows, :]
            y1all[seg, rows, :] = y.astype(bf16)
            trail = y * gate2[rows, :]
            lead[rows, :] = trail
            leadlow[rows, :] = trail.astype(bf16)

        for_rows(CH, 64, second)
        sp2[seg] = dot(spread[...], leadlow[...]).astype(bf16)
        puts[2].start()
        mix_at(seg, pieces, k2, sp2, spec, False)
        leadlow[...] = (dot(back[...], spec[...]) + par[SKIP + 1 : SKIP + 2, :] * lead[...]).astype(bf16)
        puts[3].start()

        @when(seg == 0)
        def _():
            loads[1].wait()

        wide[...] = dot(leadlow[...], woutb[...])
        before(puts[4])

        def ln2(r):
            rows = pl.ds(r, 32)
            m = hb[rows, :].astype(f32) + (wide[rows, :] + par[OUTB : OUTB + 1, :])
            mall[seg, rows, :] = m.astype(bf16)
            unit, _ = normalize(m)
            nb[rows, :] = (unit * par[GAIN + 1 : GAIN + 2, :] + par[SHIFT + 1 : SHIFT + 2, :]).astype(bf16)
            mid[rows, :] = m + par[DOWNB : DOWNB + 1, :]

        for_rows(CH, 32, ln2, 8)
        puts[4].start()

        @when(seg == 0)
        def _():
            loads[2].wait()
            loads[3].wait()

        before(puts[5])

        def up(k):
            return dot(nb[...], wupb[:, k * FT : (k + 1) * FT])

        def act(k):
            spans = pieces_of(k * FT, FT, D)
            bias = [par[UPB + row : UPB + row + 1, col : col + size] for row, col, _, size in spans]
            bias = bias[0] if len(bias) == 1 else jnp.concatenate(bias, axis=1)
            e, d = gelu_pair(tile2[k % 2] + bias)
            hid[:, k * FT : (k + 1) * FT] = e.astype(bf16)
            dall[seg, :, k * FT : (k + 1) * FT] = d.astype(bf16)

        def down(k):
            mid[...] += dot(hid[:, k * FT : (k + 1) * FT], wdownb[k * FT : (k + 1) * FT, :])

        tile2[0] = up(0)
        for k in range(tiles):
            if k + 1 < tiles:
                tile2[(k + 1) % 2] = up(k + 1)
            act(k)
            if k >= 1:
                down(k - 1)
        down(tiles - 1)
        puts[5].start()

        @when(later)
        def _():
            finish_out(seg - 1, slot)

        outb[slot] = mid[...].astype(bf16)

        @when(jnp.logical_not(final))
        def _():
            relay(outb.at[slot], inf, seg, fsem, rank + 1).start()

        @when(final)
        def _():
            for r, off, src, sem, k in out_parts(seg, outb.at[slot], stream, ssem, None):

                @when(r != rank)
                def _():
                    remote(src, stream.at[pl.ds(pl.multiple_of(off, sub), sub)], sem, ssem.at[1, k], r).start()

                @when(r == rank)
                def _():
                    local(src, stream.at[pl.ds(pl.multiple_of(off, sub), sub)], sem).start()

        return carry

    def finish_out(seg, slot):
        @when(jnp.logical_not(final))
        def _():
            relay(outb.at[slot], inf, seg, fsem, rank + 1).wait_send()

        @when(final)
        def _():
            for r, off, src, sem, k in out_parts(seg, outb.at[slot], stream, ssem, None):

                @when(r != rank)
                def _():
                    remote(src, stream.at[pl.ds(pl.multiple_of(off, sub), sub)], sem, ssem.at[1, k], r).wait_send()

                @when(r == rank)
                def _():
                    local(src, stream.at[pl.ds(pl.multiple_of(off, sub), sub)], sem).wait()

    def branch(start, b):
        rows = pall[pl.ds(pl.multiple_of(start, 16), 48), b * D : (b + 1) * D].astype(f32)
        late = [rows[16 - i : 48 - i] for i in range(3)]
        t = [par[TAP + 3 * i + b : TAP + 3 * i + b + 1, :] for i in range(3)]
        return t[0] * late[0] + t[1] * late[1] + t[2] * late[2], late

    lax.fori_loop(0, pieces, forward_chunk, 0)
    last = pieces - 1
    here = rows_at(last, CH)
    for copy in (
        put(ab, aS.at[here], 0), put(sp1.at[last], s1S.at[last], 1), put(sp2.at[last], s2S.at[last], 2),
        put(leadlow, ybS.at[here], 3), put(nb, nS.at[here], 4), put(hid, eS.at[here], 5),
    ):
        copy.wait()
    for k in range(last):
        put(sp1.at[k], s1S.at[k], 1).wait()
        put(sp2.at[k], s2S.at[k], 2).wait()
    finish_out(last, 0)

    def add_small(k, x, cols=slice(None)):
        small[k, :, cols] += fold_rows(x)

    def backward_chunk(i, carry):
        seg = pieces - 1 - i
        here = rows_at(seg, CH)
        base = pl.multiple_of(seg * CH, CH)
        gdb, hb = inb.at[seg], inf.at[seg]
        slot = 0

        def before(copy):
            @when(i > 0)
            def _():
                copy.wait()

        puts = [
            put(gdb, gdS.at[here], 6), put(hid, guS.at[here], 7), put(nb, goS.at[here], 8), put(gpb, gpS.at[here], 9),
            put(sp2.at[seg], g2S.at[seg], 10), put(sp1.at[seg], g1S.at[seg], 11),
        ]

        @when(final)
        def _():
            own_chunk(cots, inb, seg, bsem).wait()

        @when(jnp.logical_not(final))
        def _():
            relay(outb.at[slot], inb, seg, bsem, rank).wait_recv()

        before(puts[0])
        puts[0].start()
        before(puts[1])

        def down(k):
            return dot_nt(gdb[...], wdownb[k * FT : (k + 1) * FT, :])

        def act(k):
            cols = slice(k * FT, (k + 1) * FT)
            gu = (dall[seg, :, cols].astype(f32) * tile2[k % 2]).astype(bf16)
            hid[:, cols] = gu
            total = fold_rows(gu.astype(f32))
            for row, col, off, size in pieces_of(k * FT, FT, D):
                small[UPB + row, :, col : col + size] += total[:, off : off + size]

        def up(k):
            part = dot_nt(hid[:, k * FT : (k + 1) * FT], wupb[:, k * FT : (k + 1) * FT])
            if k == 0:
                gnb[...] = part
            else:
                gnb[...] += part

        tile2[0] = down(0)
        for k in range(tiles):
            if k + 1 < tiles:
                tile2[(k + 1) % 2] = down(k + 1)
            act(k)
            if k >= 1:
                up(k - 1)
        up(tiles - 1)
        puts[1].start()
        before(puts[2])

        def ln2(r):
            rows = pl.ds(r, 32)
            unit, scale = normalize(mall[seg, rows, :].astype(f32))
            z = gnb[rows, :]
            gd = gdb[rows, :].astype(f32)
            gm = gd + norm_back(z, par[GAIN + 1 : GAIN + 2, :], unit, scale)
            mid[rows, :] = gm
            go = gm.astype(bf16)
            nb[rows, :] = go
            add_small(GAIN + 1, z * unit)
            add_small(SHIFT + 1, z)
            add_small(OUTB, go.astype(f32))
            add_small(DOWNB, gd)

        for_rows(CH, 32, ln2, 8)
        puts[2].start()
        gy = dot_nt(nb[...], woutb[...])
        lead[...] = gy
        leadlow[...] = gy.astype(bf16)
        sp2[seg] = dot(spread[...], leadlow[...]).astype(bf16)
        puts[4].start()
        mix_at(seg, pieces, k2, sp2, spec, True)
        wide[...] = dot(back[...], spec[...])

        def keep(r, b, grad, late):
            gqb[pl.ds(r, 32), b * D : (b + 1) * D] = grad
            for tap in range(3):
                add_small(TAP + 3 * tap + b, grad * late[tap])

        def second(r):
            rows = pl.ds(r, 32)
            gate, late = branch(base + r, 2)
            y1 = y1all[seg, rows, :].astype(f32)
            gy2 = lead[rows, :]
            gs2 = wide[rows, :] + par[SKIP + 1 : SKIP + 2, :] * gy2
            gy1 = gs2 * gate
            gate2[rows, :] = gy1
            leadlow[rows, :] = gy1.astype(bf16)
            add_small(SKIP + 1, gy2 * (y1 * gate))
            keep(r, 2, gs2 * y1, late)

        for_rows(CH, 32, second)
        sp1[seg] = dot(spread[...], leadlow[...]).astype(bf16)
        puts[5].start()
        mix_at(seg, pieces, k1, sp1, spec, True)
        wide[...] = dot(back[...], spec[...])

        def lower(r):
            rows = pl.ds(r, 32)
            carrier, late_carrier = branch(base + r, 0)
            gate, late_gate = branch(base + r, 1)
            gy1 = gate2[rows, :]
            gs1 = wide[rows, :] + par[SKIP : SKIP + 1, :] * gy1
            add_small(SKIP, gy1 * (carrier * gate))
            keep(r, 0, gs1 * gate, late_carrier)
            keep(r, 1, gs1 * carrier, late_gate)

        for_rows(CH, 32, lower)
        before(puts[3])

        def short(r):
            for b in range(3):
                cols = slice(b * D, (b + 1) * D)
                rows = gqb[pl.ds(r, 32 + CARRY), cols]
                t = [par[TAP + 3 * tap + b : TAP + 3 * tap + b + 1, :] for tap in range(3)]
                gp = (t[0] * rows[:32] + t[1] * rows[1:33] + t[2] * rows[2:34]).astype(bf16)
                gpb[pl.ds(r, 32), cols] = gp
                add_small(INB + b, gp.astype(f32))

        for_rows(CH, 32, short)
        puts[3].start()
        gqb[pl.ds(CH, CARRY), :] = gqb[pl.ds(0, CARRY), :]
        gnb[...] = dot_nt(gpb[...], winb[...])

        @when(i > 0)
        def _():
            finish_grad(i - 1, slot)

        def ln1(r):
            rows = pl.ds(r, 32)
            unit, scale = normalize(hb[rows, :].astype(f32))
            z = gnb[rows, :]
            gh = mid[rows, :] + norm_back(z, par[GAIN : GAIN + 1, :], unit, scale)
            outfb[slot, rows, :] = gh
            outb[slot, rows, :] = gh.astype(bf16)
            add_small(GAIN, z * unit)
            add_small(SHIFT, z)

        for_rows(CH, 32, ln1, 8)

        @when(jnp.logical_not(first))
        def _():
            relay(outb.at[slot], inb, seg, bsem, rank - 1).start()

        @when(first)
        def _():
            for r, off, src, sem, k in out_parts(seg, outb.at[slot], gtok, gsem, None):
                whole = outfb.at[slot, pl.ds(lax.rem(seg * CH + off, CH) if sub < CH else 0, sub)]

                @when(r != rank)
                def _():
                    remote(src, gin.at[k], sem, gsem.at[1, k], r).start()

                @when(r == rank)
                def _():
                    local(whole, gtok.at[pl.ds(pl.multiple_of(off, sub), sub)], sem).start()

        return carry

    def finish_grad(i, slot):
        seg = pieces - 1 - i

        @when(jnp.logical_not(first))
        def _():
            relay(outb.at[slot], inb, seg, bsem, rank - 1).wait_send()

        @when(first)
        def _():
            for r, off, src, sem, k in out_parts(seg, outb.at[slot], gtok, gsem, None):
                whole = outfb.at[slot, pl.ds(0, sub)]

                @when(r != rank)
                def _():
                    remote(src, gin.at[k], sem, gsem.at[1, k], r).wait_send()

                @when(r == rank)
                def _():
                    local(whole, gtok.at[pl.ds(pl.multiple_of(off, sub), sub)], sem).wait()

    lax.fori_loop(0, pieces, backward_chunk, 0)
    here = rows_at(0, CH)
    ends = [
        put(inb.at[0], gdS.at[here], 6), put(hid, guS.at[here], 7), put(nb, goS.at[here], 8), put(gpb, gpS.at[here], 9),
        put(sp2.at[0], g2S.at[0], 10), put(sp1.at[0], g1S.at[0], 11),
    ]
    for copy in ends:
        copy.wait()
    for k in range(last):
        ends[4].wait()
        ends[5].wait()
    total = put(small, smallO, 12)
    total.start()
    finish_grad(last, 0)
    parts = share // sub

    @when(jnp.logical_not(final))
    def _():
        for k in range(parts):
            remote(outb.at[0, pl.ds(0, sub)], stream.at[pl.ds(k * sub, sub)], ssem.at[0, 0], ssem.at[1, k], rank).wait_recv()

    @when(jnp.logical_not(first))
    def _():
        for k in range(parts):
            remote(outb.at[0, pl.ds(0, sub)], gin.at[k], gsem.at[0, 0], gsem.at[1, k], rank).wait_recv()
            outfb[0, pl.ds(0, sub), :] = gin[k].astype(f32)
            copy = local(outfb.at[0, pl.ds(0, sub)], gtok.at[pl.ds(k * sub, sub)], gsem.at[0, k])
            copy.start()
            copy.wait()

    total.wait()


def pass_call(par, tokens, cots, filt, win, wout, wup, wdown, tabs, sections):
    T, D = tokens.shape
    FF = wup.shape[1]
    pieces = T // CH
    share = T // sections
    sub = min(CH, share)
    spec3 = (pieces, 2 * CH, D)
    small = (UPB + FF // D, 8, D)
    shapes = [
        ((share, D), bf16), ((share, D), f32),
        ((T, D), bf16), ((T, D), bf16), ((T, D), bf16), ((T, FF), bf16), (spec3, bf16), (spec3, bf16),
        ((T, D), bf16), ((T, FF), bf16), ((T, D), bf16), ((T, 3 * D), bf16), (spec3, bf16), (spec3, bf16),
        (small, f32),
    ]
    V, S = pltpu.VMEM, pltpu.SemaphoreType.DMA
    chunk, chunks = (CH, D), (pieces, CH, D)
    scratch = [
        V(chunks, bf16), V(chunks, bf16), V((share // sub, sub, D), bf16),
        V(win.shape, bf16), V(wout.shape, bf16), V(wup.shape, bf16), V(wdown.shape, bf16),
        V((2 * CH, CH), bf16), V((CH, 2 * CH), bf16), V((2 * CH, 2 * CH), bf16),
        V(spec3, bf16), V(spec3, bf16), V(spec3, bf16), V(spec3, bf16),
        V((16 + T, 3 * D), bf16), V(chunks, bf16), V(chunks, bf16), V((pieces, CH, FF), bf16),
        V(chunk, bf16), V(chunk, f32), V(chunk, bf16), V((2 * CH, D), bf16), V(chunk, f32), V(chunk, f32), V(chunk, f32),
        V(chunk, bf16), V((2, CH, FT), f32), V((CH, FF), bf16), V((1,) + chunk, bf16), V((1,) + chunk, f32),
        V(chunk, f32), V((CH + CARRY, 3 * D), f32), V((CH, 3 * D), bf16), V(small, f32),
        S((7 + 2 * pieces,)), S((13,)), S((2, pieces)), S((2, pieces)), S((2, T // sub)), S((2, T // sub)),
    ]
    return pl.pallas_call(
        functools.partial(pass_kernel, sections, pieces),
        out_shape=[jax.ShapeDtypeStruct(*s) for s in shapes],
        in_specs=[VM] + [ANY] * 10,
        out_specs=[ANY] * len(shapes),
        scratch_shapes=scratch,
        compiler_params=pltpu.CompilerParams(vmem_limit_bytes=63 * 1024 * 1024, collective_id=1, has_side_effects=True),
        name="layer_pass",
    )(par, tokens, cots, filt, win, wout, wup, wdown, *tabs)


def filter_kernel(pieces, s, g, back, turned, out, q):
    width = s.shape[2] // 2

    for d in range(pieces):

        def tile(i, carry, d=d):
            r = pl.multiple_of(i * 16, 16)
            for half in range(2):
                cols = slice(half * width, (half + 1) * width)
                real = jnp.zeros((16, width), f32)
                imag = jnp.zeros((16, width), f32)
                for k in range(d, pieces):
                    ar = s[k - d, pl.ds(r, 16), cols].astype(f32)
                    ai = s[k - d, pl.ds(CH + r, 16), cols].astype(f32)
                    br = g[k, pl.ds(r, 16), cols].astype(f32)
                    bi = g[k, pl.ds(CH + r, 16), cols].astype(f32)
                    real = real + (ar * br + ai * bi)
                    imag = imag + (ar * bi - ai * br)
                q[d, pl.ds(r, 16), cols] = real.astype(bf16)
                q[d, pl.ds(CH + r, 16), cols] = imag.astype(bf16)
            return carry

        lax.fori_loop(0, CH // 16, tile, 0)
    for d in range(pieces):
        rows = dot(back[...], q[d])
        if d + 1 < pieces:
            rows += dot(turned[...], q[d + 1])
        out[pl.ds(d * CH, CH), :] = rows.astype(bf16)


def filter_call(s, g, tabs):
    pieces, _, D = s.shape
    turned = (tabs[2][:, :CH].astype(f32) / CH).astype(bf16).T
    return pl.pallas_call(
        functools.partial(filter_kernel, pieces),
        out_shape=jax.ShapeDtypeStruct((pieces * CH, D), bf16),
        in_specs=[VM] * 4,
        out_specs=VM,
        scratch_shapes=[pltpu.VMEM(s.shape, bf16)],
        compiler_params=pltpu.CompilerParams(vmem_limit_bytes=VMEM_LIMIT),
        name="filter_grad",
    )(s, g, tabs[1], turned)


def exchange_plan(groups, D):
    blocks = [("product", 0, g) for g in range(groups)] + [("filter", 0, 0)]
    blocks += [("product", 1, g) for g in range(groups)] + [("filter", 1, 0)]
    blocks += [("product", 2, g) for g in range(groups)]
    half = D // 2
    sent, flows = [], []
    for b in range(len(blocks)):
        for low in (0, half):
            parts = [(b, 0, half, False)] if low == 0 else [(b, half, half - 128, False), (b, D - 128, 128, True)]
            sent.append((b, low, list(range(len(flows), len(flows) + len(parts)))))
            flows += parts
    return blocks, sent, flows


def exchange_kernel(
    pieces, small_in, back_h, turned_h, gdS, eS, nS, guS, ybS, goS, aS, gpS, s1S, g1S, s2S, g2S,
    downT, upO, outO, inO, filtO, smallO,
    x, r1, r2, rr, rl, rrz, rlz, r2z, gb, lb, lt, sb, qb, back, turned, ob, mine, got,
    lsem, osem, csem, ysem, rsem, fsem, msem,
):
    D = lb.shape[2]
    half = D // 2
    me = lax.axis_index("dp")
    c, y, z = me % 2, (me // 2) % 2, me // 4
    Z = r2.shape[1]
    groups = lt.shape[2]
    blocks, sent, flows = exchange_plan(groups, D)
    at = lambda i: {"dp": i}
    core_id, y_id = me + 1 - 2 * c, me + 2 - 4 * y
    mates = (core_id, y_id, me + 4 - 8 * (z % 2), me + 8 - 16 * (z // 2))
    inner = (z == 1) | (z == 2)

    barrier = pltpu.get_barrier_semaphore()
    for mate in mates:
        pl.semaphore_signal(barrier, inc=1, device_id=at(mate), device_id_type=pl.DeviceIdType.MESH)

    @pl.when(inner)
    def _():
        other = me + 12 - 8 * z
        pl.semaphore_signal(barrier, inc=1, device_id=at(other), device_id_type=pl.DeviceIdType.MESH)

    @pl.when(inner)
    def _():
        pl.semaphore_wait(barrier, len(mates) + 1)

    @pl.when(jnp.logical_not(inner))
    def _():
        pl.semaphore_wait(barrier, len(mates))

    def remote(src, dst, send, recv, mate):
        return pltpu.make_async_remote_copy(
            src_ref=src, dst_ref=dst, send_sem=send, recv_sem=recv, device_id=at(mate),
            device_id_type=pl.DeviceIdType.MESH,
        )

    def load(src, dst, k):
        return pltpu.make_async_copy(src, dst, lsem.at[k])

    rights = ((eS,), (guS,), (goS, gpS))
    lefts = ((gdS,), (nS,), (ybS, aS))
    turned_at = ((0,), (1,), (0, 2))

    def right_loads(m):
        found, off = [], 0
        for k, src in enumerate(rights[m]):
            wide = src.shape[1]
            found.append(load(src, gb.at[m % 2, :, pl.ds(off, wide)], 4 * m + k))
            off += wide
        return found

    def left_loads(m):
        return [load(src, lb.at[k], 4 * m + 2 + k) for k, src in enumerate(lefts[m])]

    def spectra(f):
        src = ((s1S, g1S), (s2S, g2S))[f]
        return [load(src[k], sb.at[k], 12 + 2 * f + k) for k in range(2)]

    def turn(m):
        for k, spot in enumerate(turned_at[m]):

            def part(i, carry, k=k, spot=spot):
                rows = pl.multiple_of(i * 128, 128)
                piece = jnp.transpose(lb[k, pl.ds(rows, 128), :])
                lt[spot, :, :, :, pl.ds(rows, 128)] = piece.reshape(lt.shape[1:4] + (128,))
                return carry

            lax.fori_loop(0, lb.shape[1] // 128, part, 0)

    def product(m, g, low, slot):
        def part(i, carry):
            k = jnp.where(i == 0, 0, 2) if m == 2 else m
            left = lt[k, :, g].reshape(16 * lt.shape[1], lt.shape[4])
            cols = pl.ds(pl.multiple_of(i * D + low, 128), half)
            value = dot(left, gb[m % 2, :, cols]).astype(bf16)
            x[slot, :, :, :, pl.ds(pl.multiple_of(i * 16, 16), 16), :] = value.reshape(x.shape[1:4] + (16, half))
            return carry

        lax.fori_loop(0, 4, part, 0)

    def mix(d):
        mix_spectra(sb.at[0], sb.at[1], qb.at[d], [(j - d, j) for j in range(d, pieces)], True)

    def filters(low, slot):
        cols = slice(low, low + half)

        def part(d, carry):
            rows = dot(back[...], qb[d, :, cols]) + dot(turned[...], qb[d + 1, :, cols])
            x[slot, d] = rows.astype(bf16).reshape(x.shape[2:])
            return carry

        lax.fori_loop(0, pieces, part, 0)

    def core_copy(i):
        b, low, _ = sent[i]
        return remote(
            x.at[i % x.shape[0], :, :, 1 - c], r1.at[b, :, :, :, pl.ds(low, half)], csem.at[0, i], csem.at[1, i], core_id
        )

    def add(p, q):
        return (p.astype(f32) + q.astype(f32)).astype(bf16)

    def after_core(i):
        b, low, mine_flows = sent[i]
        core_copy(i).wait()
        cols = slice(low, low + half)

        def part(k, carry):
            for j in range(2):
                r1[b, k, j, :, cols] = add(r1[b, k, j, :, cols], x[i % x.shape[0], k, j, c])
            return carry

        lax.fori_loop(0, Z, part, 0)
        for u in mine_flows:
            if not flows[u][3]:
                y_copy(u).start()

    def y_copy(u):
        b, low, wide, z_first = flows[u]
        cols = pl.ds(low, wide)
        if z_first:
            return remote(r1.at[b, z, 1 - y, :, cols], r2z.at[b], ysem.at[0, u], ysem.at[1, u], y_id)
        return remote(r1.at[b, :, 1 - y, :, cols], r2.at[b, :, :, cols], ysem.at[0, u], ysem.at[1, u], y_id)

    def after_y(u):
        b, low, wide, _ = flows[u]
        cols = slice(low, low + wide)
        y_copy(u).wait()

        def part(k, carry):
            r2[b, k, :, cols] = add(r2[b, k, :, cols], r1[b, k, y, :, cols])
            return carry

        lax.fori_loop(0, Z, part, 0)

    def own(u, d):
        b, low, wide, z_first = flows[u]
        cols = pl.ds(low, wide)
        return r1.at[b, d, :, :, cols] if z_first else r2.at[b, d, :, cols]

    def right_at(u, d):
        b, low, wide, z_first = flows[u]
        return rrz.at[b, d - 1] if z_first else rr.at[b, d - 1, :, pl.ds(low, wide)]

    def left_at(u, d):
        b, low, wide, z_first = flows[u]
        return rlz.at[b, d] if z_first else rl.at[b, d, :, pl.ds(low, wide)]

    def right_copy(u, d, src):
        return remote(src, right_at(u, d), rsem.at[0, u, d - 1], rsem.at[1, u, d - 1], me + 4)

    def left_copy(u, d, src):
        return remote(src, left_at(u, d), fsem.at[0, u, d], fsem.at[1, u, d], me - 4)

    def hop(u, h):
        @pl.when(z == h)
        def _():
            for d in range(Z - 1, h, -1):
                src = own(u, d)
                if h > 0:
                    right_copy(u, d, src).wait_recv()
                    src = right_at(u, d)
                    src[...] = add(src[...], own(u, d)[...])
                right_copy(u, d, src).start()

        @pl.when(z == Z - 1 - h)
        def _():
            for d in range(Z - 1 - h):
                src = own(u, d)
                if h > 0:
                    left_copy(u, d, src).wait_recv()
                    src = left_at(u, d)
                    src[...] = add(src[...], own(u, d)[...])
                left_copy(u, d, src).start()

    def gather(u, store):
        for p in range(Z):

            @pl.when(z == p)
            def _(p=p):
                total = own(u, p)[...].astype(f32)
                if p > 0:
                    right_copy(u, p, own(u, p)).wait_recv()
                    total += right_at(u, p)[...].astype(f32)
                if p < Z - 1:
                    left_copy(u, p, own(u, p)).wait_recv()
                    total += left_at(u, p)[...].astype(f32)
                for d in range(p + 1, Z):
                    right_copy(u, d, own(u, d)).wait_send()
                for d in range(p):
                    left_copy(u, d, own(u, d)).wait_send()
                store(p, total)

    def turn_to_y(u):
        def store(p, total):
            own(u, p)[...] = total.astype(bf16)

        gather(u, store)
        y_copy(u).start()

    def out_copies(i):
        b, low, _ = sent[i]
        kind, a, g = blocks[b]
        slot = i % 2
        src = ob.at[slot]
        if kind == "filter":
            return [pltpu.make_async_copy(src, filtO.at[a, :, pl.ds(low, half)], osem.at[4 * slot])]
        found = []
        rows = pl.ds(g * 16, 16)
        for k in range(4):
            if a < 2:
                dst = (downT, upO)[a].at[rows, pl.ds(k * D + low, half)]
            elif k == 0:
                dst = outO.at[rows, pl.ds(low, half)]
            else:
                dst = inO.at[rows, pl.ds((k - 1) * D + low, half)]
            found.append(pltpu.make_async_copy(src.at[pl.ds(16 * k, 16)], dst, osem.at[4 * slot + k]))
        return found

    def finish(i):
        b, low, mine_flows = sent[i]
        slot = i % 2
        if i >= 2:
            for copy in out_copies(i - 2):
                copy.wait()
        for u in mine_flows:
            _, first, wide, z_first = flows[u]
            cols = slice(first - low, first - low + wide)
            if z_first:
                y_copy(u).wait()
                ob[slot, :, cols] = r1[b, z, y, :, first : first + wide].astype(f32) + r2z[b].astype(f32)
            else:

                def store(p, total, cols=cols):
                    ob[slot, :, cols] = total

                gather(u, store)
        for copy in out_copies(i):
            copy.start()

    def mini_copy(k):
        return remote(mine.at[k], got.at[k], msem.at[0, k], msem.at[1, k], mates[k])

    tables_in = [load(back_h, back, 16), load(turned_h, turned, 17)]
    for copy in left_loads(0) + right_loads(0) + tables_in + spectra(0):
        copy.start()
    mine[0] = jnp.sum(small_in[...], axis=1)
    mini_copy(0).start()
    qb[pieces] = jnp.zeros(qb.shape[1:], bf16)

    def compute(i):
        b, low, _ = sent[i]
        kind, a, g = blocks[b]
        slot = i % x.shape[0]
        if kind == "product":
            if g == 0 and low == 0:
                if a == 0:
                    for copy in left_loads(0):
                        copy.wait()
                    turn(0)
                for copy in right_loads(a):
                    copy.wait()
                if a + 1 < 3:
                    for copy in left_loads(a + 1) + right_loads(a + 1):
                        copy.start()
            product(a, g, low, slot)
            core_copy(i).start()
            if a < 2:
                step = 2 * g + (low > 0)
                if step == 1:
                    for copy in spectra(a):
                        copy.wait()
                if 1 <= step <= pieces:
                    mix(step - 1)
        else:
            if a == 0 and low == 0:
                for copy in tables_in:
                    copy.wait()
            filters(low, slot)
            core_copy(i).start()
            if low == 0:
                if a == 0:
                    for copy in spectra(1):
                        copy.start()
                for copy in left_loads(a + 1):
                    copy.wait()
                turn(a + 1)

    n = len(sent)
    by_y = lambda i: [u for u in sent[i][2] if not flows[u][3]]
    by_z = lambda i: [u for u in sent[i][2] if flows[u][3]]
    for i in range(n + 5):
        if i < n:
            compute(i)
        if 0 <= i - 1 < n:
            after_core(i - 1)
            for u in by_z(i - 1):
                hop(u, 0)
        if 0 <= i - 2 < n:
            for u in by_y(i - 2):
                after_y(u)
                hop(u, 0)
            for u in by_z(i - 2):
                hop(u, 1)
        if 0 <= i - 3 < n:
            for u in by_y(i - 3):
                hop(u, 1)
            for u in by_z(i - 3):
                hop(u, 2)
        if 0 <= i - 4 < n:
            for u in by_y(i - 4):
                hop(u, 2)
            for u in by_z(i - 4):
                turn_to_y(u)
        if 0 <= i - 5 < n:
            finish(i - 5)
        if 2 <= i < 6:
            k = i - 2
            mini_copy(k).wait()
            total = mine[k] + got[k]
            if k < 3:
                mine[k + 1] = total
                mini_copy(k + 1).start()
            else:
                smallO[...] = total
    for i in (n - 2, n - 1):
        for copy in out_copies(i):
            copy.wait()


def exchange_call(small, tabs, gdS, eS, nS, guS, ybS, goS, aS, gpS, s1S, g1S, s2S, g2S, ranks):
    T, D = aS.shape
    FF = eS.shape[1]
    pieces = T // CH
    per = D // ranks
    groups = per // 16
    blocks, sent, flows = exchange_plan(groups, D)
    n_blocks, n_sent, n_flows = len(blocks), len(sent), len(flows)
    Z, Y, rows = 4, 2, T // ranks
    turned = (tabs[2][:, :CH].astype(f32) / CH).astype(bf16).T
    V, S = pltpu.VMEM, pltpu.SemaphoreType.DMA
    shard = (rows, D)
    scratch = [
        V((3, Z, Y, 2, rows, D // 2), bf16),
        V((n_blocks, Z, Y) + shard, bf16),
        V((n_blocks, Z) + shard, bf16),
        V((n_blocks, Z - 1) + shard, bf16),
        V((n_blocks, Z - 1) + shard, bf16),
        V((n_blocks, Z - 1, Y, rows, 128), bf16),
        V((n_blocks, Z - 1, Y, rows, 128), bf16),
        V((n_blocks, rows, 128), bf16),
        V((2, T, FF), bf16),
        V((2, T, D), bf16),
        V((3, ranks, groups, 16, T), bf16),
        V((2,) + s1S.shape, bf16),
        V((pieces + 1, 2 * CH, D), bf16),
        V((CH, 2 * CH), bf16),
        V((CH, 2 * CH), bf16),
        V((2, rows, D // 2), f32),
        V((4, small.shape[0], D), f32),
        V((4, small.shape[0], D), f32),
        S((18,)), S((8,)), S((2, n_sent)), S((2, n_flows)), S((2, n_flows, Z - 1)), S((2, n_flows, Z - 1)), S((2, 4)),
    ]
    out_shape = [
        jax.ShapeDtypeStruct(s, f32)
        for s in ((per, FF), (per, FF), (per, D), (per, 3 * D), (2, rows, D), (small.shape[0], D))
    ]
    return pl.pallas_call(
        functools.partial(exchange_kernel, pieces),
        out_shape=out_shape,
        in_specs=[VM] + [ANY] * 14,
        out_specs=[ANY] * 5 + [VM],
        scratch_shapes=scratch,
        compiler_params=pltpu.CompilerParams(vmem_limit_bytes=VMEM_LIMIT, collective_id=0, has_side_effects=True),
        cost_estimate=pl.CostEstimate(flops=2 * T * 12 * D * D, bytes_accessed=40 << 20, transcendentals=0),
        name="exchange",
    )(small, tabs[1], turned, gdS, eS, nS, guS, ybS, goS, aS, gpS, s1S, g1S, s2S, g2S)


def dot_rows(x, y):
    return lax.dot_general(x, y, (((0,), (0,)), ((), ())), preferred_element_type=f32).astype(bf16)


def body(
    tokens, cotangent, norm_gains, norm_shifts, in_weight, in_bias, short_taps, long_filter, skip_gains,
    out_weight, out_bias, up_weight, up_bias, down_weight, down_bias,
):
    count = lax.axis_size("section")
    ranks = lax.axis_size("dp")
    tok, cot = tokens[0], cotangent[0]
    T, D = tok.shape
    FF = up_weight.shape[2]
    pieces = T // CH
    tabs = tables()
    as_rows = lambda x: x[0].astype(f32).reshape(-1, D)
    par = jnp.concatenate(
        [as_rows(x) for x in (norm_gains, norm_shifts, in_bias, short_taps, skip_gains, out_bias, down_bias, up_bias)], 0
    )
    win, wout, wup, wdown, filt = in_weight[0], out_weight[0], up_weight[0], down_weight[0], long_filter[0]

    (stream, token_grad, aS, ybS, nS, eS, s1S, s2S, gdS, guS, goS, gpS, g1S, g2S, small) = pass_call(
        par, tok, cot, filt, win, wout, wup, wdown, tabs, count
    )
    if ranks == 16 and D % (16 * ranks) == 0 and T == 64 * ranks and FF == 4 * D and pieces == 4:
        downT, up, out, inn, taps, small = exchange_call(
            small, tabs, gdS, eS, nS, guS, ybS, goS, aS, gpS, s1S, g1S, s2S, g2S, ranks
        )
        spot = lax.axis_index("dp")
        per = D // ranks
        head = lax.dynamic_slice_in_dim(small[:UPB], spot * per, per, 1)
        up_bias_grad = lax.dynamic_slice_in_dim(small[UPB:].reshape(-1), spot * (FF // ranks), FF // ranks, 0)
    else:
        slab = jnp.concatenate([dot_rows(gdS, eS), dot_rows(nS, guS), dot_rows(ybS, goS), dot_rows(aS, gpS)], axis=1)
        taps = jnp.concatenate([filter_call(s1S, g1S, tabs), filter_call(s2S, g2S, tabs)], axis=1)
        small = jnp.sum(small, axis=1)
        per = D // ranks
        mini = jnp.concatenate(
            [small[:UPB].reshape(UPB, ranks, per).transpose(1, 0, 2).reshape(ranks, -1), small[UPB:].reshape(ranks, -1)], axis=1
        )
        scatter = lambda x: lax.psum_scatter(x, "dp", scatter_dimension=0, tiled=True).astype(f32)
        slab, taps, mini = scatter(slab), scatter(taps), scatter(mini)[0]
        head = mini[: UPB * per].reshape(UPB, per)
        up_bias_grad = mini[UPB * per :]
        taps = taps.reshape(-1, 2, D).transpose(1, 0, 2)
        downT, up, out, inn = (slab[:, i:j] for i, j in ((0, FF), (FF, 2 * FF), (2 * FF, 2 * FF + D), (2 * FF + D, None)))
    return (
        stream[None],
        token_grad[None],
        head[GAIN : GAIN + 2][None],
        head[SHIFT : SHIFT + 2][None],
        inn[None],
        head[INB : INB + 3][None],
        head[TAP : TAP + 9].reshape(1, 3, 3, per),
        taps[None],
        head[SKIP : SKIP + 2][None],
        out[None],
        head[OUTB][None],
        up[None],
        up_bias_grad[None],
        downT.T[None],
        head[DOWNB][None],
    )


def solution(mesh):
    whole = P("dp", None, None)
    split = lambda n: P("section", *([None] * n))
    return jax.shard_map(
        body,
        mesh=mesh,
        in_specs=(
            whole, whole, split(2), split(2), split(2), split(2), split(3), split(3), split(2), split(2), split(1),
            split(2), split(1), split(2), split(1),
        ),
        out_specs=(
            P("dp", "section", None),
            P("dp", "section", None),
            P("section", None, "dp"),
            P("section", None, "dp"),
            P("section", "dp", None),
            P("section", None, "dp"),
            P("section", None, None, "dp"),
            P("section", None, "dp", None),
            P("section", None, "dp"),
            P("section", "dp", None),
            P("section", "dp"),
            P("section", "dp", None),
            P("section", "dp"),
            P("section", None, "dp"),
            P("section", "dp"),
        ),
        check_vma=False,
    )
```

```python
import functools
import math

import jax
import jax.numpy as jnp
import ml_dtypes
import numpy as np
from jax import lax
from jax.experimental import pallas as pl
from jax.experimental.pallas import tpu as pltpu
from jax.sharding import PartitionSpec as P

CH = 256
FT = 512
CARRY = 8
f32, bf16 = jnp.float32, jnp.bfloat16
VMEM_LIMIT = 60 * 1024 * 1024
ANY = pl.BlockSpec(memory_space=pl.ANY)
SMEM = pl.BlockSpec(memory_space=pltpu.SMEM)
VM = pl.BlockSpec(memory_space=pltpu.VMEM)

GAIN, SHIFT, INB, TAP, SKIP, OUTB, DOWNB, UPB = 0, 2, 4, 7, 16, 18, 19, 20


def table():
    order = np.concatenate([np.arange(0, CH, 2), np.arange(1, CH, 2)])
    angle = np.pi * ((2 * order[:, None] + 1) * np.arange(CH)[None] % (4 * CH)) / (2 * CH)
    cos, sin = np.cos(angle), np.sin(angle)
    sign = np.where(order % 2 == 0, 1.0, -1.0)[:, None]
    spread = np.concatenate([cos, -sin], 0)
    turned = np.concatenate([sign * sin, sign * cos], 0)
    return jnp.asarray(np.concatenate([turned, spread], 1).astype(ml_dtypes.bfloat16))


def back_table(pair, at):
    return jnp.transpose(pair[:, at : at + CH].astype(f32) * (1.0 / CH)).astype(bf16)


def dot(x, y):
    return jnp.dot(x, y, preferred_element_type=f32)


def dot_nt(x, y):
    return lax.dot_general(x, y, (((1,), (1,)), ((), ())), preferred_element_type=f32)


def rows_at(index, size):
    return pl.ds(pl.multiple_of(index * size, size), size)


def for_rows(total, size, step, unroll=1):
    def run(i, carry):
        step(pl.multiple_of(i * size, size))
        return carry

    lax.fori_loop(0, total // size, run, 0, unroll=unroll)


def normalize(rows):
    average = jnp.mean(rows, axis=-1, keepdims=True)
    centered = rows - average
    scale = lax.rsqrt(jnp.mean(centered * centered, axis=-1, keepdims=True) + 1e-05)
    return centered * scale, scale


def norm_back(z, gain, unit, scale):
    w = z * gain
    return (
        w - jnp.mean(w, axis=-1, keepdims=True) - unit * jnp.mean(w * unit, axis=-1, keepdims=True)
    ) * scale


def gelu_pair(u):
    phi_sum = 0.5 + 0.5 * lax.erf(u * math.sqrt(0.5))
    bell = jnp.exp(-0.5 * (u * u))
    return u * phi_sum, phi_sum + u * (bell * (1.0 / math.sqrt(2.0 * math.pi)))


def mix_spectra(left, right, out, terms, conj):
    width = out.shape[1] // 2

    def tile(step, carry):
        r = pl.multiple_of(step * 16, 16)
        for half in range(2):
            cols = slice(half * width, (half + 1) * width)
            real = imag = None
            for i, j in terms:
                ar = left[i, pl.ds(r, 16), cols]
                ai = left[i, pl.ds(CH + r, 16), cols]
                br = right[j, pl.ds(r, 16), cols]
                bi = right[j, pl.ds(CH + r, 16), cols]
                if conj:
                    pr, pi = ar * br + ai * bi, ar * bi - ai * br
                else:
                    pr, pi = ar * br - ai * bi, ar * bi + ai * br
                real, imag = (pr, pi) if real is None else (real + pr, imag + pi)
            out[pl.ds(r, 16), cols] = real
            out[pl.ds(CH + r, 16), cols] = imag
        return carry

    lax.fori_loop(0, CH // 16, tile, 0)


def mix_at(seg, pieces, left, right, out, conj):
    for s in range(pieces):
        terms = [(j - s, j) for j in range(s, pieces)] if conj else [(s - j, j) for j in range(s + 1)]

        @pl.when(seg == s)
        def _(terms=terms):
            mix_spectra(left, right, out, terms, conj)


def fold_rows(x):
    return jnp.sum(x.reshape(x.shape[0] // 8, 8, x.shape[1]), axis=0)


def pieces_of(at, wide, D):
    spans, off = [], 0
    while off < wide:
        row, col = (at + off) // D, (at + off) % D
        size = min(D - col, wide - off)
        spans.append((row, col, off, size))
        off += size
    return spans


def pass_kernel(
    sections, pieces, gains, shifts, inb_p, taps_p, skips, outb_p, downb_p, upb_p, tokens, cots, filt, win, wout, wup, wdown, pair_h,
    stream, gtok, aS, ybS, nS, eS, s1S, s2S, gdS, guS, goS, gpS, g1S, g2S, smallO,
    inf, inb, gin, winb, woutb, wupb, wdownb, back, pair, k1, k2, sp1, sp2, pall, y1all, mall, dall,
    ab, lead, leadlow, spec, wide, gate2, mid, nb, tile2, hid, outb, outfb, gnb, gqb, gpb, small,
    par, wsem, osem, fsem, bsem, ssem, gsem,
):
    rank = lax.axis_index("section")
    first, final = rank == 0, rank == sections - 1
    D, FF = woutb.shape[0], wupb.shape[1]
    tiles = FF // FT
    T = pieces * CH
    share = T // sections
    sub = min(CH, share)
    at = lambda r: {"section": r}

    def when(condition):
        return pl.when(condition)

    def remote(src, dst, send, recv, r):
        return pltpu.make_async_remote_copy(
            src_ref=src, dst_ref=dst, send_sem=send, recv_sem=recv, device_id=at(r), device_id_type=pl.DeviceIdType.MESH
        )

    def local(src, dst, sem):
        return pltpu.make_async_copy(src, dst, sem)

    loads = [
        local(win, winb, wsem.at[0]),
        local(wout, woutb, wsem.at[1]),
        local(wup, wupb, wsem.at[2]),
        local(wdown, wdownb, wsem.at[3]),
        local(pair_h, pair, wsem.at[4]),
    ]
    fill = [local(filt.at[f, pl.ds(0, CH)], sp.at[0, pl.ds(CH, CH)], wsem.at[7 + f]) for f, sp in enumerate((sp1, sp2))]
    for seg in range(1, pieces):
        window = pl.ds((seg - 1) * CH, 2 * CH)
        fill += [local(filt.at[f, window], sp.at[seg], wsem.at[7 + 2 * seg + f]) for f, sp in enumerate((sp1, sp2))]

    def own_chunk(src, dst, seg, sems):
        return local(src.at[rows_at(seg, CH)], dst.at[seg], sems.at[1, seg])

    def relay(src, dst, seg, sems, r):
        return remote(src, dst.at[seg], sems.at[0, seg], sems.at[1, seg], r)

    @when(first)
    def _():
        for seg in range(pieces):
            own_chunk(tokens, inf, seg, fsem).start()

    loads[0].start()
    for copy in fill:
        copy.start()
    for k in (4, 1, 2, 3):
        loads[k].start()

    @when(final)
    def _():
        for seg in range(pieces):
            own_chunk(cots, inb, seg, bsem).start()

    for row, given in ((GAIN, gains), (SHIFT, shifts), (INB, inb_p), (SKIP, skips), (OUTB, outb_p), (DOWNB, downb_p)):
        par[row : row + given.shape[0], :] = given[...].astype(f32)
    for tap in range(3):
        par[TAP + 3 * tap : TAP + 3 * tap + 3, :] = taps_p[tap].astype(f32)
    for k in range(FF // D):
        par[UPB + k : UPB + k + 1, :] = upb_p[:, k * D : (k + 1) * D].astype(f32)

    barrier = pltpu.get_barrier_semaphore()
    for r in range(sections):

        @when(rank != r)
        def _(r=r):
            pl.semaphore_signal(barrier, inc=1, device_id=at(r), device_id_type=pl.DeviceIdType.MESH)

    if sections > 1:
        pl.semaphore_wait(barrier, sections - 1)

    pall[pl.ds(0, 16), :] = jnp.zeros((16, 3 * D), bf16)
    for sp in (sp1, sp2):
        sp[0, pl.ds(0, CH), :] = jnp.zeros((CH, D), bf16)
    small[...] = jnp.zeros(small.shape, f32)
    gqb[pl.ds(CH, CARRY), :] = jnp.zeros((CARRY, 3 * D), f32)

    def filter_spectra(seg):
        k1[seg] = dot(pair[...], sp1[seg]).astype(bf16)
        k2[seg] = dot(pair[...], sp2[seg]).astype(bf16)

    @when(jnp.logical_not(first))
    def _():
        for copy in fill:
            copy.wait()
        loads[4].wait()

        def run(seg, carry):
            filter_spectra(seg)
            return carry

        lax.fori_loop(0, pieces, run, 0)

    def out_parts(seg, src, dst, sems, to_self):
        found = []
        for j in range(CH // sub):
            row = seg * CH + j * sub
            r, off = row // share, row % share
            found.append((r, off, src.at[pl.ds(j * sub, sub)], sems.at[0, seg * (CH // sub) + j], off // sub))
        return found

    def put(src, dst, k):
        return local(src, dst, osem.at[k])

    def forward_chunk(seg, carry):
        here = rows_at(seg, CH)
        base = pl.multiple_of(seg * CH, CH)
        hb = inf.at[seg]
        slot = 0
        later = seg > 0

        def before(copy):
            @when(later)
            def _():
                copy.wait()

        puts = [
            put(ab, aS.at[here], 0), put(sp1.at[seg], s1S.at[seg], 1), put(sp2.at[seg], s2S.at[seg], 2),
            put(leadlow, ybS.at[here], 3), put(nb, nS.at[here], 4), put(hid, eS.at[here], 5),
        ]

        @when(first)
        def _():
            own_chunk(tokens, inf, seg, fsem).wait()

        @when(jnp.logical_not(first))
        def _():
            relay(outb.at[slot], inf, seg, fsem, rank).wait_recv()

        before(puts[0])

        def ln1(r):
            unit, _ = normalize(hb[pl.ds(r, 32), :].astype(f32))
            ab[pl.ds(r, 32), :] = (unit * par[GAIN : GAIN + 1, :] + par[SHIFT : SHIFT + 1, :]).astype(bf16)

        for_rows(CH, 32, ln1, 8)
        puts[0].start()

        @when(seg == 0)
        def _():
            loads[0].wait()

        for b in range(3):
            cols = slice(b * D, (b + 1) * D)
            value = dot(ab[...], winb[:, cols]) + par[INB + b : INB + b + 1, :]
            pall[pl.ds(pl.multiple_of(base + 16, 16), CH), cols] = value.astype(bf16)

        before(puts[3])

        def short(r):
            got = [branch(base + r, b)[0] for b in range(3)]
            gate2[pl.ds(r, 32), :] = got[2]
            s = got[0] * got[1]
            lead[pl.ds(r, 32), :] = s
            leadlow[pl.ds(r, 32), :] = s.astype(bf16)

        for_rows(CH, 32, short, 8)

        @when(first)
        def _():
            @when(seg == 0)
            def _():
                for copy in fill:
                    copy.wait()
                loads[4].wait()

            filter_spectra(seg)

        @when(seg == 0)
        def _():
            back[...] = back_table(pair, CH)

        sp1[seg] = dot(pair[:, CH:], leadlow[...]).astype(bf16)
        puts[1].start()
        mix_at(seg, pieces, k1, sp1, spec, False)
        wide[...] = dot(back[...], spec[...])

        def second(r):
            rows = pl.ds(r, 64)
            y = wide[rows, :] + par[SKIP : SKIP + 1, :] * lead[rows, :]
            y1all[seg, rows, :] = y.astype(bf16)
            trail = y * gate2[rows, :]
            lead[rows, :] = trail
            leadlow[rows, :] = trail.astype(bf16)

        for_rows(CH, 64, second, 4)
        sp2[seg] = dot(pair[:, CH:], leadlow[...]).astype(bf16)
        puts[2].start()
        mix_at(seg, pieces, k2, sp2, spec, False)
        leadlow[...] = (dot(back[...], spec[...]) + par[SKIP + 1 : SKIP + 2, :] * lead[...]).astype(bf16)
        puts[3].start()

        @when(seg == 0)
        def _():
            loads[1].wait()

        wide[...] = dot(leadlow[...], woutb[...])
        before(puts[4])

        def ln2(r):
            rows = pl.ds(r, 32)
            m = hb[rows, :].astype(f32) + (wide[rows, :] + par[OUTB : OUTB + 1, :])
            mall[seg, rows, :] = m.astype(bf16)
            unit, _ = normalize(m)
            nb[rows, :] = (unit * par[GAIN + 1 : GAIN + 2, :] + par[SHIFT + 1 : SHIFT + 2, :]).astype(bf16)
            mid[rows, :] = m + par[DOWNB : DOWNB + 1, :]

        for_rows(CH, 32, ln2, 8)
        puts[4].start()

        @when(seg == 0)
        def _():
            loads[2].wait()
            loads[3].wait()

        before(puts[5])

        def up(k):
            return dot(nb[...], wupb[:, k * FT : (k + 1) * FT])

        def act(k):
            spans = pieces_of(k * FT, FT, D)
            bias = [par[UPB + row : UPB + row + 1, col : col + size] for row, col, _, size in spans]
            bias = bias[0] if len(bias) == 1 else jnp.concatenate(bias, axis=1)
            e, d = gelu_pair(tile2[k % 2] + bias)
            hid[:, k * FT : (k + 1) * FT] = e.astype(bf16)
            dall[seg, :, k * FT : (k + 1) * FT] = d.astype(bf16)

        def down(k):
            mid[...] += dot(hid[:, k * FT : (k + 1) * FT], wdownb[k * FT : (k + 1) * FT, :])

        tile2[0] = up(0)
        for k in range(tiles):
            if k + 1 < tiles:
                tile2[(k + 1) % 2] = up(k + 1)
            act(k)
            if k >= 1:
                down(k - 1)
        down(tiles - 1)
        puts[5].start()

        @when(later)
        def _():
            finish_out(seg - 1, slot)

        outb[slot] = mid[...].astype(bf16)

        @when(jnp.logical_not(final))
        def _():
            relay(outb.at[slot], inf, seg, fsem, rank + 1).start()

        @when(final)
        def _():
            for r, off, src, sem, k in out_parts(seg, outb.at[slot], stream, ssem, None):

                @when(r != rank)
                def _():
                    remote(src, stream.at[pl.ds(pl.multiple_of(off, sub), sub)], sem, ssem.at[1, k], r).start()

                @when(r == rank)
                def _():
                    local(src, stream.at[pl.ds(pl.multiple_of(off, sub), sub)], sem).start()

        return carry

    def finish_out(seg, slot):
        @when(jnp.logical_not(final))
        def _():
            relay(outb.at[slot], inf, seg, fsem, rank + 1).wait_send()

        @when(final)
        def _():
            for r, off, src, sem, k in out_parts(seg, outb.at[slot], stream, ssem, None):

                @when(r != rank)
                def _():
                    remote(src, stream.at[pl.ds(pl.multiple_of(off, sub), sub)], sem, ssem.at[1, k], r).wait_send()

                @when(r == rank)
                def _():
                    local(src, stream.at[pl.ds(pl.multiple_of(off, sub), sub)], sem).wait()

    def branch(start, b):
        rows = pall[pl.ds(pl.multiple_of(start, 16), 48), b * D : (b + 1) * D].astype(f32)
        late = [rows[16 - i : 48 - i] for i in range(3)]
        t = [par[TAP + 3 * i + b : TAP + 3 * i + b + 1, :] for i in range(3)]
        return t[0] * late[0] + t[1] * late[1] + t[2] * late[2], late

    lax.fori_loop(0, pieces, forward_chunk, 0)
    last = pieces - 1
    here = rows_at(last, CH)
    for copy in (
        put(ab, aS.at[here], 0), put(sp1.at[last], s1S.at[last], 1), put(sp2.at[last], s2S.at[last], 2),
        put(leadlow, ybS.at[here], 3), put(nb, nS.at[here], 4), put(hid, eS.at[here], 5),
    ):
        copy.wait()
    for k in range(last):
        put(sp1.at[k], s1S.at[k], 1).wait()
        put(sp2.at[k], s2S.at[k], 2).wait()
    finish_out(last, 0)

    def add_small(k, x, cols=slice(None)):
        small[k, :, cols] += fold_rows(x)

    def backward_chunk(i, carry):
        seg = pieces - 1 - i
        here = rows_at(seg, CH)
        base = pl.multiple_of(seg * CH, CH)
        gdb, hb = inb.at[seg], inf.at[seg]
        slot = 0

        def before(copy):
            @when(i > 0)
            def _():
                copy.wait()

        puts = [
            put(gdb, gdS.at[here], 6), put(hid, guS.at[here], 7), put(nb, goS.at[here], 8), put(gpb, gpS.at[here], 9),
            put(sp2.at[seg], g2S.at[seg], 10), put(sp1.at[seg], g1S.at[seg], 11),
        ]

        @when(final)
        def _():
            own_chunk(cots, inb, seg, bsem).wait()

        @when(jnp.logical_not(final))
        def _():
            relay(outb.at[slot], inb, seg, bsem, rank).wait_recv()

        before(puts[0])
        puts[0].start()
        before(puts[1])

        def down(k):
            return dot_nt(gdb[...], wdownb[k * FT : (k + 1) * FT, :])

        def act(k):
            cols = slice(k * FT, (k + 1) * FT)
            gu = (dall[seg, :, cols].astype(f32) * tile2[k % 2]).astype(bf16)
            hid[:, cols] = gu
            total = fold_rows(gu.astype(f32))
            for row, col, off, size in pieces_of(k * FT, FT, D):
                small[UPB + row, :, col : col + size] += total[:, off : off + size]

        def up(k):
            part = dot_nt(hid[:, k * FT : (k + 1) * FT], wupb[:, k * FT : (k + 1) * FT])
            if k == 0:
                gnb[...] = part
            else:
                gnb[...] += part

        tile2[0] = down(0)
        for k in range(tiles):
            if k + 1 < tiles:
                tile2[(k + 1) % 2] = down(k + 1)
            act(k)
            if k >= 1:
                up(k - 1)
        up(tiles - 1)
        puts[1].start()
        before(puts[2])

        def ln2(r):
            rows = pl.ds(r, 32)
            unit, scale = normalize(mall[seg, rows, :].astype(f32))
            z = gnb[rows, :]
            gd = gdb[rows, :].astype(f32)
            gm = gd + norm_back(z, par[GAIN + 1 : GAIN + 2, :], unit, scale)
            mid[rows, :] = gm
            go = gm.astype(bf16)
            nb[rows, :] = go
            add_small(GAIN + 1, z * unit)
            add_small(SHIFT + 1, z)
            add_small(OUTB, go.astype(f32))
            add_small(DOWNB, gd)

        for_rows(CH, 32, ln2, 8)
        puts[2].start()
        gy = dot_nt(nb[...], woutb[...])
        lead[...] = gy
        leadlow[...] = gy.astype(bf16)
        sp2[seg] = dot(pair[:, CH:], leadlow[...]).astype(bf16)
        puts[4].start()
        mix_at(seg, pieces, k2, sp2, spec, True)
        wide[...] = dot(back[...], spec[...])

        def keep(r, b, grad, late):
            gqb[pl.ds(r, 32), b * D : (b + 1) * D] = grad
            for tap in range(3):
                add_small(TAP + 3 * tap + b, grad * late[tap])

        def second(r):
            rows = pl.ds(r, 32)
            gate, late = branch(base + r, 2)
            y1 = y1all[seg, rows, :].astype(f32)
            gy2 = lead[rows, :]
            gs2 = wide[rows, :] + par[SKIP + 1 : SKIP + 2, :] * gy2
            gy1 = gs2 * gate
            gate2[rows, :] = gy1
            leadlow[rows, :] = gy1.astype(bf16)
            add_small(SKIP + 1, gy2 * (y1 * gate))
            keep(r, 2, gs2 * y1, late)

        for_rows(CH, 32, second, 8)
        sp1[seg] = dot(pair[:, CH:], leadlow[...]).astype(bf16)
        puts[5].start()
        mix_at(seg, pieces, k1, sp1, spec, True)
        wide[...] = dot(back[...], spec[...])

        def lower(r):
            rows = pl.ds(r, 32)
            carrier, late_carrier = branch(base + r, 0)
            gate, late_gate = branch(base + r, 1)
            gy1 = gate2[rows, :]
            gs1 = wide[rows, :] + par[SKIP : SKIP + 1, :] * gy1
            add_small(SKIP, gy1 * (carrier * gate))
            keep(r, 0, gs1 * gate, late_carrier)
            keep(r, 1, gs1 * carrier, late_gate)

        for_rows(CH, 32, lower, 8)
        before(puts[3])

        def short(r):
            for b in range(3):
                cols = slice(b * D, (b + 1) * D)
                rows = gqb[pl.ds(r, 32 + CARRY), cols]
                t = [par[TAP + 3 * tap + b : TAP + 3 * tap + b + 1, :] for tap in range(3)]
                gp = (t[0] * rows[:32] + t[1] * rows[1:33] + t[2] * rows[2:34]).astype(bf16)
                gpb[pl.ds(r, 32), cols] = gp
                add_small(INB + b, gp.astype(f32))

        for_rows(CH, 32, short, 8)
        puts[3].start()
        gqb[pl.ds(CH, CARRY), :] = gqb[pl.ds(0, CARRY), :]
        gnb[...] = dot_nt(gpb[...], winb[...])

        @when(i > 0)
        def _():
            finish_grad(i - 1, slot)

        def ln1(r):
            rows = pl.ds(r, 32)
            unit, scale = normalize(hb[rows, :].astype(f32))
            z = gnb[rows, :]
            gh = mid[rows, :] + norm_back(z, par[GAIN : GAIN + 1, :], unit, scale)
            outfb[slot, rows, :] = gh
            outb[slot, rows, :] = gh.astype(bf16)
            add_small(GAIN, z * unit)
            add_small(SHIFT, z)

        for_rows(CH, 32, ln1, 8)

        @when(jnp.logical_not(first))
        def _():
            relay(outb.at[slot], inb, seg, bsem, rank - 1).start()

        @when(first)
        def _():
            for r, off, src, sem, k in out_parts(seg, outb.at[slot], gtok, gsem, None):
                whole = outfb.at[slot, pl.ds(lax.rem(seg * CH + off, CH) if sub < CH else 0, sub)]

                @when(r != rank)
                def _():
                    remote(src, gin.at[k], sem, gsem.at[1, k], r).start()

                @when(r == rank)
                def _():
                    local(whole, gtok.at[pl.ds(pl.multiple_of(off, sub), sub)], sem).start()

        return carry

    def finish_grad(i, slot):
        seg = pieces - 1 - i

        @when(jnp.logical_not(first))
        def _():
            relay(outb.at[slot], inb, seg, bsem, rank - 1).wait_send()

        @when(first)
        def _():
            for r, off, src, sem, k in out_parts(seg, outb.at[slot], gtok, gsem, None):
                whole = outfb.at[slot, pl.ds(0, sub)]

                @when(r != rank)
                def _():
                    remote(src, gin.at[k], sem, gsem.at[1, k], r).wait_send()

                @when(r == rank)
                def _():
                    local(whole, gtok.at[pl.ds(pl.multiple_of(off, sub), sub)], sem).wait()

    lax.fori_loop(0, pieces, backward_chunk, 0)
    here = rows_at(0, CH)
    ends = [
        put(inb.at[0], gdS.at[here], 6), put(hid, guS.at[here], 7), put(nb, goS.at[here], 8), put(gpb, gpS.at[here], 9),
        put(sp2.at[0], g2S.at[0], 10), put(sp1.at[0], g1S.at[0], 11),
    ]
    for copy in ends:
        copy.wait()
    for k in range(last):
        ends[4].wait()
        ends[5].wait()
    total = put(small, smallO, 12)
    total.start()
    finish_grad(last, 0)
    parts = share // sub

    @when(jnp.logical_not(final))
    def _():
        for k in range(parts):
            remote(outb.at[0, pl.ds(0, sub)], stream.at[pl.ds(k * sub, sub)], ssem.at[0, 0], ssem.at[1, k], rank).wait_recv()

    @when(jnp.logical_not(first))
    def _():
        for k in range(parts):
            remote(outb.at[0, pl.ds(0, sub)], gin.at[k], gsem.at[0, 0], gsem.at[1, k], rank).wait_recv()
            outfb[0, pl.ds(0, sub), :] = gin[k].astype(f32)
            copy = local(outfb.at[0, pl.ds(0, sub)], gtok.at[pl.ds(k * sub, sub)], gsem.at[0, k])
            copy.start()
            copy.wait()

    total.wait()


def pass_call(params, tokens, cots, filt, win, wout, wup, wdown, pair, sections):
    T, D = tokens.shape
    FF = wup.shape[1]
    pieces = T // CH
    share = T // sections
    sub = min(CH, share)
    spec3 = (pieces, 2 * CH, D)
    small = (UPB + FF // D, 8, D)
    shapes = [
        ((share, D), bf16), ((share, D), f32),
        ((T, D), bf16), ((T, D), bf16), ((T, D), bf16), ((T, FF), bf16), (spec3, bf16), (spec3, bf16),
        ((T, D), bf16), ((T, FF), bf16), ((T, D), bf16), ((T, 3 * D), bf16), (spec3, bf16), (spec3, bf16),
        (small, f32),
    ]
    V, S = pltpu.VMEM, pltpu.SemaphoreType.DMA
    chunk, chunks = (CH, D), (pieces, CH, D)
    scratch = [
        V(chunks, bf16), V(chunks, bf16), V((share // sub, sub, D), bf16),
        V(win.shape, bf16), V(wout.shape, bf16), V(wup.shape, bf16), V(wdown.shape, bf16),
        V((CH, 2 * CH), bf16), V((2 * CH, 2 * CH), bf16),
        V(spec3, bf16), V(spec3, bf16), V(spec3, bf16), V(spec3, bf16),
        V((16 + T, 3 * D), bf16), V(chunks, bf16), V(chunks, bf16), V((pieces, CH, FF), bf16),
        V(chunk, bf16), V(chunk, f32), V(chunk, bf16), V((2 * CH, D), bf16), V(chunk, f32), V(chunk, f32), V(chunk, f32),
        V(chunk, bf16), V((2, CH, FT), f32), V((CH, FF), bf16), V((1,) + chunk, bf16), V((1,) + chunk, f32),
        V(chunk, f32), V((CH + CARRY, 3 * D), f32), V((CH, 3 * D), bf16), V(small, f32), V((UPB + FF // D, D), f32),
        S((7 + 2 * pieces,)), S((13,)), S((2, pieces)), S((2, pieces)), S((2, T // sub)), S((2, T // sub)),
    ]
    return pl.pallas_call(
        functools.partial(pass_kernel, sections, pieces),
        out_shape=[jax.ShapeDtypeStruct(*s) for s in shapes],
        in_specs=[VM] * 8 + [ANY] * 8,
        out_specs=[ANY] * len(shapes),
        scratch_shapes=scratch,
        compiler_params=pltpu.CompilerParams(vmem_limit_bytes=63 * 1024 * 1024, collective_id=1, has_side_effects=True),
        name="layer_pass",
    )(*params, tokens, cots, filt, win, wout, wup, wdown, pair)


def filter_kernel(pieces, s, g, back, turned, out, q):
    for d in range(pieces):
        mix_spectra(s, g, q.at[d], [(j - d, j) for j in range(d, pieces)], True)
    for d in range(pieces):
        rows = dot(back[...], q[d])
        if d + 1 < pieces:
            rows += dot(turned[...], q[d + 1])
        out[pl.ds(d * CH, CH), :] = rows.astype(bf16)


def filter_call(s, g, pair):
    pieces, _, D = s.shape
    turned, back = ((pair[:, k : k + CH].astype(f32) / CH).astype(bf16).T for k in (0, CH))
    return pl.pallas_call(
        functools.partial(filter_kernel, pieces),
        out_shape=jax.ShapeDtypeStruct((pieces * CH, D), bf16),
        in_specs=[VM] * 4,
        out_specs=VM,
        scratch_shapes=[pltpu.VMEM(s.shape, bf16)],
        compiler_params=pltpu.CompilerParams(vmem_limit_bytes=VMEM_LIMIT),
        name="filter_grad",
    )(s, g, back, turned)


def exchange_plan(groups, D):
    blocks = [("product", 0, g) for g in range(groups)] + [("filter", 0, 0)]
    blocks += [("product", 1, g) for g in range(groups)] + [("filter", 1, 0)]
    blocks += [("product", 2, g) for g in range(groups)]
    half = D // 2
    sent, flows = [], []
    for b in range(len(blocks)):
        for low in (0, half):
            parts = [(b, 0, half, False)] if low == 0 else [(b, half, half - 128, False), (b, D - 128, 128, True)]
            sent.append((b, low, list(range(len(flows), len(flows) + len(parts)))))
            flows += parts
    return blocks, sent, flows


def exchange_kernel(
    pieces, small_in, pair_h, gdS, eS, nS, guS, ybS, goS, aS, gpS, s1S, g1S, s2S, g2S,
    downT, upO, outO, inO, filtO, smallO,
    x, r1, r2, rr, rl, rrz, rlz, r2z, gb, lb, lt, sb, qb, pair, back, turned, ob, mine, got,
    lsem, osem, csem, ysem, rsem, fsem, msem,
):
    D = lb.shape[2]
    half = D // 2
    me = lax.axis_index("dp")
    c, y, z = me % 2, (me // 2) % 2, me // 4
    Z = r2.shape[1]
    groups = lt.shape[2]
    blocks, sent, flows = exchange_plan(groups, D)
    at = lambda i: {"dp": i}
    core_id, y_id = me + 1 - 2 * c, me + 2 - 4 * y
    mates = (core_id, y_id, me + 4 - 8 * (z % 2), me + 8 - 16 * (z // 2))
    inner = (z == 1) | (z == 2)

    barrier = pltpu.get_barrier_semaphore()
    for mate in mates:
        pl.semaphore_signal(barrier, inc=1, device_id=at(mate), device_id_type=pl.DeviceIdType.MESH)

    @pl.when(inner)
    def _():
        other = me + 12 - 8 * z
        pl.semaphore_signal(barrier, inc=1, device_id=at(other), device_id_type=pl.DeviceIdType.MESH)

    @pl.when(inner)
    def _():
        pl.semaphore_wait(barrier, len(mates) + 1)

    @pl.when(jnp.logical_not(inner))
    def _():
        pl.semaphore_wait(barrier, len(mates))

    def remote(src, dst, send, recv, mate):
        return pltpu.make_async_remote_copy(
            src_ref=src, dst_ref=dst, send_sem=send, recv_sem=recv, device_id=at(mate),
            device_id_type=pl.DeviceIdType.MESH,
        )

    def load(src, dst, k):
        return pltpu.make_async_copy(src, dst, lsem.at[k])

    rights = ((eS,), (guS,), (goS, gpS))
    lefts = ((gdS,), (nS,), (ybS, aS))
    turned_at = ((0,), (1,), (0, 2))

    def right_loads(m):
        found, off = [], 0
        for k, src in enumerate(rights[m]):
            wide = src.shape[1]
            found.append(load(src, gb.at[m % 2, :, pl.ds(off, wide)], 4 * m + k))
            off += wide
        return found

    def left_loads(m):
        return [load(src, lb.at[k], 4 * m + 2 + k) for k, src in enumerate(lefts[m])]

    def spectra(f):
        src = ((s1S, g1S), (s2S, g2S))[f]
        return [load(src[k], sb.at[k], 12 + 2 * f + k) for k in range(2)]

    def turn(m):
        for k, spot in enumerate(turned_at[m]):

            def part(i, carry, k=k, spot=spot):
                rows = pl.multiple_of(i * 128, 128)
                piece = jnp.transpose(lb[k, pl.ds(rows, 128), :])
                lt[spot, :, :, :, pl.ds(rows, 128)] = piece.reshape(lt.shape[1:4] + (128,))
                return carry

            lax.fori_loop(0, lb.shape[1] // 128, part, 0)

    def product(m, g, low, slot):
        def part(i, carry):
            k = jnp.where(i == 0, 0, 2) if m == 2 else m
            left = lt[k, :, g].reshape(16 * lt.shape[1], lt.shape[4])
            cols = pl.ds(pl.multiple_of(i * D + low, 128), half)
            value = dot(left, gb[m % 2, :, cols]).astype(bf16)
            x[slot, :, :, :, pl.ds(pl.multiple_of(i * 16, 16), 16), :] = value.reshape(x.shape[1:4] + (16, half))
            return carry

        lax.fori_loop(0, 4, part, 0)

    def mix(d):
        mix_spectra(sb.at[0], sb.at[1], qb.at[d], [(j - d, j) for j in range(d, pieces)], True)

    def filters(low, slot):
        cols = slice(low, low + half)

        def part(d, carry):
            rows = dot(back[...], qb[d, :, cols]) + dot(turned[...], qb[d + 1, :, cols])
            x[slot, d] = rows.astype(bf16).reshape(x.shape[2:])
            return carry

        lax.fori_loop(0, pieces, part, 0)

    def core_copy(i):
        b, low, _ = sent[i]
        return remote(
            x.at[i % x.shape[0], :, :, 1 - c], r1.at[b, :, :, :, pl.ds(low, half)], csem.at[0, i], csem.at[1, i], core_id
        )

    def add(p, q):
        return (p.astype(f32) + q.astype(f32)).astype(bf16)

    def after_core(i):
        b, low, mine_flows = sent[i]
        core_copy(i).wait()
        cols = slice(low, low + half)

        def part(k, carry):
            for j in range(2):
                r1[b, k, j, :, cols] = add(r1[b, k, j, :, cols], x[i % x.shape[0], k, j, c])
            return carry

        lax.fori_loop(0, Z, part, 0)
        for u in mine_flows:
            if not flows[u][3]:
                y_copy(u).start()

    def y_copy(u):
        b, low, wide, z_first = flows[u]
        cols = pl.ds(low, wide)
        if z_first:
            return remote(r1.at[b, z, 1 - y, :, cols], r2z.at[b], ysem.at[0, u], ysem.at[1, u], y_id)
        return remote(r1.at[b, :, 1 - y, :, cols], r2.at[b, :, :, cols], ysem.at[0, u], ysem.at[1, u], y_id)

    def after_y(u):
        b, low, wide, _ = flows[u]
        cols = slice(low, low + wide)
        y_copy(u).wait()

        def part(k, carry):
            r2[b, k, :, cols] = add(r2[b, k, :, cols], r1[b, k, y, :, cols])
            return carry

        lax.fori_loop(0, Z, part, 0)

    def own(u, d):
        b, low, wide, z_first = flows[u]
        cols = pl.ds(low, wide)
        return r1.at[b, d, :, :, cols] if z_first else r2.at[b, d, :, cols]

    def right_at(u, d):
        b, low, wide, z_first = flows[u]
        return rrz.at[b, d - 1] if z_first else rr.at[b, d - 1, :, pl.ds(low, wide)]

    def left_at(u, d):
        b, low, wide, z_first = flows[u]
        return rlz.at[b, d] if z_first else rl.at[b, d, :, pl.ds(low, wide)]

    def right_copy(u, d, src):
        return remote(src, right_at(u, d), rsem.at[0, u, d - 1], rsem.at[1, u, d - 1], me + 4)

    def left_copy(u, d, src):
        return remote(src, left_at(u, d), fsem.at[0, u, d], fsem.at[1, u, d], me - 4)

    def hop(u, h):
        @pl.when(z == h)
        def _():
            for d in range(Z - 1, h, -1):
                src = own(u, d)
                if h > 0:
                    right_copy(u, d, src).wait_recv()
                    src = right_at(u, d)
                    src[...] = add(src[...], own(u, d)[...])
                right_copy(u, d, src).start()

        @pl.when(z == Z - 1 - h)
        def _():
            for d in range(Z - 1 - h):
                src = own(u, d)
                if h > 0:
                    left_copy(u, d, src).wait_recv()
                    src = left_at(u, d)
                    src[...] = add(src[...], own(u, d)[...])
                left_copy(u, d, src).start()

    def gather(u, store):
        for p in range(Z):

            @pl.when(z == p)
            def _(p=p):
                total = own(u, p)[...].astype(f32)
                if p > 0:
                    right_copy(u, p, own(u, p)).wait_recv()
                    total += right_at(u, p)[...].astype(f32)
                if p < Z - 1:
                    left_copy(u, p, own(u, p)).wait_recv()
                    total += left_at(u, p)[...].astype(f32)
                for d in range(p + 1, Z):
                    right_copy(u, d, own(u, d)).wait_send()
                for d in range(p):
                    left_copy(u, d, own(u, d)).wait_send()
                store(p, total)

    def turn_to_y(u):
        def store(p, total):
            own(u, p)[...] = total.astype(bf16)

        gather(u, store)
        y_copy(u).start()

    def out_copies(i):
        b, low, _ = sent[i]
        kind, a, g = blocks[b]
        slot = i % 2
        src = ob.at[slot]
        if kind == "filter":
            return [pltpu.make_async_copy(src, filtO.at[a, :, pl.ds(low, half)], osem.at[4 * slot])]
        found = []
        rows = pl.ds(g * 16, 16)
        for k in range(4):
            if a < 2:
                dst = (downT, upO)[a].at[rows, pl.ds(k * D + low, half)]
            elif k == 0:
                dst = outO.at[rows, pl.ds(low, half)]
            else:
                dst = inO.at[rows, pl.ds((k - 1) * D + low, half)]
            found.append(pltpu.make_async_copy(src.at[pl.ds(16 * k, 16)], dst, osem.at[4 * slot + k]))
        return found

    def finish(i):
        b, low, mine_flows = sent[i]
        slot = i % 2
        if i >= 2:
            for copy in out_copies(i - 2):
                copy.wait()
        for u in mine_flows:
            _, first, wide, z_first = flows[u]
            cols = slice(first - low, first - low + wide)
            if z_first:
                y_copy(u).wait()
                ob[slot, :, cols] = r1[b, z, y, :, first : first + wide].astype(f32) + r2z[b].astype(f32)
            else:

                def store(p, total, cols=cols):
                    ob[slot, :, cols] = total

                gather(u, store)
        for copy in out_copies(i):
            copy.start()

    def mini_copy(k):
        return remote(mine.at[k], got.at[k], msem.at[0, k], msem.at[1, k], mates[k])

    tables_in = [load(pair_h, pair, 16)]
    for copy in left_loads(0) + right_loads(0) + tables_in + spectra(0):
        copy.start()
    mine[0] = jnp.sum(small_in[...], axis=1)
    mini_copy(0).start()
    qb[pieces] = jnp.zeros(qb.shape[1:], bf16)

    def compute(i):
        b, low, _ = sent[i]
        kind, a, g = blocks[b]
        slot = i % x.shape[0]
        if kind == "product":
            if g == 0 and low == 0:
                if a == 0:
                    for copy in left_loads(0):
                        copy.wait()
                    turn(0)
                for copy in right_loads(a):
                    copy.wait()
                if a + 1 < 3:
                    for copy in left_loads(a + 1) + right_loads(a + 1):
                        copy.start()
            product(a, g, low, slot)
            core_copy(i).start()
            if a < 2:
                step = 2 * g + (low > 0)
                if step == 1:
                    for copy in spectra(a):
                        copy.wait()
                if 1 <= step <= pieces:
                    mix(step - 1)
        else:
            if a == 0 and low == 0:
                for copy in tables_in:
                    copy.wait()
                back[...] = back_table(pair, CH)
                turned[...] = back_table(pair, 0)
            filters(low, slot)
            core_copy(i).start()
            if low == 0:
                if a == 0:
                    for copy in spectra(1):
                        copy.start()
                for copy in left_loads(a + 1):
                    copy.wait()
                turn(a + 1)

    n = len(sent)
    by_y = lambda i: [u for u in sent[i][2] if not flows[u][3]]
    by_z = lambda i: [u for u in sent[i][2] if flows[u][3]]
    CORE, Y_DONE, HOP1, HOP2, DONE = 1, 3, 5, 7, 9
    for i in range(n + DONE):
        if i < n:
            compute(i)
        if 0 <= i - CORE < n:
            after_core(i - CORE)
            for u in by_z(i - CORE):
                hop(u, 0)
        if 0 <= i - Y_DONE < n:
            for u in by_z(i - Y_DONE):
                hop(u, 1)
            for u in by_y(i - Y_DONE):
                after_y(u)
                hop(u, 0)
        if 0 <= i - HOP1 < n:
            for u in by_z(i - HOP1):
                hop(u, 2)
            for u in by_y(i - HOP1):
                hop(u, 1)
        if 0 <= i - HOP2 < n:
            for u in by_z(i - HOP2):
                turn_to_y(u)
            for u in by_y(i - HOP2):
                hop(u, 2)
        if 0 <= i - DONE < n:
            finish(i - DONE)
        if 2 <= i < 6:
            k = i - 2
            mini_copy(k).wait()
            total = mine[k] + got[k]
            if k < 3:
                mine[k + 1] = total
                mini_copy(k + 1).start()
            else:
                smallO[...] = total
    for i in (n - 2, n - 1):
        for copy in out_copies(i):
            copy.wait()


def exchange_call(small, pair, gdS, eS, nS, guS, ybS, goS, aS, gpS, s1S, g1S, s2S, g2S, ranks):
    T, D = aS.shape
    FF = eS.shape[1]
    pieces = T // CH
    per = D // ranks
    groups = per // 16
    blocks, sent, flows = exchange_plan(groups, D)
    n_blocks, n_sent, n_flows = len(blocks), len(sent), len(flows)
    Z, Y, rows = 4, 2, T // ranks
    V, S = pltpu.VMEM, pltpu.SemaphoreType.DMA
    shard = (rows, D)
    scratch = [
        V((3, Z, Y, 2, rows, D // 2), bf16),
        V((n_blocks, Z, Y) + shard, bf16),
        V((n_blocks, Z) + shard, bf16),
        V((n_blocks, Z - 1) + shard, bf16),
        V((n_blocks, Z - 1) + shard, bf16),
        V((n_blocks, Z - 1, Y, rows, 128), bf16),
        V((n_blocks, Z - 1, Y, rows, 128), bf16),
        V((n_blocks, rows, 128), bf16),
        V((2, T, FF), bf16),
        V((2, T, D), bf16),
        V((3, ranks, groups, 16, T), bf16),
        V((2,) + s1S.shape, bf16),
        V((pieces + 1, 2 * CH, D), bf16),
        V((2 * CH, 2 * CH), bf16),
        V((CH, 2 * CH), bf16),
        V((CH, 2 * CH), bf16),
        V((2, rows, D // 2), f32),
        V((4, small.shape[0], D), f32),
        V((4, small.shape[0], D), f32),
        S((18,)), S((8,)), S((2, n_sent)), S((2, n_flows)), S((2, n_flows, Z - 1)), S((2, n_flows, Z - 1)), S((2, 4)),
    ]
    out_shape = [
        jax.ShapeDtypeStruct(s, f32)
        for s in ((per, FF), (per, FF), (per, D), (per, 3 * D), (2, rows, D), (small.shape[0], D))
    ]
    return pl.pallas_call(
        functools.partial(exchange_kernel, pieces),
        out_shape=out_shape,
        in_specs=[VM] + [ANY] * 13,
        out_specs=[ANY] * 5 + [VM],
        scratch_shapes=scratch,
        compiler_params=pltpu.CompilerParams(vmem_limit_bytes=VMEM_LIMIT, collective_id=0, has_side_effects=True),
        cost_estimate=pl.CostEstimate(flops=2 * T * 12 * D * D, bytes_accessed=40 << 20, transcendentals=0),
        name="exchange",
    )(small, pair, gdS, eS, nS, guS, ybS, goS, aS, gpS, s1S, g1S, s2S, g2S)


def finish_kernel(ranks, stream, token_grad, inn, taps, out, up, down, small, *refs):
    outs, (gains, shifts, in_bias, taps_g, skips, out_bias, down_bias, up_bias, sem) = refs[:7], refs[7:]
    copies = [
        pltpu.make_async_copy(src, dst, sem.at[k])
        for k, (src, dst) in enumerate(zip((stream, token_grad, inn, taps, out, up, down), outs))
    ]
    for copy in copies:
        copy.start()
    D = small.shape[1]
    spot = lax.axis_index("dp")
    per, wide = gains.shape[1], up_bias.shape[1]
    turned = pltpu.roll(small[:UPB, :], lax.rem(D - spot * per, D), 1)
    for row, dst in ((GAIN, gains), (SHIFT, shifts), (SKIP, skips), (OUTB, out_bias), (DOWNB, down_bias)):
        dst[...] = turned[row : row + dst.shape[0], :per]
    for b in range(3):
        in_bias[b] = turned[INB + b : INB + b + 1, :per]
        for tap in range(3):
            taps_g[tap, b] = turned[TAP + 3 * tap + b : TAP + 3 * tap + b + 1, :per]
    row = small[pl.ds(UPB + spot * wide // D, 1), :]
    row = jnp.broadcast_to(row, (8, D))
    up_bias[...] = pltpu.roll(row, lax.rem(D - lax.rem(spot * wide, D), D), 1)[:1, :wide]
    for copy in copies:
        copy.wait()


def finish_call(stream, token_grad, inn, taps, out, up, down, small, ranks):
    D = small.shape[1]
    given = (stream, token_grad, inn, taps, out, up, down)
    shapes = [jax.ShapeDtypeStruct(x.shape, x.dtype) for x in given]
    per = D // ranks
    for shape in ((2, per), (2, per), (3, 1, per), (3, 3, 1, per), (2, per), (1, per), (1, per), (1, up.shape[1] // ranks)):
        shapes.append(jax.ShapeDtypeStruct(shape, f32))
    return pl.pallas_call(
        functools.partial(finish_kernel, ranks),
        out_shape=shapes,
        in_specs=[ANY] * 7 + [VM],
        out_specs=[ANY] * 7 + [VM] * 8,
        scratch_shapes=[pltpu.SemaphoreType.DMA((7,))],
        compiler_params=pltpu.CompilerParams(vmem_limit_bytes=VMEM_LIMIT),
        name="place_results",
    )(*given, small)


def dot_rows(x, y):
    return lax.dot_general(x, y, (((0,), (0,)), ((), ())), preferred_element_type=f32).astype(bf16)


def body(
    tokens, cotangent, norm_gains, norm_shifts, in_weight, in_bias, short_taps, long_filter, skip_gains,
    out_weight, out_bias, up_weight, up_bias, down_weight, down_bias,
):
    count = lax.axis_size("section")
    ranks = lax.axis_size("dp")
    tok, cot = tokens[0], cotangent[0]
    T, D = tok.shape
    FF = up_weight.shape[2]
    pieces = T // CH
    pair = table()
    params = (
        norm_gains[0], norm_shifts[0], in_bias[0], short_taps[0], skip_gains[0], out_bias, down_bias, up_bias,
    )
    win, wout, wup, wdown, filt = in_weight[0], out_weight[0], up_weight[0], down_weight[0], long_filter[0]

    (stream, token_grad, aS, ybS, nS, eS, s1S, s2S, gdS, guS, goS, gpS, g1S, g2S, small) = pass_call(
        params, tok, cot, filt, win, wout, wup, wdown, pair, count
    )
    if ranks == 16 and D % (16 * ranks) == 0 and T == 64 * ranks and FF == 4 * D and pieces == 4:
        downT, up, out, inn, taps, small = exchange_call(
            small, pair, gdS, eS, nS, guS, ybS, goS, aS, gpS, s1S, g1S, s2S, g2S, ranks
        )
        stream, token_grad, inn, taps, out, up, downT, *smalls, up_bias_grad = finish_call(
            stream, token_grad, inn, taps, out, up, downT, small, ranks
        )
        gains, shifts, in_b, taps_g, skips, out_b, down_b = smalls
        in_b, taps_g = in_b.transpose(1, 0, 2), taps_g.transpose(2, 0, 1, 3)
    else:
        slab = jnp.concatenate([dot_rows(gdS, eS), dot_rows(nS, guS), dot_rows(ybS, goS), dot_rows(aS, gpS)], axis=1)
        taps = jnp.concatenate([filter_call(s1S, g1S, pair), filter_call(s2S, g2S, pair)], axis=1)
        small = jnp.sum(small, axis=1)
        per = D // ranks
        mini = jnp.concatenate(
            [small[:UPB].reshape(UPB, ranks, per).transpose(1, 0, 2).reshape(ranks, -1), small[UPB:].reshape(ranks, -1)], axis=1
        )
        scatter = lambda x: lax.psum_scatter(x, "dp", scatter_dimension=0, tiled=True).astype(f32)
        slab, taps, mini = scatter(slab), scatter(taps), scatter(mini)[0]
        head = mini[: UPB * per].reshape(UPB, per)
        up_bias_grad = mini[UPB * per :]
        taps = taps.reshape(-1, 2, D).transpose(1, 0, 2)
        downT, up, out, inn = (slab[:, i:j] for i, j in ((0, FF), (FF, 2 * FF), (2 * FF, 2 * FF + D), (2 * FF + D, None)))
        gains, shifts, skips = (head[k : k + 2] for k in (GAIN, SHIFT, SKIP))
        in_b, taps_g = head[INB : INB + 3][None], head[TAP : TAP + 9].reshape(1, 3, 3, per)
        out_b, down_b = head[OUTB][None], head[DOWNB][None]
    return (
        stream[None], token_grad[None], gains[None], shifts[None], inn[None], in_b, taps_g, taps[None], skips[None],
        out[None], out_b, up[None], up_bias_grad.reshape(1, -1), downT.T[None], down_b,
    )


def solution(mesh):
    whole = P("dp", None, None)
    split = lambda n: P("section", *([None] * n))
    return jax.shard_map(
        body,
        mesh=mesh,
        in_specs=(
            whole, whole, split(2), split(2), split(2), split(2), split(3), split(3), split(2), split(2), split(1),
            split(2), split(1), split(2), split(1),
        ),
        out_specs=(
            P("dp", "section", None),
            P("dp", "section", None),
            P("section", None, "dp"),
            P("section", None, "dp"),
            P("section", "dp", None),
            P("section", None, "dp"),
            P("section", None, None, "dp"),
            P("section", None, "dp", None),
            P("section", None, "dp"),
            P("section", "dp", None),
            P("section", "dp"),
            P("section", "dp", None),
            P("section", "dp"),
            P("section", None, "dp"),
            P("section", "dp"),
        ),
        check_vma=False,
    )
```

```python
import functools
import math

import jax
import jax.numpy as jnp
import ml_dtypes
import numpy as np
from jax import lax
from jax.experimental import pallas as pl
from jax.experimental.pallas import tpu as pltpu
from jax.sharding import PartitionSpec as P

CH = 256
FT = 512
CARRY = 8
f32, bf16 = jnp.float32, jnp.bfloat16
VMEM_LIMIT = 60 * 1024 * 1024
ANY = pl.BlockSpec(memory_space=pl.ANY)
SMEM = pl.BlockSpec(memory_space=pltpu.SMEM)
VM = pl.BlockSpec(memory_space=pltpu.VMEM)

GAIN, SHIFT, INB, TAP, SKIP, OUTB, DOWNB, UPB = 0, 2, 4, 7, 16, 18, 19, 20


def table():
    order = np.concatenate([np.arange(0, CH, 2), np.arange(1, CH, 2)])
    angle = np.pi * ((2 * order[:, None] + 1) * np.arange(CH)[None] % (4 * CH)) / (2 * CH)
    cos, sin = np.cos(angle), np.sin(angle)
    sign = np.where(order % 2 == 0, 1.0, -1.0)[:, None]
    spread = np.concatenate([cos, -sin], 0)
    turned = np.concatenate([sign * sin, sign * cos], 0)
    return jnp.asarray(np.concatenate([turned, spread], 1).astype(ml_dtypes.bfloat16))


def back_table(pair, at):
    return jnp.transpose(pair[:, at : at + CH].astype(f32) * (1.0 / CH)).astype(bf16)


def dot(x, y):
    return jnp.dot(x, y, preferred_element_type=f32)


def dot_nt(x, y):
    return lax.dot_general(x, y, (((1,), (1,)), ((), ())), preferred_element_type=f32)


def rows_at(index, size):
    return pl.ds(pl.multiple_of(index * size, size), size)


def for_rows(total, size, step, unroll=1):
    def run(i, carry):
        step(pl.multiple_of(i * size, size))
        return carry

    lax.fori_loop(0, total // size, run, 0, unroll=unroll)


def normalize(rows):
    average = jnp.mean(rows, axis=-1, keepdims=True)
    centered = rows - average
    scale = lax.rsqrt(jnp.mean(centered * centered, axis=-1, keepdims=True) + 1e-05)
    return centered * scale, scale


def norm_back(z, gain, unit, scale):
    w = z * gain
    return (
        w - jnp.mean(w, axis=-1, keepdims=True) - unit * jnp.mean(w * unit, axis=-1, keepdims=True)
    ) * scale


def gelu_pair(u):
    phi_sum = 0.5 + 0.5 * lax.erf(u * math.sqrt(0.5))
    bell = jnp.exp(-0.5 * (u * u))
    return u * phi_sum, phi_sum + u * (bell * (1.0 / math.sqrt(2.0 * math.pi)))


def mix_spectra(left, right, out, terms, conj):
    width = out.shape[1] // 2

    def tile(step, carry):
        r = pl.multiple_of(step * 16, 16)
        for half in range(2):
            cols = slice(half * width, (half + 1) * width)
            real = imag = None
            for i, j in terms:
                ar = left[i, pl.ds(r, 16), cols]
                ai = left[i, pl.ds(CH + r, 16), cols]
                br = right[j, pl.ds(r, 16), cols]
                bi = right[j, pl.ds(CH + r, 16), cols]
                if conj:
                    pr, pi = ar * br + ai * bi, ar * bi - ai * br
                else:
                    pr, pi = ar * br - ai * bi, ar * bi + ai * br
                real, imag = (pr, pi) if real is None else (real + pr, imag + pi)
            out[pl.ds(r, 16), cols] = real
            out[pl.ds(CH + r, 16), cols] = imag
        return carry

    lax.fori_loop(0, CH // 16, tile, 0, unroll=16)


def mix_at(seg, pieces, left, right, out, conj):
    for s in range(pieces):
        terms = [(j - s, j) for j in range(s, pieces)] if conj else [(s - j, j) for j in range(s + 1)]

        @pl.when(seg == s)
        def _(terms=terms):
            mix_spectra(left, right, out, terms, conj)


def fold_rows(x):
    return jnp.sum(x.reshape(x.shape[0] // 8, 8, x.shape[1]), axis=0)


def pieces_of(at, wide, D):
    spans, off = [], 0
    while off < wide:
        row, col = (at + off) // D, (at + off) % D
        size = min(D - col, wide - off)
        spans.append((row, col, off, size))
        off += size
    return spans


def pass_kernel(
    sections, pieces, gains, shifts, inb_p, taps_p, skips, outb_p, downb_p, upb_p, tokens, cots, filt, win, wout, wup, wdown, pair_h,
    stream, gtok, aS, ybS, nS, eS, s1S, s2S, gdS, guS, goS, gpS, g1S, g2S, smallO,
    inf, inb, gin, winb, woutb, wupb, wdownb, back, pair, k1, k2, sp1, sp2, pall, y1all, mall, dall,
    ab, lead, leadlow, spec, wide, gate2, mid, nb, tile2, hid, outb, outfb, gnb, gqb, gpb, small,
    par, wsem, osem, fsem, bsem, ssem, gsem,
):
    rank = lax.axis_index("section")
    first, final = rank == 0, rank == sections - 1
    D, FF = woutb.shape[0], wupb.shape[1]
    tiles = FF // FT
    T = pieces * CH
    share = T // sections
    sub = min(CH, share)
    at = lambda r: {"section": r}

    def when(condition):
        return pl.when(condition)

    def remote(src, dst, send, recv, r):
        return pltpu.make_async_remote_copy(
            src_ref=src, dst_ref=dst, send_sem=send, recv_sem=recv, device_id=at(r), device_id_type=pl.DeviceIdType.MESH
        )

    def local(src, dst, sem):
        return pltpu.make_async_copy(src, dst, sem)

    loads = [
        local(win, winb, wsem.at[0]),
        local(wout, woutb, wsem.at[1]),
        local(wup, wupb, wsem.at[2]),
        local(wdown, wdownb, wsem.at[3]),
        local(pair_h, pair, wsem.at[4]),
    ]
    fill = [local(filt.at[f, pl.ds(0, CH)], sp.at[0, pl.ds(CH, CH)], wsem.at[7 + f]) for f, sp in enumerate((sp1, sp2))]
    for seg in range(1, pieces):
        window = pl.ds((seg - 1) * CH, 2 * CH)
        fill += [local(filt.at[f, window], sp.at[seg], wsem.at[7 + 2 * seg + f]) for f, sp in enumerate((sp1, sp2))]

    def own_chunk(src, dst, seg, sems):
        return local(src.at[rows_at(seg, CH)], dst.at[seg], sems.at[1, seg])

    def relay(src, dst, seg, sems, r):
        return remote(src, dst.at[seg], sems.at[0, seg], sems.at[1, seg], r)

    @when(first)
    def _():
        own_chunk(tokens, inf, 0, fsem).start()

    loads[4].start()
    for copy in fill[:2]:
        copy.start()
    loads[0].start()

    @when(first)
    def _():
        for seg in range(1, pieces):
            own_chunk(tokens, inf, seg, fsem).start()

    for copy in loads[1:4] + fill[2:]:
        copy.start()

    @when(final)
    def _():
        for seg in range(pieces):
            own_chunk(cots, inb, seg, bsem).start()

    for row, given in ((GAIN, gains), (SHIFT, shifts), (INB, inb_p), (SKIP, skips), (OUTB, outb_p), (DOWNB, downb_p)):
        par[row : row + given.shape[0], :] = given[...].astype(f32)
    for tap in range(3):
        par[TAP + 3 * tap : TAP + 3 * tap + 3, :] = taps_p[tap].astype(f32)
    for k in range(FF // D):
        par[UPB + k : UPB + k + 1, :] = upb_p[:, k * D : (k + 1) * D].astype(f32)

    barrier = pltpu.get_barrier_semaphore()
    for r in range(sections):

        @when(rank != r)
        def _(r=r):
            pl.semaphore_signal(barrier, inc=1, device_id=at(r), device_id_type=pl.DeviceIdType.MESH)

    if sections > 1:
        pl.semaphore_wait(barrier, sections - 1)

    pall[pl.ds(0, 16), :] = jnp.zeros((16, 3 * D), bf16)
    for sp in (sp1, sp2):
        sp[0, pl.ds(0, CH), :] = jnp.zeros((CH, D), bf16)
    small[...] = jnp.zeros(small.shape, f32)
    gqb[pl.ds(CH, CARRY), :] = jnp.zeros((CARRY, 3 * D), f32)

    def filter_spectra(seg):
        k1[seg] = dot(pair[...], sp1[seg]).astype(bf16)
        k2[seg] = dot(pair[...], sp2[seg]).astype(bf16)

    loads[4].wait()
    back[...] = back_table(pair, CH)
    for copy in fill[:2]:
        copy.wait()
    filter_spectra(0)

    @when(jnp.logical_not(first))
    def _():
        for copy in fill[2:]:
            copy.wait()

        def run(seg, carry):
            filter_spectra(seg)
            return carry

        lax.fori_loop(1, pieces, run, 0)

    def out_parts(seg, src, dst, sems, to_self):
        found = []
        for j in range(CH // sub):
            row = seg * CH + j * sub
            r, off = row // share, row % share
            found.append((r, off, src.at[pl.ds(j * sub, sub)], sems.at[0, seg * (CH // sub) + j], off // sub))
        return found

    def put(src, dst, k):
        return local(src, dst, osem.at[k])

    def forward_chunk(seg, carry):
        here = rows_at(seg, CH)
        base = pl.multiple_of(seg * CH, CH)
        hb = inf.at[seg]
        slot = 0
        later = seg > 0

        def before(copy):
            @when(later)
            def _():
                copy.wait()

        puts = [
            put(ab, aS.at[here], 0), put(sp1.at[seg], s1S.at[seg], 1), put(sp2.at[seg], s2S.at[seg], 2),
            put(leadlow, ybS.at[here], 3), put(nb, nS.at[here], 4), put(hid, eS.at[here], 5),
        ]

        @when(first)
        def _():
            own_chunk(tokens, inf, seg, fsem).wait()

        @when(jnp.logical_not(first))
        def _():
            relay(outb.at[slot], inf, seg, fsem, rank).wait_recv()

        before(puts[0])

        def ln1(r):
            unit, _ = normalize(hb[pl.ds(r, 32), :].astype(f32))
            ab[pl.ds(r, 32), :] = (unit * par[GAIN : GAIN + 1, :] + par[SHIFT : SHIFT + 1, :]).astype(bf16)

        for_rows(CH, 32, ln1, 8)
        puts[0].start()

        @when(seg == 0)
        def _():
            loads[0].wait()

        for b in range(3):
            cols = slice(b * D, (b + 1) * D)
            value = dot(ab[...], winb[:, cols]) + par[INB + b : INB + b + 1, :]
            pall[pl.ds(pl.multiple_of(base + 16, 16), CH), cols] = value.astype(bf16)

        before(puts[3])

        def short(r):
            got = [branch(base + r, b)[0] for b in range(3)]
            gate2[pl.ds(r, 32), :] = got[2]
            s = got[0] * got[1]
            lead[pl.ds(r, 32), :] = s
            leadlow[pl.ds(r, 32), :] = s.astype(bf16)

        ahead = first & (seg < pieces - 1)

        @when(ahead)
        def _():
            @when(seg == 0)
            def _():
                for copy in fill[2:]:
                    copy.wait()

            for_rows(CH, 32, short, 8)
            filter_spectra(seg + 1)

        @when(jnp.logical_not(ahead))
        def _():
            for_rows(CH, 32, short, 8)

        sp1[seg] = dot(pair[:, CH:], leadlow[...]).astype(bf16)
        puts[1].start()
        mix_at(seg, pieces, k1, sp1, spec, False)
        wide[...] = dot(back[...], spec[...])

        def second(r):
            rows = pl.ds(r, 64)
            y = wide[rows, :] + par[SKIP : SKIP + 1, :] * lead[rows, :]
            y1all[seg, rows, :] = y.astype(bf16)
            trail = y * gate2[rows, :]
            lead[rows, :] = trail
            leadlow[rows, :] = trail.astype(bf16)

        for_rows(CH, 64, second, 4)
        sp2[seg] = dot(pair[:, CH:], leadlow[...]).astype(bf16)
        puts[2].start()
        mix_at(seg, pieces, k2, sp2, spec, False)
        leadlow[...] = (dot(back[...], spec[...]) + par[SKIP + 1 : SKIP + 2, :] * lead[...]).astype(bf16)
        puts[3].start()

        @when(seg == 0)
        def _():
            loads[1].wait()

        wide[...] = dot(leadlow[...], woutb[...])
        before(puts[4])

        def ln2(r):
            rows = pl.ds(r, 32)
            m = hb[rows, :].astype(f32) + (wide[rows, :] + par[OUTB : OUTB + 1, :])
            mall[seg, rows, :] = m.astype(bf16)
            unit, _ = normalize(m)
            nb[rows, :] = (unit * par[GAIN + 1 : GAIN + 2, :] + par[SHIFT + 1 : SHIFT + 2, :]).astype(bf16)
            mid[rows, :] = m + par[DOWNB : DOWNB + 1, :]

        for_rows(CH, 32, ln2, 8)
        puts[4].start()

        @when(seg == 0)
        def _():
            loads[2].wait()
            loads[3].wait()

        before(puts[5])

        def up(k):
            return dot(nb[...], wupb[:, k * FT : (k + 1) * FT])

        def act(k):
            spans = pieces_of(k * FT, FT, D)
            bias = [par[UPB + row : UPB + row + 1, col : col + size] for row, col, _, size in spans]
            bias = bias[0] if len(bias) == 1 else jnp.concatenate(bias, axis=1)
            e, d = gelu_pair(tile2[k % 2] + bias)
            hid[:, k * FT : (k + 1) * FT] = e.astype(bf16)
            dall[seg, :, k * FT : (k + 1) * FT] = d.astype(bf16)

        def down(k):
            mid[...] += dot(hid[:, k * FT : (k + 1) * FT], wdownb[k * FT : (k + 1) * FT, :])

        tile2[0] = up(0)
        for k in range(tiles):
            if k + 1 < tiles:
                tile2[(k + 1) % 2] = up(k + 1)
            act(k)
            if k >= 1:
                down(k - 1)
        down(tiles - 1)
        puts[5].start()

        @when(later)
        def _():
            finish_out(seg - 1, slot)

        outb[slot] = mid[...].astype(bf16)

        @when(jnp.logical_not(final))
        def _():
            relay(outb.at[slot], inf, seg, fsem, rank + 1).start()

        @when(final)
        def _():
            for r, off, src, sem, k in out_parts(seg, outb.at[slot], stream, ssem, None):

                @when(r != rank)
                def _():
                    remote(src, stream.at[pl.ds(pl.multiple_of(off, sub), sub)], sem, ssem.at[1, k], r).start()

                @when(r == rank)
                def _():
                    local(src, stream.at[pl.ds(pl.multiple_of(off, sub), sub)], sem).start()

        return carry

    def finish_out(seg, slot):
        @when(jnp.logical_not(final))
        def _():
            relay(outb.at[slot], inf, seg, fsem, rank + 1).wait_send()

        @when(final)
        def _():
            for r, off, src, sem, k in out_parts(seg, outb.at[slot], stream, ssem, None):

                @when(r != rank)
                def _():
                    remote(src, stream.at[pl.ds(pl.multiple_of(off, sub), sub)], sem, ssem.at[1, k], r).wait_send()

                @when(r == rank)
                def _():
                    local(src, stream.at[pl.ds(pl.multiple_of(off, sub), sub)], sem).wait()

    def branch(start, b):
        rows = pall[pl.ds(pl.multiple_of(start, 16), 48), b * D : (b + 1) * D].astype(f32)
        late = [rows[16 - i : 48 - i] for i in range(3)]
        t = [par[TAP + 3 * i + b : TAP + 3 * i + b + 1, :] for i in range(3)]
        return t[0] * late[0] + t[1] * late[1] + t[2] * late[2], late

    lax.fori_loop(0, pieces, forward_chunk, 0)
    last = pieces - 1
    here = rows_at(last, CH)
    for copy in (
        put(ab, aS.at[here], 0), put(sp1.at[last], s1S.at[last], 1), put(sp2.at[last], s2S.at[last], 2),
        put(leadlow, ybS.at[here], 3), put(nb, nS.at[here], 4), put(hid, eS.at[here], 5),
    ):
        copy.wait()
    for k in range(last):
        put(sp1.at[k], s1S.at[k], 1).wait()
        put(sp2.at[k], s2S.at[k], 2).wait()
    finish_out(last, 0)

    def add_small(k, x, cols=slice(None)):
        small[k, :, cols] += fold_rows(x)

    def backward_chunk(i, carry):
        seg = pieces - 1 - i
        here = rows_at(seg, CH)
        base = pl.multiple_of(seg * CH, CH)
        gdb, hb = inb.at[seg], inf.at[seg]
        slot = 0

        def before(copy):
            @when(i > 0)
            def _():
                copy.wait()

        puts = [
            put(gdb, gdS.at[here], 6), put(hid, guS.at[here], 7), put(nb, goS.at[here], 8), put(gpb, gpS.at[here], 9),
            put(sp2.at[seg], g2S.at[seg], 10), put(sp1.at[seg], g1S.at[seg], 11),
        ]

        @when(final)
        def _():
            own_chunk(cots, inb, seg, bsem).wait()

        @when(jnp.logical_not(final))
        def _():
            relay(outb.at[slot], inb, seg, bsem, rank).wait_recv()

        before(puts[0])
        puts[0].start()
        before(puts[1])

        def down(k):
            return dot_nt(gdb[...], wdownb[k * FT : (k + 1) * FT, :])

        def act(k):
            cols = slice(k * FT, (k + 1) * FT)
            gu = (dall[seg, :, cols].astype(f32) * tile2[k % 2]).astype(bf16)
            hid[:, cols] = gu
            total = fold_rows(gu.astype(f32))
            for row, col, off, size in pieces_of(k * FT, FT, D):
                small[UPB + row, :, col : col + size] += total[:, off : off + size]

        def up(k):
            part = dot_nt(hid[:, k * FT : (k + 1) * FT], wupb[:, k * FT : (k + 1) * FT])
            if k == 0:
                gnb[...] = part
            else:
                gnb[...] += part

        tile2[0] = down(0)
        for k in range(tiles):
            if k + 1 < tiles:
                tile2[(k + 1) % 2] = down(k + 1)
            act(k)
            if k >= 1:
                up(k - 1)
        up(tiles - 1)
        puts[1].start()
        before(puts[2])

        def ln2(r):
            rows = pl.ds(r, 32)
            unit, scale = normalize(mall[seg, rows, :].astype(f32))
            z = gnb[rows, :]
            gd = gdb[rows, :].astype(f32)
            gm = gd + norm_back(z, par[GAIN + 1 : GAIN + 2, :], unit, scale)
            mid[rows, :] = gm
            go = gm.astype(bf16)
            nb[rows, :] = go
            add_small(GAIN + 1, z * unit)
            add_small(SHIFT + 1, z)
            add_small(OUTB, go.astype(f32))
            add_small(DOWNB, gd)

        for_rows(CH, 32, ln2, 8)
        puts[2].start()
        gy = dot_nt(nb[...], woutb[...])
        lead[...] = gy
        leadlow[...] = gy.astype(bf16)
        sp2[seg] = dot(pair[:, CH:], leadlow[...]).astype(bf16)
        puts[4].start()
        mix_at(seg, pieces, k2, sp2, spec, True)
        wide[...] = dot(back[...], spec[...])

        def keep(r, b, grad, late):
            gqb[pl.ds(r, 32), b * D : (b + 1) * D] = grad
            for tap in range(3):
                add_small(TAP + 3 * tap + b, grad * late[tap])

        def second(r):
            rows = pl.ds(r, 32)
            gate, late = branch(base + r, 2)
            y1 = y1all[seg, rows, :].astype(f32)
            gy2 = lead[rows, :]
            gs2 = wide[rows, :] + par[SKIP + 1 : SKIP + 2, :] * gy2
            gy1 = gs2 * gate
            gate2[rows, :] = gy1
            leadlow[rows, :] = gy1.astype(bf16)
            add_small(SKIP + 1, gy2 * (y1 * gate))
            keep(r, 2, gs2 * y1, late)

        for_rows(CH, 32, second, 8)
        sp1[seg] = dot(pair[:, CH:], leadlow[...]).astype(bf16)
        puts[5].start()
        mix_at(seg, pieces, k1, sp1, spec, True)
        wide[...] = dot(back[...], spec[...])

        def lower(r):
            rows = pl.ds(r, 32)
            carrier, late_carrier = branch(base + r, 0)
            gate, late_gate = branch(base + r, 1)
            gy1 = gate2[rows, :]
            gs1 = wide[rows, :] + par[SKIP : SKIP + 1, :] * gy1
            add_small(SKIP, gy1 * (carrier * gate))
            keep(r, 0, gs1 * gate, late_carrier)
            keep(r, 1, gs1 * carrier, late_gate)

        for_rows(CH, 32, lower, 8)
        before(puts[3])

        def short(r):
            for b in range(3):
                cols = slice(b * D, (b + 1) * D)
                rows = gqb[pl.ds(r, 32 + CARRY), cols]
                t = [par[TAP + 3 * tap + b : TAP + 3 * tap + b + 1, :] for tap in range(3)]
                gp = (t[0] * rows[:32] + t[1] * rows[1:33] + t[2] * rows[2:34]).astype(bf16)
                gpb[pl.ds(r, 32), cols] = gp
                add_small(INB + b, gp.astype(f32))

        for_rows(CH, 32, short, 8)
        puts[3].start()
        gqb[pl.ds(CH, CARRY), :] = gqb[pl.ds(0, CARRY), :]
        gnb[...] = dot_nt(gpb[...], winb[...])

        @when(i > 0)
        def _():
            finish_grad(i - 1, slot)

        def ln1(r):
            rows = pl.ds(r, 32)
            unit, scale = normalize(hb[rows, :].astype(f32))
            z = gnb[rows, :]
            gh = mid[rows, :] + norm_back(z, par[GAIN : GAIN + 1, :], unit, scale)
            outfb[slot, rows, :] = gh
            outb[slot, rows, :] = gh.astype(bf16)
            add_small(GAIN, z * unit)
            add_small(SHIFT, z)

        for_rows(CH, 32, ln1, 8)

        @when(jnp.logical_not(first))
        def _():
            relay(outb.at[slot], inb, seg, bsem, rank - 1).start()

        @when(first)
        def _():
            for r, off, src, sem, k in out_parts(seg, outb.at[slot], gtok, gsem, None):
                whole = outfb.at[slot, pl.ds(lax.rem(seg * CH + off, CH) if sub < CH else 0, sub)]

                @when(r != rank)
                def _():
                    remote(src, gin.at[k], sem, gsem.at[1, k], r).start()

                @when(r == rank)
                def _():
                    local(whole, gtok.at[pl.ds(pl.multiple_of(off, sub), sub)], sem).start()

        return carry

    def finish_grad(i, slot):
        seg = pieces - 1 - i

        @when(jnp.logical_not(first))
        def _():
            relay(outb.at[slot], inb, seg, bsem, rank - 1).wait_send()

        @when(first)
        def _():
            for r, off, src, sem, k in out_parts(seg, outb.at[slot], gtok, gsem, None):
                whole = outfb.at[slot, pl.ds(0, sub)]

                @when(r != rank)
                def _():
                    remote(src, gin.at[k], sem, gsem.at[1, k], r).wait_send()

                @when(r == rank)
                def _():
                    local(whole, gtok.at[pl.ds(pl.multiple_of(off, sub), sub)], sem).wait()

    lax.fori_loop(0, pieces, backward_chunk, 0)
    here = rows_at(0, CH)
    ends = [
        put(inb.at[0], gdS.at[here], 6), put(hid, guS.at[here], 7), put(nb, goS.at[here], 8), put(gpb, gpS.at[here], 9),
        put(sp2.at[0], g2S.at[0], 10), put(sp1.at[0], g1S.at[0], 11),
    ]
    for copy in ends:
        copy.wait()
    for k in range(last):
        ends[4].wait()
        ends[5].wait()
    total = put(small, smallO, 12)
    total.start()
    finish_grad(last, 0)
    parts = share // sub

    @when(jnp.logical_not(final))
    def _():
        for k in range(parts):
            remote(outb.at[0, pl.ds(0, sub)], stream.at[pl.ds(k * sub, sub)], ssem.at[0, 0], ssem.at[1, k], rank).wait_recv()

    @when(jnp.logical_not(first))
    def _():
        for k in range(parts):
            remote(outb.at[0, pl.ds(0, sub)], gin.at[k], gsem.at[0, 0], gsem.at[1, k], rank).wait_recv()
            outfb[0, pl.ds(0, sub), :] = gin[k].astype(f32)
            copy = local(outfb.at[0, pl.ds(0, sub)], gtok.at[pl.ds(k * sub, sub)], gsem.at[0, k])
            copy.start()
            copy.wait()

    total.wait()


def pass_call(params, tokens, cots, filt, win, wout, wup, wdown, pair, sections):
    T, D = tokens.shape
    FF = wup.shape[1]
    pieces = T // CH
    share = T // sections
    sub = min(CH, share)
    spec3 = (pieces, 2 * CH, D)
    small = (UPB + FF // D, 8, D)
    shapes = [
        ((share, D), bf16), ((share, D), f32),
        ((T, D), bf16), ((T, D), bf16), ((T, D), bf16), ((T, FF), bf16), (spec3, bf16), (spec3, bf16),
        ((T, D), bf16), ((T, FF), bf16), ((T, D), bf16), ((T, 3 * D), bf16), (spec3, bf16), (spec3, bf16),
        (small, f32),
    ]
    V, S = pltpu.VMEM, pltpu.SemaphoreType.DMA
    chunk, chunks = (CH, D), (pieces, CH, D)
    scratch = [
        V(chunks, bf16), V(chunks, bf16), V((share // sub, sub, D), bf16),
        V(win.shape, bf16), V(wout.shape, bf16), V(wup.shape, bf16), V(wdown.shape, bf16),
        V((CH, 2 * CH), bf16), V((2 * CH, 2 * CH), bf16),
        V(spec3, bf16), V(spec3, bf16), V(spec3, bf16), V(spec3, bf16),
        V((16 + T, 3 * D), bf16), V(chunks, bf16), V(chunks, bf16), V((pieces, CH, FF), bf16),
        V(chunk, bf16), V(chunk, f32), V(chunk, bf16), V((2 * CH, D), bf16), V(chunk, f32), V(chunk, f32), V(chunk, f32),
        V(chunk, bf16), V((2, CH, FT), f32), V((CH, FF), bf16), V((1,) + chunk, bf16), V((1,) + chunk, f32),
        V(chunk, f32), V((CH + CARRY, 3 * D), f32), V((CH, 3 * D), bf16), V(small, f32), V((UPB + FF // D, D), f32),
        S((7 + 2 * pieces,)), S((13,)), S((2, pieces)), S((2, pieces)), S((2, T // sub)), S((2, T // sub)),
    ]
    return pl.pallas_call(
        functools.partial(pass_kernel, sections, pieces),
        out_shape=[jax.ShapeDtypeStruct(*s) for s in shapes],
        in_specs=[VM] * 8 + [ANY] * 8,
        out_specs=[ANY] * len(shapes),
        scratch_shapes=scratch,
        compiler_params=pltpu.CompilerParams(vmem_limit_bytes=63 * 1024 * 1024, collective_id=1, has_side_effects=True),
        name="layer_pass",
    )(*params, tokens, cots, filt, win, wout, wup, wdown, pair)


def filter_kernel(pieces, s, g, back, turned, out, q):
    for d in range(pieces):
        mix_spectra(s, g, q.at[d], [(j - d, j) for j in range(d, pieces)], True)
    for d in range(pieces):
        rows = dot(back[...], q[d])
        if d + 1 < pieces:
            rows += dot(turned[...], q[d + 1])
        out[pl.ds(d * CH, CH), :] = rows.astype(bf16)


def filter_call(s, g, pair):
    pieces, _, D = s.shape
    turned, back = ((pair[:, k : k + CH].astype(f32) / CH).astype(bf16).T for k in (0, CH))
    return pl.pallas_call(
        functools.partial(filter_kernel, pieces),
        out_shape=jax.ShapeDtypeStruct((pieces * CH, D), bf16),
        in_specs=[VM] * 4,
        out_specs=VM,
        scratch_shapes=[pltpu.VMEM(s.shape, bf16)],
        compiler_params=pltpu.CompilerParams(vmem_limit_bytes=VMEM_LIMIT),
        name="filter_grad",
    )(s, g, back, turned)


def exchange_plan(groups, D):
    blocks = [("product", 0, g) for g in range(groups)] + [("filter", 0, 0)]
    blocks += [("product", 1, g) for g in range(groups)] + [("filter", 1, 0)]
    blocks += [("product", 2, g) for g in range(groups)]
    half = D // 2
    sent, flows = [], []
    for b in range(len(blocks)):
        spans = [(0, [(0, half, False)]), (half, [(half, half - 128, False), (D - 128, 128, True)])]
        if b == len(blocks) - 1:
            spans = [spans[1], (0, [(0, half - 128, False)]), (half - 128, [(half - 128, 128, False)])]
        for low, parts in spans:
            wide = sum(part[1] for part in parts)
            sent.append((b, low, wide, list(range(len(flows), len(flows) + len(parts)))))
            flows += [(b,) + part for part in parts]
    return blocks, sent, flows


def exchange_kernel(
    pieces, small_in, pair_h, gdS, eS, nS, guS, ybS, goS, aS, gpS, s1S, g1S, s2S, g2S,
    downT, upO, outO, inO, filtO, smallO,
    x, r1, r2, rr, rl, rrz, rlz, r2z, gb, lb, lt, sb, qb, pair, back, turned, ob, mine, got,
    lsem, osem, csem, ysem, rsem, fsem, msem,
):
    D = lb.shape[2]
    half = D // 2
    me = lax.axis_index("dp")
    c, y, z = me % 2, (me // 2) % 2, me // 4
    Z = r2.shape[1]
    groups = lt.shape[2]
    blocks, sent, flows = exchange_plan(groups, D)
    at = lambda i: {"dp": i}
    core_id, y_id = me + 1 - 2 * c, me + 2 - 4 * y
    mates = (core_id, y_id, me + 4 - 8 * (z % 2), me + 8 - 16 * (z // 2))
    inner = (z == 1) | (z == 2)

    def remote(src, dst, send, recv, mate):
        return pltpu.make_async_remote_copy(
            src_ref=src, dst_ref=dst, send_sem=send, recv_sem=recv, device_id=at(mate),
            device_id_type=pl.DeviceIdType.MESH,
        )

    def load(src, dst, k):
        return pltpu.make_async_copy(src, dst, lsem.at[k])

    rights = ((eS,), (guS,), (goS, gpS))
    lefts = ((gdS,), (nS,), (ybS, aS))
    turned_at = ((0,), (1,), (0, 2))

    def right_loads(m):
        found, off = [], 0
        for k, src in enumerate(rights[m]):
            wide = src.shape[1]
            found.append(load(src, gb.at[m % 2, :, pl.ds(off, wide)], 4 * m + k))
            off += wide
        return found

    def left_loads(m):
        return [load(src, lb.at[k], 4 * m + 2 + k) for k, src in enumerate(lefts[m])]

    def spectra(f):
        src = ((s1S, g1S), (s2S, g2S))[f]
        return [load(src[k], sb.at[k], 12 + 2 * f + k) for k in range(2)]

    def turn(m):
        for k, spot in enumerate(turned_at[m]):

            def part(i, carry, k=k, spot=spot):
                rows = pl.multiple_of(i * 128, 128)
                piece = jnp.transpose(lb[k, pl.ds(rows, 128), :])
                lt[spot, :, :, :, pl.ds(rows, 128)] = piece.reshape(lt.shape[1:4] + (128,))
                return carry

            lax.fori_loop(0, lb.shape[1] // 128, part, 0)

    def product(m, g, low, wide, slot):
        def part(i, carry):
            k = jnp.where(i == 0, 0, 2) if m == 2 else m
            left = lt[k, :, g].reshape(16 * lt.shape[1], lt.shape[4])
            cols = pl.ds(pl.multiple_of(i * D + low, 128), wide)
            value = dot(left, gb[m % 2, :, cols]).astype(bf16)
            x[slot, :, :, :, pl.ds(pl.multiple_of(i * 16, 16), 16), :wide] = value.reshape(x.shape[1:4] + (16, wide))
            return carry

        lax.fori_loop(0, 4, part, 0)

    def mix(d):
        mix_spectra(sb.at[0], sb.at[1], qb.at[d], [(j - d, j) for j in range(d, pieces)], True)

    def filters(low, slot):
        cols = slice(low, low + half)

        def part(d, carry):
            rows = dot(back[...], qb[d, :, cols]) + dot(turned[...], qb[d + 1, :, cols])
            x[slot, d] = rows.astype(bf16).reshape(x.shape[2:])
            return carry

        lax.fori_loop(0, pieces, part, 0)

    def core_copy(i):
        b, low, wide, _ = sent[i]
        return remote(
            x.at[i % x.shape[0], :, :, 1 - c, :, pl.ds(0, wide)], r1.at[b, :, :, :, pl.ds(low, wide)],
            csem.at[0, i], csem.at[1, i], core_id,
        )

    def add(p, q):
        return (p.astype(f32) + q.astype(f32)).astype(bf16)

    def after_core(i):
        b, low, wide, mine_flows = sent[i]
        core_copy(i).wait()
        cols = slice(low, low + wide)

        def part(k, carry):
            for j in range(2):
                r1[b, k, j, :, cols] = add(r1[b, k, j, :, cols], x[i % x.shape[0], k, j, c, :, :wide])
            return carry

        lax.fori_loop(0, Z, part, 0)
        for u in mine_flows:
            if not flows[u][3]:
                y_copy(u).start()

    def y_copy(u):
        b, low, wide, z_first = flows[u]
        cols = pl.ds(low, wide)
        if z_first:
            return remote(r1.at[b, z, 1 - y, :, cols], r2z.at[b], ysem.at[0, u], ysem.at[1, u], y_id)
        return remote(r1.at[b, :, 1 - y, :, cols], r2.at[b, :, :, cols], ysem.at[0, u], ysem.at[1, u], y_id)

    def after_y(u):
        b, low, wide, _ = flows[u]
        cols = slice(low, low + wide)
        y_copy(u).wait()

        def part(k, carry):
            r2[b, k, :, cols] = add(r2[b, k, :, cols], r1[b, k, y, :, cols])
            return carry

        lax.fori_loop(0, Z, part, 0)

    def own(u, d):
        b, low, wide, z_first = flows[u]
        cols = pl.ds(low, wide)
        return r1.at[b, d, :, :, cols] if z_first else r2.at[b, d, :, cols]

    def right_at(u, d):
        b, low, wide, z_first = flows[u]
        return rrz.at[b, d - 1] if z_first else rr.at[b, d - 1, :, pl.ds(low, wide)]

    def left_at(u, d):
        b, low, wide, z_first = flows[u]
        return rlz.at[b, d] if z_first else rl.at[b, d, :, pl.ds(low, wide)]

    def right_copy(u, d, src):
        return remote(src, right_at(u, d), rsem.at[0, u, d - 1], rsem.at[1, u, d - 1], me + 4)

    def left_copy(u, d, src):
        return remote(src, left_at(u, d), fsem.at[0, u, d], fsem.at[1, u, d], me - 4)

    def hop(u, h):
        @pl.when(z == h)
        def _():
            for d in range(Z - 1, h, -1):
                src = own(u, d)
                if h > 0:
                    right_copy(u, d, src).wait_recv()
                    src = right_at(u, d)
                    src[...] = add(src[...], own(u, d)[...])
                right_copy(u, d, src).start()

        @pl.when(z == Z - 1 - h)
        def _():
            for d in range(Z - 1 - h):
                src = own(u, d)
                if h > 0:
                    left_copy(u, d, src).wait_recv()
                    src = left_at(u, d)
                    src[...] = add(src[...], own(u, d)[...])
                left_copy(u, d, src).start()

    def gather(u, store):
        for p in range(Z):

            @pl.when(z == p)
            def _(p=p):
                total = own(u, p)[...].astype(f32)
                if p > 0:
                    right_copy(u, p, own(u, p)).wait_recv()
                    total += right_at(u, p)[...].astype(f32)
                if p < Z - 1:
                    left_copy(u, p, own(u, p)).wait_recv()
                    total += left_at(u, p)[...].astype(f32)
                for d in range(p + 1, Z):
                    right_copy(u, d, own(u, d)).wait_send()
                for d in range(p):
                    left_copy(u, d, own(u, d)).wait_send()
                store(p, total)

    def turn_to_y(u):
        def store(p, total):
            own(u, p)[...] = total.astype(bf16)

        gather(u, store)
        y_copy(u).start()

    def out_copies(i):
        b, low, wide, _ = sent[i]
        kind, a, g = blocks[b]
        slot = i % 2
        if kind == "filter":
            src = ob.at[slot, :, pl.ds(0, wide)]
            return [pltpu.make_async_copy(src, filtO.at[a, :, pl.ds(low, wide)], osem.at[4 * slot])]
        found = []
        rows = pl.ds(g * 16, 16)
        for k in range(4):
            if a < 2:
                dst = (downT, upO)[a].at[rows, pl.ds(k * D + low, wide)]
            elif k == 0:
                dst = outO.at[rows, pl.ds(low, wide)]
            else:
                dst = inO.at[rows, pl.ds((k - 1) * D + low, wide)]
            src = ob.at[slot, pl.ds(16 * k, 16), pl.ds(0, wide)]
            found.append(pltpu.make_async_copy(src, dst, osem.at[4 * slot + k]))
        return found

    def finish(i):
        b, low, _, mine_flows = sent[i]
        slot = i % 2
        if i >= 2:
            for copy in out_copies(i - 2):
                copy.wait()
        for u in mine_flows:
            _, first, wide, z_first = flows[u]
            cols = slice(first - low, first - low + wide)
            if z_first:
                y_copy(u).wait()
                ob[slot, :, cols] = r1[b, z, y, :, first : first + wide].astype(f32) + r2z[b].astype(f32)
            else:

                def store(p, total, cols=cols):
                    ob[slot, :, cols] = total

                gather(u, store)
        for copy in out_copies(i):
            copy.start()

    def mini_copy(k):
        return remote(mine.at[k], got.at[k], msem.at[0, k], msem.at[1, k], mates[k])

    tables_in = [load(pair_h, pair, 16)]
    early = [
        [load(eS.at[:, pl.ds(k * D + low, half)], gb.at[0, :, pl.ds(k * D + low, half)], 18 + 4 * (low > 0) + k) for k in range(4)]
        for low in (0, half)
    ]
    for copy in left_loads(0) + early[0] + early[1]:
        copy.start()
    barrier = pltpu.get_barrier_semaphore()
    for mate in mates:
        pl.semaphore_signal(barrier, inc=1, device_id=at(mate), device_id_type=pl.DeviceIdType.MESH)

    @pl.when(inner)
    def _():
        other = me + 12 - 8 * z
        pl.semaphore_signal(barrier, inc=1, device_id=at(other), device_id_type=pl.DeviceIdType.MESH)

    @pl.when(inner)
    def _():
        pl.semaphore_wait(barrier, len(mates) + 1)

    @pl.when(jnp.logical_not(inner))
    def _():
        pl.semaphore_wait(barrier, len(mates))

    mine[0] = jnp.sum(small_in[...], axis=1)
    qb[pieces] = jnp.zeros(qb.shape[1:], bf16)

    def compute(i):
        b, low, wide, _ = sent[i]
        kind, a, g = blocks[b]
        slot = i % x.shape[0]
        if kind == "product":
            if g == 0 and low == 0:
                if a == 0:
                    for copy in left_loads(0):
                        copy.wait()
                    turn(0)
                for copy in early[0] if a == 0 else right_loads(a):
                    copy.wait()
                if a == 1:
                    for copy in left_loads(a + 1) + right_loads(a + 1):
                        copy.start()
            if a == 0 and g == 0 and low > 0:
                for copy in early[1]:
                    copy.wait()
                for copy in tables_in + spectra(0) + left_loads(1) + right_loads(1):
                    copy.start()
            product(a, g, low, wide, slot)
            core_copy(i).start()
            if a < 2:
                step = 2 * g + (low > 0)
                if step == 2:
                    for copy in spectra(a):
                        copy.wait()
                if 2 <= step < 2 + pieces:
                    mix(step - 2)
        else:
            if a == 0 and low == 0:
                for copy in tables_in:
                    copy.wait()
                back[...] = back_table(pair, CH)
                turned[...] = back_table(pair, 0)
            filters(low, slot)
            core_copy(i).start()
            if low == 0:
                if a == 0:
                    for copy in spectra(1):
                        copy.start()
                for copy in left_loads(a + 1):
                    copy.wait()
                turn(a + 1)

    n = len(sent)
    by_y = lambda i: [u for u in sent[i][3] if not flows[u][3]]
    by_z = lambda i: [u for u in sent[i][3] if flows[u][3]]
    CORE, Y_DONE, HOP1, HOP2, DONE = 1, 3, 6, 9, 12
    for i in range(n + DONE):
        if i < n:
            compute(i)
        if 0 <= i - CORE < n:
            after_core(i - CORE)
            for u in by_z(i - CORE):
                hop(u, 0)
        if 0 <= i - Y_DONE < n:
            for u in by_z(i - Y_DONE):
                hop(u, 1)
            for u in by_y(i - Y_DONE):
                after_y(u)
                hop(u, 0)
        if 0 <= i - HOP1 < n:
            for u in by_z(i - HOP1):
                hop(u, 2)
            for u in by_y(i - HOP1):
                hop(u, 1)
        if 0 <= i - HOP2 < n:
            for u in by_z(i - HOP2):
                turn_to_y(u)
            for u in by_y(i - HOP2):
                hop(u, 2)
        if 0 <= i - DONE < n:
            finish(i - DONE)
        if i == 2:
            mini_copy(0).start()
        if i in (8, 14, 20, 26):
            k = (i - 8) // 6
            mini_copy(k).wait()
            total = mine[k] + got[k]
            if k < 3:
                mine[k + 1] = total
                mini_copy(k + 1).start()
            else:
                smallO[...] = total
    for i in (n - 2, n - 1):
        for copy in out_copies(i):
            copy.wait()


def exchange_call(small, pair, gdS, eS, nS, guS, ybS, goS, aS, gpS, s1S, g1S, s2S, g2S, ranks):
    T, D = aS.shape
    FF = eS.shape[1]
    pieces = T // CH
    per = D // ranks
    groups = per // 16
    blocks, sent, flows = exchange_plan(groups, D)
    n_blocks, n_sent, n_flows = len(blocks), len(sent), len(flows)
    Z, Y, rows = 4, 2, T // ranks
    V, S = pltpu.VMEM, pltpu.SemaphoreType.DMA
    shard = (rows, D)
    scratch = [
        V((3, Z, Y, 2, rows, D // 2), bf16),
        V((n_blocks, Z, Y) + shard, bf16),
        V((n_blocks, Z) + shard, bf16),
        V((n_blocks, Z - 1) + shard, bf16),
        V((n_blocks, Z - 1) + shard, bf16),
        V((n_blocks, Z - 1, Y, rows, 128), bf16),
        V((n_blocks, Z - 1, Y, rows, 128), bf16),
        V((n_blocks, rows, 128), bf16),
        V((2, T, FF), bf16),
        V((2, T, D), bf16),
        V((3, ranks, groups, 16, T), bf16),
        V((2,) + s1S.shape, bf16),
        V((pieces + 1, 2 * CH, D), bf16),
        V((2 * CH, 2 * CH), bf16),
        V((CH, 2 * CH), bf16),
        V((CH, 2 * CH), bf16),
        V((2, rows, D // 2), f32),
        V((4, small.shape[0], D), f32),
        V((4, small.shape[0], D), f32),
        S((26,)), S((8,)), S((2, n_sent)), S((2, n_flows)), S((2, n_flows, Z - 1)), S((2, n_flows, Z - 1)), S((2, 4)),
    ]
    out_shape = [
        jax.ShapeDtypeStruct(s, f32)
        for s in ((per, FF), (per, FF), (per, D), (per, 3 * D), (2, rows, D), (small.shape[0], D))
    ]
    return pl.pallas_call(
        functools.partial(exchange_kernel, pieces),
        out_shape=out_shape,
        in_specs=[VM] + [ANY] * 13,
        out_specs=[ANY] * 5 + [VM],
        scratch_shapes=scratch,
        compiler_params=pltpu.CompilerParams(vmem_limit_bytes=VMEM_LIMIT, collective_id=0, has_side_effects=True),
        cost_estimate=pl.CostEstimate(flops=2 * T * 12 * D * D, bytes_accessed=40 << 20, transcendentals=0),
        name="exchange",
    )(small, pair, gdS, eS, nS, guS, ybS, goS, aS, gpS, s1S, g1S, s2S, g2S)


def finish_kernel(ranks, stream, token_grad, inn, taps, out, up, down, small, *refs):
    outs, (gains, shifts, in_bias, taps_g, skips, out_bias, down_bias, up_bias) = refs[:7], refs[7:15]
    held, sem = refs[15:22], refs[22]
    given = (stream, token_grad, inn, taps, out, up, down)
    loads = [pltpu.make_async_copy(src, dst, sem.at[0, k]) for k, (src, dst) in enumerate(zip(given, held))]
    stores = [pltpu.make_async_copy(src, dst, sem.at[1, k]) for k, (src, dst) in enumerate(zip(held, outs))]
    for copy in loads:
        copy.start()
    D = small.shape[1]
    spot = lax.axis_index("dp")
    per, wide = gains.shape[1], up_bias.shape[1]
    turned = pltpu.roll(small[:UPB, :], lax.rem(D - spot * per, D), 1)
    for row, dst in ((GAIN, gains), (SHIFT, shifts), (SKIP, skips), (OUTB, out_bias), (DOWNB, down_bias)):
        dst[...] = turned[row : row + dst.shape[0], :per]
    for b in range(3):
        in_bias[b] = turned[INB + b : INB + b + 1, :per]
        for tap in range(3):
            taps_g[tap, b] = turned[TAP + 3 * tap + b : TAP + 3 * tap + b + 1, :per]
    row = small[pl.ds(UPB + spot * wide // D, 1), :]
    row = jnp.broadcast_to(row, (8, D))
    up_bias[...] = pltpu.roll(row, lax.rem(D - lax.rem(spot * wide, D), D), 1)[:1, :wide]
    for load, store in zip(loads, stores):
        load.wait()
        store.start()
    for store in stores:
        store.wait()


def finish_call(stream, token_grad, inn, taps, out, up, down, small, ranks):
    D = small.shape[1]
    given = (stream, token_grad, inn, taps, out, up, down)
    shapes = [jax.ShapeDtypeStruct(x.shape, x.dtype) for x in given]
    per = D // ranks
    for shape in ((2, per), (2, per), (3, 1, per), (3, 3, 1, per), (2, per), (1, per), (1, per), (1, up.shape[1] // ranks)):
        shapes.append(jax.ShapeDtypeStruct(shape, f32))
    return pl.pallas_call(
        functools.partial(finish_kernel, ranks),
        out_shape=shapes,
        in_specs=[ANY] * 7 + [VM],
        out_specs=[ANY] * 7 + [VM] * 8,
        scratch_shapes=[pltpu.VMEM(x.shape, x.dtype) for x in given] + [pltpu.SemaphoreType.DMA((2, 7))],
        compiler_params=pltpu.CompilerParams(vmem_limit_bytes=VMEM_LIMIT),
        name="place_results",
    )(*given, small)


def dot_rows(x, y):
    return lax.dot_general(x, y, (((0,), (0,)), ((), ())), preferred_element_type=f32).astype(bf16)


def body(
    tokens, cotangent, norm_gains, norm_shifts, in_weight, in_bias, short_taps, long_filter, skip_gains,
    out_weight, out_bias, up_weight, up_bias, down_weight, down_bias,
):
    count = lax.axis_size("section")
    ranks = lax.axis_size("dp")
    tok, cot = tokens[0], cotangent[0]
    T, D = tok.shape
    FF = up_weight.shape[2]
    pieces = T // CH
    pair = table()
    params = (
        norm_gains[0], norm_shifts[0], in_bias[0], short_taps[0], skip_gains[0], out_bias, down_bias, up_bias,
    )
    win, wout, wup, wdown, filt = in_weight[0], out_weight[0], up_weight[0], down_weight[0], long_filter[0]

    (stream, token_grad, aS, ybS, nS, eS, s1S, s2S, gdS, guS, goS, gpS, g1S, g2S, small) = pass_call(
        params, tok, cot, filt, win, wout, wup, wdown, pair, count
    )
    if ranks == 16 and D % (16 * ranks) == 0 and T == 64 * ranks and FF == 4 * D and pieces == 4:
        downT, up, out, inn, taps, small = exchange_call(
            small, pair, gdS, eS, nS, guS, ybS, goS, aS, gpS, s1S, g1S, s2S, g2S, ranks
        )
        stream, token_grad, inn, taps, out, up, downT, *smalls, up_bias_grad = finish_call(
            stream, token_grad, inn, taps, out, up, downT, small, ranks
        )
        gains, shifts, in_b, taps_g, skips, out_b, down_b = smalls
        in_b, taps_g = in_b.transpose(1, 0, 2), taps_g.transpose(2, 0, 1, 3)
    else:
        slab = jnp.concatenate([dot_rows(gdS, eS), dot_rows(nS, guS), dot_rows(ybS, goS), dot_rows(aS, gpS)], axis=1)
        taps = jnp.concatenate([filter_call(s1S, g1S, pair), filter_call(s2S, g2S, pair)], axis=1)
        small = jnp.sum(small, axis=1)
        per = D // ranks
        mini = jnp.concatenate(
            [small[:UPB].reshape(UPB, ranks, per).transpose(1, 0, 2).reshape(ranks, -1), small[UPB:].reshape(ranks, -1)], axis=1
        )
        scatter = lambda x: lax.psum_scatter(x, "dp", scatter_dimension=0, tiled=True).astype(f32)
        slab, taps, mini = scatter(slab), scatter(taps), scatter(mini)[0]
        head = mini[: UPB * per].reshape(UPB, per)
        up_bias_grad = mini[UPB * per :]
        taps = taps.reshape(-1, 2, D).transpose(1, 0, 2)
        downT, up, out, inn = (slab[:, i:j] for i, j in ((0, FF), (FF, 2 * FF), (2 * FF, 2 * FF + D), (2 * FF + D, None)))
        gains, shifts, skips = (head[k : k + 2] for k in (GAIN, SHIFT, SKIP))
        in_b, taps_g = head[INB : INB + 3][None], head[TAP : TAP + 9].reshape(1, 3, 3, per)
        out_b, down_b = head[OUTB][None], head[DOWNB][None]
    return (
        stream[None], token_grad[None], gains[None], shifts[None], inn[None], in_b, taps_g, taps[None], skips[None],
        out[None], out_b, up[None], up_bias_grad.reshape(1, -1), downT.T[None], down_b,
    )


def solution(mesh):
    whole = P("dp", None, None)
    split = lambda n: P("section", *([None] * n))
    return jax.shard_map(
        body,
        mesh=mesh,
        in_specs=(
            whole, whole, split(2), split(2), split(2), split(2), split(3), split(3), split(2), split(2), split(1),
            split(2), split(1), split(2), split(1),
        ),
        out_specs=(
            P("dp", "section", None),
            P("dp", "section", None),
            P("section", None, "dp"),
            P("section", None, "dp"),
            P("section", "dp", None),
            P("section", None, "dp"),
            P("section", None, None, "dp"),
            P("section", None, "dp", None),
            P("section", None, "dp"),
            P("section", "dp", None),
            P("section", "dp"),
            P("section", "dp", None),
            P("section", "dp"),
            P("section", None, "dp"),
            P("section", "dp"),
        ),
        check_vma=False,
    )
```

```python
import functools
import math

import jax
import jax.numpy as jnp
import ml_dtypes
import numpy as np
from jax import lax
from jax.experimental import pallas as pl
from jax.experimental.pallas import tpu as pltpu
from jax.sharding import PartitionSpec as P

CH = 256
FT = 512
CARRY = 8
f32, bf16 = jnp.float32, jnp.bfloat16
VMEM_LIMIT = 60 * 1024 * 1024
ANY = pl.BlockSpec(memory_space=pl.ANY)
SMEM = pl.BlockSpec(memory_space=pltpu.SMEM)
VM = pl.BlockSpec(memory_space=pltpu.VMEM)

GAIN, SHIFT, INB, TAP, SKIP, OUTB, DOWNB, UPB = 0, 2, 4, 7, 16, 18, 19, 20


def table():
    order = np.concatenate([np.arange(0, CH, 2), np.arange(1, CH, 2)])
    angle = np.pi * ((2 * order[:, None] + 1) * np.arange(CH)[None] % (4 * CH)) / (2 * CH)
    cos, sin = np.cos(angle), np.sin(angle)
    sign = np.where(order % 2 == 0, 1.0, -1.0)[:, None]
    spread = np.concatenate([cos, -sin], 0)
    turned = np.concatenate([sign * sin, sign * cos], 0)
    return jnp.asarray(np.concatenate([turned, spread], 1).astype(ml_dtypes.bfloat16))


def back_table(pair, at):
    return jnp.transpose(pair[:, at : at + CH].astype(f32) * (1.0 / CH)).astype(bf16)


def dot(x, y):
    return jnp.dot(x, y, preferred_element_type=f32)


def dot_nt(x, y):
    return lax.dot_general(x, y, (((1,), (1,)), ((), ())), preferred_element_type=f32)


def rows_at(index, size):
    return pl.ds(pl.multiple_of(index * size, size), size)


def for_rows(total, size, step, unroll=1):
    def run(i, carry):
        step(pl.multiple_of(i * size, size))
        return carry

    lax.fori_loop(0, total // size, run, 0, unroll=unroll)


def normalize(rows):
    average = jnp.mean(rows, axis=-1, keepdims=True)
    centered = rows - average
    scale = lax.rsqrt(jnp.mean(centered * centered, axis=-1, keepdims=True) + 1e-05)
    return centered * scale, scale


def norm_back(z, gain, unit, scale):
    w = z * gain
    return (
        w - jnp.mean(w, axis=-1, keepdims=True) - unit * jnp.mean(w * unit, axis=-1, keepdims=True)
    ) * scale


def gelu_pair(u):
    phi_sum = 0.5 + 0.5 * lax.erf(u * math.sqrt(0.5))
    bell = jnp.exp(-0.5 * (u * u))
    return u * phi_sum, phi_sum + u * (bell * (1.0 / math.sqrt(2.0 * math.pi)))


def mix_spectra(left, right, out, terms, conj):
    width = out.shape[1] // 2

    def tile(step, carry):
        r = pl.multiple_of(step * 16, 16)
        for half in range(2):
            cols = slice(half * width, (half + 1) * width)
            real = imag = None
            for i, j in terms:
                ar = left[i, pl.ds(r, 16), cols]
                ai = left[i, pl.ds(CH + r, 16), cols]
                br = right[j, pl.ds(r, 16), cols]
                bi = right[j, pl.ds(CH + r, 16), cols]
                if conj:
                    pr, pi = ar * br + ai * bi, ar * bi - ai * br
                else:
                    pr, pi = ar * br - ai * bi, ar * bi + ai * br
                real, imag = (pr, pi) if real is None else (real + pr, imag + pi)
            out[pl.ds(r, 16), cols] = real
            out[pl.ds(CH + r, 16), cols] = imag
        return carry

    lax.fori_loop(0, CH // 16, tile, 0, unroll=16)


def mix_units(left, right, out, terms, conj, plus):
    width = 256

    def unit(r, cols):
        real = imag = None
        if plus:
            real, imag = out[r : r + 16, cols], out[CH + r : CH + r + 16, cols]
        for i, j in terms:
            ar, ai = left[i, r : r + 16, cols], left[i, CH + r : CH + r + 16, cols]
            br, bi = right[j, r : r + 16, cols], right[j, CH + r : CH + r + 16, cols]
            if conj:
                pr, pi = ar * br + ai * bi, ar * bi - ai * br
            else:
                pr, pi = ar * br - ai * bi, ar * bi + ai * br
            real, imag = (pr, pi) if real is None else (real + pr, imag + pi)
        out[r : r + 16, cols] = real
        out[CH + r : CH + r + 16, cols] = imag

    return [
        functools.partial(unit, r, slice(c, c + width)) for c in range(0, out.shape[1], width) for r in range(0, CH, 16)
    ]


def run_skewed(stages, parts):
    for step in range(len(stages) + parts - 1):
        for p in range(parts):
            if 0 <= step - p < len(stages):
                stages[step - p](p)


def run_beside(steps, units):
    done = 0
    for k, step in enumerate(steps):
        step()
        upto = len(units) * (k + 1) // len(steps)
        for unit in units[done:upto]:
            unit()
        done = upto


def fold_rows(x):
    return jnp.sum(x.reshape(x.shape[0] // 8, 8, x.shape[1]), axis=0)


def pieces_of(at, wide, D):
    spans, off = [], 0
    while off < wide:
        row, col = (at + off) // D, (at + off) % D
        size = min(D - col, wide - off)
        spans.append((row, col, off, size))
        off += size
    return spans


def pass_kernel(
    sections, pieces, gains, shifts, inb_p, taps_p, skips, outb_p, downb_p, upb_p, tokens, cots, filt, win, wout, wup, wdown, pair_h,
    stream, gtok, aS, ybS, nS, eS, s1S, s2S, gdS, guS, goS, gpS, g1S, g2S, smallO,
    inf, inb, winb, woutb, wupb, wdownb, back, pair, k1, k2, sp1, sp2, pall, y1all, mall, dall,
    ab, lead, leadlow, part1, part2, wide, gate2, mid, nb, tile2, hid, outb, outfb, gnb, gqb, gpb, small,
    par, wsem, osem, fsem, bsem, ssem, gsem,
):
    rank = lax.axis_index("section")
    first, final = rank == 0, rank == sections - 1
    D, FF = woutb.shape[0], wupb.shape[1]
    tiles = FF // FT
    T = pieces * CH
    share = T // sections
    sub = min(CH, share)
    at = lambda r: {"section": r}

    def when(condition):
        return pl.when(condition)

    def remote(src, dst, send, recv, r):
        return pltpu.make_async_remote_copy(
            src_ref=src, dst_ref=dst, send_sem=send, recv_sem=recv, device_id=at(r), device_id_type=pl.DeviceIdType.MESH
        )

    def local(src, dst, sem):
        return pltpu.make_async_copy(src, dst, sem)

    loads = [
        local(win, winb, wsem.at[0]),
        local(wout, woutb, wsem.at[1]),
        local(wup, wupb, wsem.at[2]),
        local(wdown, wdownb, wsem.at[3]),
        local(pair_h, pair, wsem.at[4]),
    ]
    fill = [local(filt.at[f, pl.ds(0, CH)], sp.at[0, pl.ds(CH, CH)], wsem.at[7 + f]) for f, sp in enumerate((sp1, sp2))]
    for seg in range(1, pieces):
        window = pl.ds((seg - 1) * CH, 2 * CH)
        fill += [local(filt.at[f, window], sp.at[seg], wsem.at[7 + 2 * seg + f]) for f, sp in enumerate((sp1, sp2))]

    def own_chunk(src, dst, seg, sems):
        return local(src.at[rows_at(seg, CH)], dst.at[seg], sems.at[1, seg])

    def relay(src, dst, seg, sems, r):
        return remote(src, dst.at[seg], sems.at[0, seg], sems.at[1, seg], r)

    @when(first)
    def _():
        own_chunk(tokens, inf, 0, fsem).start()

    loads[4].start()
    for copy in fill[:2]:
        copy.start()
    loads[0].start()

    @when(first)
    def _():
        for seg in range(1, pieces):
            own_chunk(tokens, inf, seg, fsem).start()

    for copy in loads[1:4] + fill[2:]:
        copy.start()

    @when(final)
    def _():
        for seg in range(pieces):
            own_chunk(cots, inb, seg, bsem).start()

    for row, given in ((GAIN, gains), (SHIFT, shifts), (INB, inb_p), (SKIP, skips), (OUTB, outb_p), (DOWNB, downb_p)):
        par[row : row + given.shape[0], :] = given[...].astype(f32)
    for tap in range(3):
        par[TAP + 3 * tap : TAP + 3 * tap + 3, :] = taps_p[tap].astype(f32)
    for k in range(FF // D):
        par[UPB + k : UPB + k + 1, :] = upb_p[:, k * D : (k + 1) * D].astype(f32)

    barrier = pltpu.get_barrier_semaphore()
    for r in range(sections):

        @when(rank != r)
        def _(r=r):
            pl.semaphore_signal(barrier, inc=1, device_id=at(r), device_id_type=pl.DeviceIdType.MESH)

    if sections > 1:
        pl.semaphore_wait(barrier, sections - 1)

    pall[pl.ds(0, 16), :] = jnp.zeros((16, 3 * D), bf16)
    for sp in (sp1, sp2):
        sp[0, pl.ds(0, CH), :] = jnp.zeros((CH, D), bf16)
    small[...] = jnp.zeros(small.shape, f32)
    gqb[pl.ds(CH, CARRY), :] = jnp.zeros((CARRY, 3 * D), f32)

    def filter_spectra(seg):
        k1[seg] = dot(pair[...], sp1[seg]).astype(bf16)
        k2[seg] = dot(pair[...], sp2[seg]).astype(bf16)

    loads[4].wait()
    back[...] = back_table(pair, CH)
    for copy in fill[:2]:
        copy.wait()
    filter_spectra(0)

    @when(jnp.logical_not(first))
    def _():
        for copy in fill[2:]:
            copy.wait()

        def run(seg, carry):
            filter_spectra(seg)
            return carry

        lax.fori_loop(1, pieces, run, 0)

    def out_parts(seg, src, dst, sems, to_self):
        found = []
        for j in range(CH // sub):
            row = seg * CH + j * sub
            r, off = row // share, row % share
            found.append((r, off, j * sub, src.at[pl.ds(j * sub, sub)], sems.at[0, seg * (CH // sub) + j], off // sub))
        return found

    def put(src, dst, k):
        return local(src, dst, osem.at[k])

    def tile_steps(into, act, out):
        def begin(k):
            tile2[k % 2] = into(k)

        steps = [functools.partial(begin, 0)]
        for k in range(tiles):
            if k + 1 < tiles:
                steps.append(functools.partial(begin, k + 1))
            steps.append(functools.partial(act, k))
            if k >= 1:
                steps.append(functools.partial(out, k - 1))
        return steps + [functools.partial(out, tiles - 1)]

    def conv_stages(seg, sp, k, part, after, conj):
        per = CH // 16
        units = mix_units(k, sp, part, [(0, seg)], conj, True)

        def to(p):
            cols = slice(256 * p, 256 * p + 256)
            sp[seg, :, cols] = dot(pair[:, CH:], leadlow[:, cols]).astype(bf16)

        def mix(p):
            for unit in units[per * p : per * (p + 1)]:
                unit()

        def back_to(p):
            cols = slice(256 * p, 256 * p + 256)
            after(cols, dot(back[...], part[:, cols]))

        return [to, mix, back_to]

    def clear_parts():
        part1[...] = jnp.zeros(part1.shape, bf16)
        part2[...] = jnp.zeros(part2.shape, bf16)

    def forward_chunk(seg, carry):
        here = rows_at(seg, CH)
        base = pl.multiple_of(seg * CH, CH)
        hb = inf.at[seg]
        slot = 0
        later = seg > 0

        def before(copy):
            @when(later)
            def _():
                copy.wait()

        puts = [
            put(ab, aS.at[here], 0), put(sp1.at[seg], s1S.at[seg], 1), put(sp2.at[seg], s2S.at[seg], 2),
            put(leadlow, ybS.at[here], 3), put(nb, nS.at[here], 4), put(hid, eS.at[here], 5),
        ]

        @when(first)
        def _():
            own_chunk(tokens, inf, seg, fsem).wait()

        @when(jnp.logical_not(first))
        def _():
            relay(outb.at[slot], inf, seg, fsem, rank).wait_recv()

        before(puts[0])

        def ln1(r):
            unit, _ = normalize(hb[pl.ds(r, 32), :].astype(f32))
            ab[pl.ds(r, 32), :] = (unit * par[GAIN : GAIN + 1, :] + par[SHIFT : SHIFT + 1, :]).astype(bf16)

        for_rows(CH, 32, ln1, 8)
        puts[0].start()

        @when(seg == 0)
        def _():
            loads[0].wait()

        for b in range(3):
            cols = slice(b * D, (b + 1) * D)
            value = dot(ab[...], winb[:, cols]) + par[INB + b : INB + b + 1, :]
            pall[pl.ds(pl.multiple_of(base + 16, 16), CH), cols] = value.astype(bf16)

        before(puts[3])

        def short(r):
            got = [branch(base + r, b)[0] for b in range(3)]
            gate2[pl.ds(r, 32), :] = got[2]
            s = got[0] * got[1]
            lead[pl.ds(r, 32), :] = s
            leadlow[pl.ds(r, 32), :] = s.astype(bf16)

        ahead = first & (seg < pieces - 1)

        @when(ahead)
        def _():
            @when(seg == 0)
            def _():
                for copy in fill[2:]:
                    copy.wait()

            for_rows(CH, 32, short, 8)
            filter_spectra(seg + 1)

        @when(jnp.logical_not(ahead))
        def _():
            for_rows(CH, 32, short, 8)

        def second(cols, value):
            y = value + par[SKIP : SKIP + 1, cols] * lead[:, cols]
            y1all[seg, :, cols] = y.astype(bf16)
            trail = y * gate2[:, cols]
            lead[:, cols] = trail
            leadlow[:, cols] = trail.astype(bf16)

        def third(cols, value):
            leadlow[:, cols] = (value + par[SKIP + 1 : SKIP + 2, cols] * lead[:, cols]).astype(bf16)

        run_skewed(conv_stages(seg, sp1, k1, part1, second, False) + conv_stages(seg, sp2, k2, part2, third, False), D // 256)
        puts[1].start()
        puts[2].start()
        puts[3].start()

        @when(seg == 0)
        def _():
            loads[1].wait()

        wide[...] = dot(leadlow[...], woutb[...])
        before(puts[4])

        def ln2(r):
            rows = pl.ds(r, 32)
            m = hb[rows, :].astype(f32) + (wide[rows, :] + par[OUTB : OUTB + 1, :])
            mall[seg, rows, :] = m.astype(bf16)
            unit, _ = normalize(m)
            nb[rows, :] = (unit * par[GAIN + 1 : GAIN + 2, :] + par[SHIFT + 1 : SHIFT + 2, :]).astype(bf16)
            mid[rows, :] = m + par[DOWNB : DOWNB + 1, :]

        for_rows(CH, 32, ln2, 8)
        puts[4].start()

        @when(seg == 0)
        def _():
            loads[2].wait()
            loads[3].wait()

        before(puts[5])

        def up(k):
            return dot(nb[...], wupb[:, k * FT : (k + 1) * FT])

        def act(k):
            spans = pieces_of(k * FT, FT, D)
            bias = [par[UPB + row : UPB + row + 1, col : col + size] for row, col, _, size in spans]
            bias = bias[0] if len(bias) == 1 else jnp.concatenate(bias, axis=1)
            e, d = gelu_pair(tile2[k % 2] + bias)
            hid[:, k * FT : (k + 1) * FT] = e.astype(bf16)
            dall[seg, :, k * FT : (k + 1) * FT] = d.astype(bf16)

        def down(k):
            mid[...] += dot(hid[:, k * FT : (k + 1) * FT], wdownb[k * FT : (k + 1) * FT, :])

        for s in range(pieces):

            @when(seg == s)
            def _(s=s):
                terms = [(s + 1 - j, j) for j in range(s + 1)]
                units = []
                if s + 1 < pieces:
                    units = mix_units(k1, sp1, part1, terms, False, False) + mix_units(k2, sp2, part2, terms, False, False)
                run_beside(tile_steps(up, act, down), units)

        puts[5].start()

        @when(later)
        def _():
            finish_out(seg - 1, slot)

        outb[slot] = mid[...].astype(bf16)

        @when(jnp.logical_not(final))
        def _():
            relay(outb.at[slot], inf, seg, fsem, rank + 1).start()

        @when(final)
        def _():
            for r, off, inner, src, sem, k in out_parts(seg, outb.at[slot], stream, ssem, None):

                @when(r != rank)
                def _():
                    remote(src, stream.at[pl.ds(pl.multiple_of(off, sub), sub)], sem, ssem.at[1, k], r).start()

                @when(r == rank)
                def _():
                    local(src, stream.at[pl.ds(pl.multiple_of(off, sub), sub)], sem).start()

        return carry

    def finish_out(seg, slot):
        @when(jnp.logical_not(final))
        def _():
            relay(outb.at[slot], inf, seg, fsem, rank + 1).wait_send()

        @when(final)
        def _():
            for r, off, inner, src, sem, k in out_parts(seg, outb.at[slot], stream, ssem, None):

                @when(r != rank)
                def _():
                    remote(src, stream.at[pl.ds(pl.multiple_of(off, sub), sub)], sem, ssem.at[1, k], r).wait_send()

                @when(r == rank)
                def _():
                    local(src, stream.at[pl.ds(pl.multiple_of(off, sub), sub)], sem).wait()

    def branch(start, b):
        rows = pall[pl.ds(pl.multiple_of(start, 16), 48), b * D : (b + 1) * D].astype(f32)
        late = [rows[16 - i : 48 - i] for i in range(3)]
        t = [par[TAP + 3 * i + b : TAP + 3 * i + b + 1, :] for i in range(3)]
        return t[0] * late[0] + t[1] * late[1] + t[2] * late[2], late

    clear_parts()
    lax.fori_loop(0, pieces, forward_chunk, 0)
    last = pieces - 1
    here = rows_at(last, CH)
    for copy in (
        put(ab, aS.at[here], 0), put(sp1.at[last], s1S.at[last], 1), put(sp2.at[last], s2S.at[last], 2),
        put(leadlow, ybS.at[here], 3), put(nb, nS.at[here], 4), put(hid, eS.at[here], 5),
    ):
        copy.wait()
    for k in range(last):
        put(sp1.at[k], s1S.at[k], 1).wait()
        put(sp2.at[k], s2S.at[k], 2).wait()
    finish_out(last, 0)

    def add_small(k, x, cols=slice(None)):
        small[k, :, cols] += fold_rows(x)

    def backward_chunk(i, carry):
        seg = pieces - 1 - i
        here = rows_at(seg, CH)
        base = pl.multiple_of(seg * CH, CH)
        gdb, hb = inb.at[seg], inf.at[seg]
        slot = 0

        def before(copy):
            @when(i > 0)
            def _():
                copy.wait()

        puts = [
            put(gdb, gdS.at[here], 6), put(hid, guS.at[here], 7), put(nb, goS.at[here], 8), put(gpb, gpS.at[here], 9),
            put(sp2.at[seg], g2S.at[seg], 10), put(sp1.at[seg], g1S.at[seg], 11),
        ]

        @when(final)
        def _():
            own_chunk(cots, inb, seg, bsem).wait()

        @when(jnp.logical_not(final))
        def _():
            relay(outb.at[slot], inb, seg, bsem, rank).wait_recv()

        before(puts[0])
        puts[0].start()
        before(puts[1])

        def down(k):
            return dot_nt(gdb[...], wdownb[k * FT : (k + 1) * FT, :])

        def act(k):
            cols = slice(k * FT, (k + 1) * FT)
            gu = (dall[seg, :, cols].astype(f32) * tile2[k % 2]).astype(bf16)
            hid[:, cols] = gu
            total = fold_rows(gu.astype(f32))
            for row, col, off, size in pieces_of(k * FT, FT, D):
                small[UPB + row, :, col : col + size] += total[:, off : off + size]

        def up(k):
            part = dot_nt(hid[:, k * FT : (k + 1) * FT], wupb[:, k * FT : (k + 1) * FT])
            if k == 0:
                gnb[...] = part
            else:
                gnb[...] += part

        for s in range(pieces):

            @when(seg == s)
            def _(s=s):
                terms = [(j - s, j) for j in range(s + 1, pieces)]
                units = []
                if terms:
                    units = mix_units(k2, sp2, part2, terms, True, False) + mix_units(k1, sp1, part1, terms, True, False)
                run_beside(tile_steps(down, act, up), units)

        puts[1].start()
        before(puts[2])

        def ln2(r):
            rows = pl.ds(r, 32)
            unit, scale = normalize(mall[seg, rows, :].astype(f32))
            z = gnb[rows, :]
            gd = gdb[rows, :].astype(f32)
            gm = gd + norm_back(z, par[GAIN + 1 : GAIN + 2, :], unit, scale)
            mid[rows, :] = gm
            go = gm.astype(bf16)
            nb[rows, :] = go
            add_small(GAIN + 1, z * unit)
            add_small(SHIFT + 1, z)
            add_small(OUTB, go.astype(f32))
            add_small(DOWNB, gd)

        for_rows(CH, 32, ln2, 8)
        puts[2].start()
        gy = dot_nt(nb[...], woutb[...])
        lead[...] = gy
        leadlow[...] = gy.astype(bf16)
        sp2[seg] = dot(pair[:, CH:], leadlow[...]).astype(bf16)
        puts[4].start()
        for unit in mix_units(k2, sp2, part2, [(0, seg)], True, True):
            unit()
        wide[...] = dot(back[...], part2[...])

        def keep(r, b, grad, late):
            gqb[pl.ds(r, 32), b * D : (b + 1) * D] = grad
            for tap in range(3):
                add_small(TAP + 3 * tap + b, grad * late[tap])

        def second(r):
            rows = pl.ds(r, 32)
            gate, late = branch(base + r, 2)
            y1 = y1all[seg, rows, :].astype(f32)
            gy2 = lead[rows, :]
            gs2 = wide[rows, :] + par[SKIP + 1 : SKIP + 2, :] * gy2
            gy1 = gs2 * gate
            gate2[rows, :] = gy1
            leadlow[rows, :] = gy1.astype(bf16)
            add_small(SKIP + 1, gy2 * (y1 * gate))
            keep(r, 2, gs2 * y1, late)

        for_rows(CH, 32, second, 8)
        sp1[seg] = dot(pair[:, CH:], leadlow[...]).astype(bf16)
        puts[5].start()
        for unit in mix_units(k1, sp1, part1, [(0, seg)], True, True):
            unit()
        wide[...] = dot(back[...], part1[...])

        def lower(r):
            rows = pl.ds(r, 32)
            carrier, late_carrier = branch(base + r, 0)
            gate, late_gate = branch(base + r, 1)
            gy1 = gate2[rows, :]
            gs1 = wide[rows, :] + par[SKIP : SKIP + 1, :] * gy1
            add_small(SKIP, gy1 * (carrier * gate))
            keep(r, 0, gs1 * gate, late_carrier)
            keep(r, 1, gs1 * carrier, late_gate)

        for_rows(CH, 32, lower, 8)
        before(puts[3])

        def short(r):
            for b in range(3):
                cols = slice(b * D, (b + 1) * D)
                rows = gqb[pl.ds(r, 32 + CARRY), cols]
                t = [par[TAP + 3 * tap + b : TAP + 3 * tap + b + 1, :] for tap in range(3)]
                gp = (t[0] * rows[:32] + t[1] * rows[1:33] + t[2] * rows[2:34]).astype(bf16)
                gpb[pl.ds(r, 32), cols] = gp
                add_small(INB + b, gp.astype(f32))

        for_rows(CH, 32, short, 8)
        puts[3].start()
        gqb[pl.ds(CH, CARRY), :] = gqb[pl.ds(0, CARRY), :]
        gnb[...] = dot_nt(gpb[...], winb[...])

        @when(i > 0)
        def _():
            finish_grad(i - 1, slot)

        def ln1(r):
            rows = pl.ds(r, 32)
            unit, scale = normalize(hb[rows, :].astype(f32))
            z = gnb[rows, :]
            gh = mid[rows, :] + norm_back(z, par[GAIN : GAIN + 1, :], unit, scale)
            outfb[slot, rows, :] = gh
            outb[slot, rows, :] = gh.astype(bf16)
            add_small(GAIN, z * unit)
            add_small(SHIFT, z)

        for_rows(CH, 32, ln1, 8)

        @when(jnp.logical_not(first))
        def _():
            relay(outb.at[slot], inb, seg, bsem, rank - 1).start()

        @when(first)
        def _():
            for r, off, inner, src, sem, k in out_parts(seg, outb.at[slot], gtok, gsem, None):
                whole = outfb.at[slot, pl.ds(inner, sub)]

                @when(r != rank)
                def _():
                    remote(src, inf.at[seg, pl.ds(inner, sub)], sem, gsem.at[1, k], r).start()

                @when(r == rank)
                def _():
                    local(whole, gtok.at[pl.ds(pl.multiple_of(off, sub), sub)], sem).start()

        return carry

    def finish_grad(i, slot):
        seg = pieces - 1 - i

        @when(jnp.logical_not(first))
        def _():
            relay(outb.at[slot], inb, seg, bsem, rank - 1).wait_send()

        @when(first)
        def _():
            for r, off, inner, src, sem, k in out_parts(seg, outb.at[slot], gtok, gsem, None):
                whole = outfb.at[slot, pl.ds(inner, sub)]

                @when(r != rank)
                def _():
                    remote(src, inf.at[seg, pl.ds(inner, sub)], sem, gsem.at[1, k], r).wait_send()

                @when(r == rank)
                def _():
                    local(whole, gtok.at[pl.ds(pl.multiple_of(off, sub), sub)], sem).wait()

    clear_parts()
    lax.fori_loop(0, pieces, backward_chunk, 0)
    here = rows_at(0, CH)
    ends = [
        put(inb.at[0], gdS.at[here], 6), put(hid, guS.at[here], 7), put(nb, goS.at[here], 8), put(gpb, gpS.at[here], 9),
        put(sp2.at[0], g2S.at[0], 10), put(sp1.at[0], g1S.at[0], 11),
    ]
    for copy in ends:
        copy.wait()
    for k in range(last):
        ends[4].wait()
        ends[5].wait()
    total = put(small, smallO, 12)
    total.start()
    finish_grad(last, 0)
    parts = share // sub

    @when(jnp.logical_not(final))
    def _():
        for k in range(parts):
            remote(outb.at[0, pl.ds(0, sub)], stream.at[pl.ds(k * sub, sub)], ssem.at[0, 0], ssem.at[1, k], rank).wait_recv()

    @when(jnp.logical_not(first))
    def _():
        for k in range(parts):
            row = rank * share + k * sub
            landed = inf.at[row // CH, pl.ds(pl.multiple_of(row % CH, sub), sub)]
            remote(outb.at[0, pl.ds(0, sub)], landed, gsem.at[0, 0], gsem.at[1, k], rank).wait_recv()
            outfb[0, pl.ds(0, sub), :] = landed[...].astype(f32)
            copy = local(outfb.at[0, pl.ds(0, sub)], gtok.at[pl.ds(k * sub, sub)], gsem.at[0, k])
            copy.start()
            copy.wait()

    total.wait()


def pass_call(params, tokens, cots, filt, win, wout, wup, wdown, pair, sections):
    T, D = tokens.shape
    FF = wup.shape[1]
    pieces = T // CH
    share = T // sections
    sub = min(CH, share)
    spec3 = (pieces, 2 * CH, D)
    small = (UPB + FF // D, 8, D)
    shapes = [
        ((share, D), bf16), ((share, D), f32),
        ((T, D), bf16), ((T, D), bf16), ((T, D), bf16), ((T, FF), bf16), (spec3, bf16), (spec3, bf16),
        ((T, D), bf16), ((T, FF), bf16), ((T, D), bf16), ((T, 3 * D), bf16), (spec3, bf16), (spec3, bf16),
        (small, f32),
    ]
    V, S = pltpu.VMEM, pltpu.SemaphoreType.DMA
    chunk, chunks = (CH, D), (pieces, CH, D)
    scratch = [
        V(chunks, bf16), V(chunks, bf16),
        V(win.shape, bf16), V(wout.shape, bf16), V(wup.shape, bf16), V(wdown.shape, bf16),
        V((CH, 2 * CH), bf16), V((2 * CH, 2 * CH), bf16),
        V(spec3, bf16), V(spec3, bf16), V(spec3, bf16), V(spec3, bf16),
        V((16 + T, 3 * D), bf16), V(chunks, bf16), V(chunks, bf16), V((pieces, CH, FF), bf16),
        V(chunk, bf16), V(chunk, f32), V(chunk, bf16), V((2 * CH, D), bf16), V((2 * CH, D), bf16), V(chunk, f32), V(chunk, f32),
        V(chunk, f32),
        V(chunk, bf16), V((2, CH, FT), f32), V((CH, FF), bf16), V((1,) + chunk, bf16), V((1,) + chunk, f32),
        V(chunk, f32), V((CH + CARRY, 3 * D), f32), V((CH, 3 * D), bf16), V(small, f32), V((UPB + FF // D, D), f32),
        S((7 + 2 * pieces,)), S((13,)), S((2, pieces)), S((2, pieces)), S((2, T // sub)), S((2, T // sub)),
    ]
    return pl.pallas_call(
        functools.partial(pass_kernel, sections, pieces),
        out_shape=[jax.ShapeDtypeStruct(*s) for s in shapes],
        in_specs=[VM] * 8 + [ANY] * 8,
        out_specs=[ANY] * len(shapes),
        scratch_shapes=scratch,
        compiler_params=pltpu.CompilerParams(vmem_limit_bytes=63 * 1024 * 1024, collective_id=1, has_side_effects=True),
        name="layer_pass",
    )(*params, tokens, cots, filt, win, wout, wup, wdown, pair)


def filter_kernel(pieces, s, g, back, turned, out, q):
    for d in range(pieces):
        mix_spectra(s, g, q.at[d], [(j - d, j) for j in range(d, pieces)], True)
    for d in range(pieces):
        rows = dot(back[...], q[d])
        if d + 1 < pieces:
            rows += dot(turned[...], q[d + 1])
        out[pl.ds(d * CH, CH), :] = rows.astype(bf16)


def filter_call(s, g, pair):
    pieces, _, D = s.shape
    turned, back = ((pair[:, k : k + CH].astype(f32) / CH).astype(bf16).T for k in (0, CH))
    return pl.pallas_call(
        functools.partial(filter_kernel, pieces),
        out_shape=jax.ShapeDtypeStruct((pieces * CH, D), bf16),
        in_specs=[VM] * 4,
        out_specs=VM,
        scratch_shapes=[pltpu.VMEM(s.shape, bf16)],
        compiler_params=pltpu.CompilerParams(vmem_limit_bytes=VMEM_LIMIT),
        name="filter_grad",
    )(s, g, back, turned)


def exchange_plan(groups, D):
    blocks = [("product", 0, g) for g in range(groups)] + [("filter", 0, 0)]
    blocks += [("product", 1, g) for g in range(groups)] + [("filter", 1, 0)]
    blocks += [("product", 2, g) for g in range(groups)]
    half = D // 2
    sent, flows = [], []
    for b in range(len(blocks)):
        spans = [(0, [(0, half, False)]), (half, [(half, half - 128, False), (D - 128, 128, True)])]
        if b == len(blocks) - 1:
            spans = [spans[1], (0, [(0, half - 128, False)]), (half - 128, [(half - 128, 128, False)])]
        for low, parts in spans:
            wide = sum(part[1] for part in parts)
            sent.append((b, low, wide, list(range(len(flows), len(flows) + len(parts)))))
            flows += [(b,) + part for part in parts]
    return blocks, sent, flows


def exchange_kernel(
    pieces, small_in, pair_h, gdS, eS, nS, guS, ybS, goS, aS, gpS, s1S, g1S, s2S, g2S,
    downT, upO, outO, inO, filtO, smallO,
    x, r1, r2, rr, rl, rrz, rlz, r2z, gb, lb, lt, sb, qb, pair, back, turned, ob, mine, got,
    lsem, osem, csem, ysem, rsem, fsem, msem,
):
    D = lb.shape[2]
    half = D // 2
    me = lax.axis_index("dp")
    c, y, z = me % 2, (me // 2) % 2, me // 4
    Z = r2.shape[1]
    groups = lt.shape[2]
    blocks, sent, flows = exchange_plan(groups, D)
    at = lambda i: {"dp": i}
    core_id, y_id = me + 1 - 2 * c, me + 2 - 4 * y
    mates = (core_id, y_id, me + 4 - 8 * (z % 2), me + 8 - 16 * (z // 2))
    inner = (z == 1) | (z == 2)

    def remote(src, dst, send, recv, mate):
        return pltpu.make_async_remote_copy(
            src_ref=src, dst_ref=dst, send_sem=send, recv_sem=recv, device_id=at(mate),
            device_id_type=pl.DeviceIdType.MESH,
        )

    def load(src, dst, k):
        return pltpu.make_async_copy(src, dst, lsem.at[k])

    rights = ((eS,), (guS,), (goS, gpS))
    lefts = ((gdS,), (nS,), (ybS, aS))
    turned_at = ((0,), (1,), (0, 2))

    def right_loads(m):
        found, off = [], 0
        for k, src in enumerate(rights[m]):
            wide = src.shape[1]
            found.append(load(src, gb.at[m % 2, :, pl.ds(off, wide)], 4 * m + k))
            off += wide
        return found

    def left_loads(m):
        return [load(src, lb.at[k], 4 * m + 2 + k) for k, src in enumerate(lefts[m])]

    def spectra(f):
        src = ((s1S, g1S), (s2S, g2S))[f]
        return [load(src[k], sb.at[k], 12 + 2 * f + k) for k in range(2)]

    def turn(m):
        for k, spot in enumerate(turned_at[m]):

            def part(i, carry, k=k, spot=spot):
                rows = pl.multiple_of(i * 128, 128)
                piece = jnp.transpose(lb[k, pl.ds(rows, 128), :])
                lt[spot, :, :, :, pl.ds(rows, 128)] = piece.reshape(lt.shape[1:4] + (128,))
                return carry

            lax.fori_loop(0, lb.shape[1] // 128, part, 0)

    def product(m, g, low, wide, slot):
        def part(i, carry):
            k = jnp.where(i == 0, 0, 2) if m == 2 else m
            left = lt[k, :, g].reshape(16 * lt.shape[1], lt.shape[4])
            cols = pl.ds(pl.multiple_of(i * D + low, 128), wide)
            value = dot(left, gb[m % 2, :, cols]).astype(bf16)
            x[slot, :, :, :, pl.ds(pl.multiple_of(i * 16, 16), 16), :wide] = value.reshape(x.shape[1:4] + (16, wide))
            return carry

        lax.fori_loop(0, 4, part, 0)

    def mix(d):
        mix_spectra(sb.at[0], sb.at[1], qb.at[d], [(j - d, j) for j in range(d, pieces)], True)

    def filters(low, slot):
        cols = slice(low, low + half)

        def part(d, carry):
            rows = dot(back[...], qb[d, :, cols]) + dot(turned[...], qb[d + 1, :, cols])
            x[slot, d] = rows.astype(bf16).reshape(x.shape[2:])
            return carry

        lax.fori_loop(0, pieces, part, 0)

    def core_copy(i):
        b, low, wide, _ = sent[i]
        return remote(
            x.at[i % x.shape[0], :, :, 1 - c, :, pl.ds(0, wide)], r1.at[b, :, :, :, pl.ds(low, wide)],
            csem.at[0, i], csem.at[1, i], core_id,
        )

    def add(p, q):
        return (p.astype(f32) + q.astype(f32)).astype(bf16)

    def after_core(i):
        b, low, wide, mine_flows = sent[i]
        core_copy(i).wait()
        cols = slice(low, low + wide)

        def part(k, carry):
            for j in range(2):
                r1[b, k, j, :, cols] = add(r1[b, k, j, :, cols], x[i % x.shape[0], k, j, c, :, :wide])
            return carry

        lax.fori_loop(0, Z, part, 0)
        for u in mine_flows:
            if not flows[u][3]:
                y_copy(u).start()

    def y_copy(u):
        b, low, wide, z_first = flows[u]
        cols = pl.ds(low, wide)
        if z_first:
            return remote(r1.at[b, z, 1 - y, :, cols], r2z.at[b], ysem.at[0, u], ysem.at[1, u], y_id)
        return remote(r1.at[b, :, 1 - y, :, cols], r2.at[b, :, :, cols], ysem.at[0, u], ysem.at[1, u], y_id)

    def after_y(u):
        b, low, wide, _ = flows[u]
        cols = slice(low, low + wide)
        y_copy(u).wait()

        def part(k, carry):
            r2[b, k, :, cols] = add(r2[b, k, :, cols], r1[b, k, y, :, cols])
            return carry

        lax.fori_loop(0, Z, part, 0)

    def own(u, d):
        b, low, wide, z_first = flows[u]
        cols = pl.ds(low, wide)
        return r1.at[b, d, :, :, cols] if z_first else r2.at[b, d, :, cols]

    def right_at(u, d):
        b, low, wide, z_first = flows[u]
        return rrz.at[b, d - 1] if z_first else rr.at[b, d - 1, :, pl.ds(low, wide)]

    def left_at(u, d):
        b, low, wide, z_first = flows[u]
        return rlz.at[b, d] if z_first else rl.at[b, d, :, pl.ds(low, wide)]

    def right_copy(u, d, src):
        return remote(src, right_at(u, d), rsem.at[0, u, d - 1], rsem.at[1, u, d - 1], me + 4)

    def left_copy(u, d, src):
        return remote(src, left_at(u, d), fsem.at[0, u, d], fsem.at[1, u, d], me - 4)

    def hop(u, h):
        @pl.when(z == h)
        def _():
            for d in range(Z - 1, h, -1):
                src = own(u, d)
                if h > 0:
                    right_copy(u, d, src).wait_recv()
                    src = right_at(u, d)
                    src[...] = add(src[...], own(u, d)[...])
                right_copy(u, d, src).start()

        @pl.when(z == Z - 1 - h)
        def _():
            for d in range(Z - 1 - h):
                src = own(u, d)
                if h > 0:
                    left_copy(u, d, src).wait_recv()
                    src = left_at(u, d)
                    src[...] = add(src[...], own(u, d)[...])
                left_copy(u, d, src).start()

    def gather(u, store):
        for p in range(Z):

            @pl.when(z == p)
            def _(p=p):
                total = own(u, p)[...].astype(f32)
                if p > 0:
                    right_copy(u, p, own(u, p)).wait_recv()
                    total += right_at(u, p)[...].astype(f32)
                if p < Z - 1:
                    left_copy(u, p, own(u, p)).wait_recv()
                    total += left_at(u, p)[...].astype(f32)
                for d in range(p + 1, Z):
                    right_copy(u, d, own(u, d)).wait_send()
                for d in range(p):
                    left_copy(u, d, own(u, d)).wait_send()
                store(p, total)

    def turn_to_y(u):
        def store(p, total):
            own(u, p)[...] = total.astype(bf16)

        gather(u, store)
        y_copy(u).start()

    def out_copies(i):
        b, low, wide, _ = sent[i]
        kind, a, g = blocks[b]
        slot = i % 2
        if kind == "filter":
            src = ob.at[slot, :, pl.ds(0, wide)]
            return [pltpu.make_async_copy(src, filtO.at[a, :, pl.ds(low, wide)], osem.at[4 * slot])]
        found = []
        rows = pl.ds(g * 16, 16)
        for k in range(4):
            if a < 2:
                dst = (downT, upO)[a].at[rows, pl.ds(k * D + low, wide)]
            elif k == 0:
                dst = outO.at[rows, pl.ds(low, wide)]
            else:
                dst = inO.at[rows, pl.ds((k - 1) * D + low, wide)]
            src = ob.at[slot, pl.ds(16 * k, 16), pl.ds(0, wide)]
            found.append(pltpu.make_async_copy(src, dst, osem.at[4 * slot + k]))
        return found

    def finish(i):
        b, low, _, mine_flows = sent[i]
        slot = i % 2
        if i >= 2:
            for copy in out_copies(i - 2):
                copy.wait()
        for u in mine_flows:
            _, first, wide, z_first = flows[u]
            cols = slice(first - low, first - low + wide)
            if z_first:
                y_copy(u).wait()
                ob[slot, :, cols] = r1[b, z, y, :, first : first + wide].astype(f32) + r2z[b].astype(f32)
            else:

                def store(p, total, cols=cols):
                    ob[slot, :, cols] = total

                gather(u, store)
        for copy in out_copies(i):
            copy.start()

    def mini_copy(k):
        return remote(mine.at[k], got.at[k], msem.at[0, k], msem.at[1, k], mates[k])

    tables_in = [load(pair_h, pair, 16)]
    early = [
        [load(eS.at[:, pl.ds(k * D + low, half)], gb.at[0, :, pl.ds(k * D + low, half)], 18 + 4 * (low > 0) + k) for k in range(4)]
        for low in (0, half)
    ]
    for copy in left_loads(0) + early[0] + early[1]:
        copy.start()
    barrier = pltpu.get_barrier_semaphore()
    for mate in mates:
        pl.semaphore_signal(barrier, inc=1, device_id=at(mate), device_id_type=pl.DeviceIdType.MESH)

    @pl.when(inner)
    def _():
        other = me + 12 - 8 * z
        pl.semaphore_signal(barrier, inc=1, device_id=at(other), device_id_type=pl.DeviceIdType.MESH)

    @pl.when(inner)
    def _():
        pl.semaphore_wait(barrier, len(mates) + 1)

    @pl.when(jnp.logical_not(inner))
    def _():
        pl.semaphore_wait(barrier, len(mates))

    mine[0] = jnp.sum(small_in[...], axis=1)
    qb[pieces] = jnp.zeros(qb.shape[1:], bf16)

    def compute(i):
        b, low, wide, _ = sent[i]
        kind, a, g = blocks[b]
        slot = i % x.shape[0]
        if kind == "product":
            if g == 0 and low == 0:
                if a == 0:
                    for copy in left_loads(0):
                        copy.wait()
                    turn(0)
                for copy in early[0] if a == 0 else right_loads(a):
                    copy.wait()
                if a == 1:
                    for copy in left_loads(a + 1) + right_loads(a + 1):
                        copy.start()
            if a == 0 and g == 0 and low > 0:
                for copy in early[1]:
                    copy.wait()
                for copy in tables_in + spectra(0) + left_loads(1) + right_loads(1):
                    copy.start()
            product(a, g, low, wide, slot)
            core_copy(i).start()
            if a < 2:
                step = 2 * g + (low > 0)
                if step == 2:
                    for copy in spectra(a):
                        copy.wait()
                if 2 <= step < 2 + pieces:
                    mix(step - 2)
        else:
            if a == 0 and low == 0:
                for copy in tables_in:
                    copy.wait()
                back[...] = back_table(pair, CH)
                turned[...] = back_table(pair, 0)
            filters(low, slot)
            core_copy(i).start()
            if low == 0:
                if a == 0:
                    for copy in spectra(1):
                        copy.start()
                for copy in left_loads(a + 1):
                    copy.wait()
                turn(a + 1)

    n = len(sent)
    by_y = lambda i: [u for u in sent[i][3] if not flows[u][3]]
    by_z = lambda i: [u for u in sent[i][3] if flows[u][3]]
    CORE, Y_DONE, HOP1, HOP2, DONE = 1, 3, 6, 9, 12
    for i in range(n + DONE):
        if i < n:
            compute(i)
        if 0 <= i - CORE < n:
            after_core(i - CORE)
            for u in by_z(i - CORE):
                hop(u, 0)
        if 0 <= i - Y_DONE < n:
            for u in by_z(i - Y_DONE):
                hop(u, 1)
            for u in by_y(i - Y_DONE):
                after_y(u)
                hop(u, 0)
        if 0 <= i - HOP1 < n:
            for u in by_z(i - HOP1):
                hop(u, 2)
            for u in by_y(i - HOP1):
                hop(u, 1)
        if 0 <= i - HOP2 < n:
            for u in by_z(i - HOP2):
                turn_to_y(u)
            for u in by_y(i - HOP2):
                hop(u, 2)
        if 0 <= i - DONE < n:
            finish(i - DONE)
        if i == 2:
            mini_copy(0).start()
        if i in (8, 14, 20, 26):
            k = (i - 8) // 6
            mini_copy(k).wait()
            total = mine[k] + got[k]
            if k < 3:
                mine[k + 1] = total
                mini_copy(k + 1).start()
            else:
                smallO[...] = total
    for i in (n - 2, n - 1):
        for copy in out_copies(i):
            copy.wait()


def exchange_call(small, pair, gdS, eS, nS, guS, ybS, goS, aS, gpS, s1S, g1S, s2S, g2S, ranks):
    T, D = aS.shape
    FF = eS.shape[1]
    pieces = T // CH
    per = D // ranks
    groups = per // 16
    blocks, sent, flows = exchange_plan(groups, D)
    n_blocks, n_sent, n_flows = len(blocks), len(sent), len(flows)
    Z, Y, rows = 4, 2, T // ranks
    V, S = pltpu.VMEM, pltpu.SemaphoreType.DMA
    shard = (rows, D)
    scratch = [
        V((3, Z, Y, 2, rows, D // 2), bf16),
        V((n_blocks, Z, Y) + shard, bf16),
        V((n_blocks, Z) + shard, bf16),
        V((n_blocks, Z - 1) + shard, bf16),
        V((n_blocks, Z - 1) + shard, bf16),
        V((n_blocks, Z - 1, Y, rows, 128), bf16),
        V((n_blocks, Z - 1, Y, rows, 128), bf16),
        V((n_blocks, rows, 128), bf16),
        V((2, T, FF), bf16),
        V((2, T, D), bf16),
        V((3, ranks, groups, 16, T), bf16),
        V((2,) + s1S.shape, bf16),
        V((pieces + 1, 2 * CH, D), bf16),
        V((2 * CH, 2 * CH), bf16),
        V((CH, 2 * CH), bf16),
        V((CH, 2 * CH), bf16),
        V((2, rows, D // 2), f32),
        V((4, small.shape[0], D), f32),
        V((4, small.shape[0], D), f32),
        S((26,)), S((8,)), S((2, n_sent)), S((2, n_flows)), S((2, n_flows, Z - 1)), S((2, n_flows, Z - 1)), S((2, 4)),
    ]
    out_shape = [
        jax.ShapeDtypeStruct(s, f32)
        for s in ((per, FF), (per, FF), (per, D), (per, 3 * D), (2, rows, D), (small.shape[0], D))
    ]
    return pl.pallas_call(
        functools.partial(exchange_kernel, pieces),
        out_shape=out_shape,
        in_specs=[VM] + [ANY] * 13,
        out_specs=[ANY] * 5 + [VM],
        scratch_shapes=scratch,
        compiler_params=pltpu.CompilerParams(vmem_limit_bytes=VMEM_LIMIT, collective_id=0, has_side_effects=True),
        cost_estimate=pl.CostEstimate(flops=2 * T * 12 * D * D, bytes_accessed=40 << 20, transcendentals=0),
        name="exchange",
    )(small, pair, gdS, eS, nS, guS, ybS, goS, aS, gpS, s1S, g1S, s2S, g2S)


def finish_kernel(ranks, stream, token_grad, inn, taps, out, up, down, small, *refs):
    outs, (gains, shifts, in_bias, taps_g, skips, out_bias, down_bias, up_bias) = refs[:7], refs[7:15]
    held, sem = refs[15:22], refs[22]
    given = (stream, token_grad, inn, taps, out, up, down)
    loads = [pltpu.make_async_copy(src, dst, sem.at[0, k]) for k, (src, dst) in enumerate(zip(given, held))]
    stores = [pltpu.make_async_copy(src, dst, sem.at[1, k]) for k, (src, dst) in enumerate(zip(held, outs))]
    for copy in loads:
        copy.start()
    D = small.shape[1]
    spot = lax.axis_index("dp")
    per, wide = gains.shape[1], up_bias.shape[1]
    turned = pltpu.roll(small[:UPB, :], lax.rem(D - spot * per, D), 1)
    for row, dst in ((GAIN, gains), (SHIFT, shifts), (SKIP, skips), (OUTB, out_bias), (DOWNB, down_bias)):
        dst[...] = turned[row : row + dst.shape[0], :per]
    for b in range(3):
        in_bias[b] = turned[INB + b : INB + b + 1, :per]
        for tap in range(3):
            taps_g[tap, b] = turned[TAP + 3 * tap + b : TAP + 3 * tap + b + 1, :per]
    row = small[pl.ds(UPB + spot * wide // D, 1), :]
    row = jnp.broadcast_to(row, (8, D))
    up_bias[...] = pltpu.roll(row, lax.rem(D - lax.rem(spot * wide, D), D), 1)[:1, :wide]
    for load, store in zip(loads, stores):
        load.wait()
        store.start()
    for store in stores:
        store.wait()


def finish_call(stream, token_grad, inn, taps, out, up, down, small, ranks):
    D = small.shape[1]
    given = (stream, token_grad, inn, taps, out, up, down)
    shapes = [jax.ShapeDtypeStruct(x.shape, x.dtype) for x in given]
    per = D // ranks
    for shape in ((2, per), (2, per), (3, 1, per), (3, 3, 1, per), (2, per), (1, per), (1, per), (1, up.shape[1] // ranks)):
        shapes.append(jax.ShapeDtypeStruct(shape, f32))
    return pl.pallas_call(
        functools.partial(finish_kernel, ranks),
        out_shape=shapes,
        in_specs=[ANY] * 7 + [VM],
        out_specs=[ANY] * 7 + [VM] * 8,
        scratch_shapes=[pltpu.VMEM(x.shape, x.dtype) for x in given] + [pltpu.SemaphoreType.DMA((2, 7))],
        compiler_params=pltpu.CompilerParams(vmem_limit_bytes=VMEM_LIMIT),
        name="place_results",
    )(*given, small)


def dot_rows(x, y):
    return lax.dot_general(x, y, (((0,), (0,)), ((), ())), preferred_element_type=f32).astype(bf16)


def body(
    tokens, cotangent, norm_gains, norm_shifts, in_weight, in_bias, short_taps, long_filter, skip_gains,
    out_weight, out_bias, up_weight, up_bias, down_weight, down_bias,
):
    count = lax.axis_size("section")
    ranks = lax.axis_size("dp")
    tok, cot = tokens[0], cotangent[0]
    T, D = tok.shape
    FF = up_weight.shape[2]
    pieces = T // CH
    pair = table()
    params = (
        norm_gains[0], norm_shifts[0], in_bias[0], short_taps[0], skip_gains[0], out_bias, down_bias, up_bias,
    )
    win, wout, wup, wdown, filt = in_weight[0], out_weight[0], up_weight[0], down_weight[0], long_filter[0]

    (stream, token_grad, aS, ybS, nS, eS, s1S, s2S, gdS, guS, goS, gpS, g1S, g2S, small) = pass_call(
        params, tok, cot, filt, win, wout, wup, wdown, pair, count
    )
    if ranks == 16 and D % (16 * ranks) == 0 and T == 64 * ranks and FF == 4 * D and pieces == 4:
        downT, up, out, inn, taps, small = exchange_call(
            small, pair, gdS, eS, nS, guS, ybS, goS, aS, gpS, s1S, g1S, s2S, g2S, ranks
        )
        stream, token_grad, inn, taps, out, up, downT, *smalls, up_bias_grad = finish_call(
            stream, token_grad, inn, taps, out, up, downT, small, ranks
        )
        gains, shifts, in_b, taps_g, skips, out_b, down_b = smalls
        in_b, taps_g = in_b.transpose(1, 0, 2), taps_g.transpose(2, 0, 1, 3)
    else:
        slab = jnp.concatenate([dot_rows(gdS, eS), dot_rows(nS, guS), dot_rows(ybS, goS), dot_rows(aS, gpS)], axis=1)
        taps = jnp.concatenate([filter_call(s1S, g1S, pair), filter_call(s2S, g2S, pair)], axis=1)
        small = jnp.sum(small, axis=1)
        per = D // ranks
        mini = jnp.concatenate(
            [small[:UPB].reshape(UPB, ranks, per).transpose(1, 0, 2).reshape(ranks, -1), small[UPB:].reshape(ranks, -1)], axis=1
        )
        scatter = lambda x: lax.psum_scatter(x, "dp", scatter_dimension=0, tiled=True).astype(f32)
        slab, taps, mini = scatter(slab), scatter(taps), scatter(mini)[0]
        head = mini[: UPB * per].reshape(UPB, per)
        up_bias_grad = mini[UPB * per :]
        taps = taps.reshape(-1, 2, D).transpose(1, 0, 2)
        downT, up, out, inn = (slab[:, i:j] for i, j in ((0, FF), (FF, 2 * FF), (2 * FF, 2 * FF + D), (2 * FF + D, None)))
        gains, shifts, skips = (head[k : k + 2] for k in (GAIN, SHIFT, SKIP))
        in_b, taps_g = head[INB : INB + 3][None], head[TAP : TAP + 9].reshape(1, 3, 3, per)
        out_b, down_b = head[OUTB][None], head[DOWNB][None]
    return (
        stream[None], token_grad[None], gains[None], shifts[None], inn[None], in_b, taps_g, taps[None], skips[None],
        out[None], out_b, up[None], up_bias_grad.reshape(1, -1), downT.T[None], down_b,
    )


def solution(mesh):
    whole = P("dp", None, None)
    split = lambda n: P("section", *([None] * n))
    return jax.shard_map(
        body,
        mesh=mesh,
        in_specs=(
            whole, whole, split(2), split(2), split(2), split(2), split(3), split(3), split(2), split(2), split(1),
            split(2), split(1), split(2), split(1),
        ),
        out_specs=(
            P("dp", "section", None),
            P("dp", "section", None),
            P("section", None, "dp"),
            P("section", None, "dp"),
            P("section", "dp", None),
            P("section", None, "dp"),
            P("section", None, None, "dp"),
            P("section", None, "dp", None),
            P("section", None, "dp"),
            P("section", "dp", None),
            P("section", "dp"),
            P("section", "dp", None),
            P("section", "dp"),
            P("section", None, "dp"),
            P("section", "dp"),
        ),
        check_vma=False,
    )
```

```python
import functools
import math

import jax
import jax.numpy as jnp
import ml_dtypes
import numpy as np
from jax import lax
from jax.experimental import pallas as pl
from jax.experimental.pallas import tpu as pltpu
from jax.sharding import PartitionSpec as P

CH = 256
FT = 512
CARRY = 8
f32, bf16 = jnp.float32, jnp.bfloat16
VMEM_LIMIT = 60 * 1024 * 1024
ANY = pl.BlockSpec(memory_space=pl.ANY)
SMEM = pl.BlockSpec(memory_space=pltpu.SMEM)
VM = pl.BlockSpec(memory_space=pltpu.VMEM)

GAIN, SHIFT, INB, TAP, SKIP, OUTB, DOWNB, UPB = 0, 2, 4, 7, 16, 18, 19, 20


def table():
    order = np.concatenate([np.arange(0, CH, 2), np.arange(1, CH, 2)])
    angle = np.pi * ((2 * order[:, None] + 1) * np.arange(CH)[None] % (4 * CH)) / (2 * CH)
    cos, sin = np.cos(angle), np.sin(angle)
    sign = np.where(order % 2 == 0, 1.0, -1.0)[:, None]
    spread = np.concatenate([cos, -sin], 0)
    turned = np.concatenate([sign * sin, sign * cos], 0)
    return jnp.asarray(np.concatenate([turned, spread], 1).astype(ml_dtypes.bfloat16))


def back_table(pair, at):
    return jnp.transpose(pair[:, at : at + CH].astype(f32) * (1.0 / CH)).astype(bf16)


def dot(x, y):
    return jnp.dot(x, y, preferred_element_type=f32)


def dot_nt(x, y):
    return lax.dot_general(x, y, (((1,), (1,)), ((), ())), preferred_element_type=f32)


def rows_at(index, size):
    return pl.ds(pl.multiple_of(index * size, size), size)


def for_rows(total, size, step, unroll=1):
    def run(i, carry):
        step(pl.multiple_of(i * size, size))
        return carry

    lax.fori_loop(0, total // size, run, 0, unroll=unroll)


def normalize(rows):
    average = jnp.mean(rows, axis=-1, keepdims=True)
    centered = rows - average
    scale = lax.rsqrt(jnp.mean(centered * centered, axis=-1, keepdims=True) + 1e-05)
    return centered * scale, scale


def norm_back(z, gain, unit, scale):
    w = z * gain
    return (
        w - jnp.mean(w, axis=-1, keepdims=True) - unit * jnp.mean(w * unit, axis=-1, keepdims=True)
    ) * scale


def gelu_pair(u):
    phi_sum = 0.5 + 0.5 * lax.erf(u * math.sqrt(0.5))
    bell = jnp.exp(-0.5 * (u * u))
    return u * phi_sum, phi_sum + u * (bell * (1.0 / math.sqrt(2.0 * math.pi)))


def mix_spectra(left, right, out, terms, conj):
    width = out.shape[1] // 2

    def tile(step, carry):
        r = pl.multiple_of(step * 16, 16)
        for half in range(2):
            cols = slice(half * width, (half + 1) * width)
            real = imag = None
            for i, j in terms:
                ar = left[i, pl.ds(r, 16), cols]
                ai = left[i, pl.ds(CH + r, 16), cols]
                br = right[j, pl.ds(r, 16), cols]
                bi = right[j, pl.ds(CH + r, 16), cols]
                if conj:
                    pr, pi = ar * br + ai * bi, ar * bi - ai * br
                else:
                    pr, pi = ar * br - ai * bi, ar * bi + ai * br
                real, imag = (pr, pi) if real is None else (real + pr, imag + pi)
            out[pl.ds(r, 16), cols] = real
            out[pl.ds(CH + r, 16), cols] = imag
        return carry

    lax.fori_loop(0, CH // 16, tile, 0, unroll=16)


def mix_units(left, right, out, terms, conj, plus):
    width = 256

    def unit(r, cols):
        real = imag = None
        if plus:
            real, imag = out[r : r + 16, cols], out[CH + r : CH + r + 16, cols]
        for i, j in terms:
            ar, ai = left[i, r : r + 16, cols], left[i, CH + r : CH + r + 16, cols]
            br, bi = right[j, r : r + 16, cols], right[j, CH + r : CH + r + 16, cols]
            if conj:
                pr, pi = ar * br + ai * bi, ar * bi - ai * br
            else:
                pr, pi = ar * br - ai * bi, ar * bi + ai * br
            real, imag = (pr, pi) if real is None else (real + pr, imag + pi)
        out[r : r + 16, cols] = real
        out[CH + r : CH + r + 16, cols] = imag

    return [
        functools.partial(unit, r, slice(c, c + width)) for c in range(0, out.shape[1], width) for r in range(0, CH, 16)
    ]


def run_skewed(stages, parts):
    for step in range(len(stages) + parts - 1):
        for p in range(parts):
            if 0 <= step - p < len(stages):
                stages[step - p](p)


def run_beside(steps, units):
    done = 0
    for k, step in enumerate(steps):
        step()
        upto = len(units) * (k + 1) // len(steps)
        for unit in units[done:upto]:
            unit()
        done = upto


def fold_rows(x):
    return jnp.sum(x.reshape(x.shape[0] // 8, 8, x.shape[1]), axis=0)


def pieces_of(at, wide, D):
    spans, off = [], 0
    while off < wide:
        row, col = (at + off) // D, (at + off) % D
        size = min(D - col, wide - off)
        spans.append((row, col, off, size))
        off += size
    return spans


def pass_kernel(
    sections, pieces, gains, shifts, inb_p, taps_p, skips, outb_p, downb_p, upb_p, tokens, cots, filt, win, wout, wup, wdown, pair_h,
    stream, gtok, aS, ybS, nS, eS, s1S, s2S, gdS, guS, goS, gpS, g1S, g2S, smallO,
    inf, inb, winb, woutb, wupb, wdownb, back, pair, k1, k2, sp1, sp2, pall, y1all, mall, dall,
    ab, lead, leadlow, part1, part2, wide, gate2, mid, nb, tile2, hid, outb, outfb, gnb, gqb, gpb, small,
    par, wsem, osem, fsem, bsem, ssem, gsem,
):
    rank = lax.axis_index("section")
    first, final = rank == 0, rank == sections - 1
    D, FF = woutb.shape[0], wupb.shape[1]
    tiles = FF // FT
    T = pieces * CH
    share = T // sections
    sub = min(CH, share)
    at = lambda r: {"section": r}

    def when(condition):
        return pl.when(condition)

    def remote(src, dst, send, recv, r):
        return pltpu.make_async_remote_copy(
            src_ref=src, dst_ref=dst, send_sem=send, recv_sem=recv, device_id=at(r), device_id_type=pl.DeviceIdType.MESH
        )

    def local(src, dst, sem):
        return pltpu.make_async_copy(src, dst, sem)

    loads = [
        local(win, winb, wsem.at[0]),
        local(wout, woutb, wsem.at[1]),
        local(wup, wupb, wsem.at[2]),
        local(wdown, wdownb, wsem.at[3]),
        local(pair_h, pair, wsem.at[4]),
    ]
    fill = [local(filt.at[f, pl.ds(0, CH)], sp.at[0, pl.ds(CH, CH)], wsem.at[7 + f]) for f, sp in enumerate((sp1, sp2))]
    for seg in range(1, pieces):
        window = pl.ds((seg - 1) * CH, 2 * CH)
        fill += [local(filt.at[f, window], sp.at[seg], wsem.at[7 + 2 * seg + f]) for f, sp in enumerate((sp1, sp2))]

    def own_chunk(src, dst, seg, sems):
        return local(src.at[rows_at(seg, CH)], dst.at[seg], sems.at[1, seg])

    def relay(src, dst, seg, sems, r):
        return remote(src, dst.at[seg], sems.at[0, seg], sems.at[1, seg], r)

    @when(first)
    def _():
        own_chunk(tokens, inf, 0, fsem).start()

    loads[4].start()
    for copy in fill[:2]:
        copy.start()
    loads[0].start()

    @when(first)
    def _():
        for seg in range(1, pieces):
            own_chunk(tokens, inf, seg, fsem).start()

    for copy in loads[1:4] + fill[2:]:
        copy.start()

    @when(final)
    def _():
        for seg in range(pieces):
            own_chunk(cots, inb, seg, bsem).start()

    for row, given in ((GAIN, gains), (SHIFT, shifts), (INB, inb_p), (SKIP, skips), (OUTB, outb_p), (DOWNB, downb_p)):
        par[row : row + given.shape[0], :] = given[...].astype(f32)
    for tap in range(3):
        par[TAP + 3 * tap : TAP + 3 * tap + 3, :] = taps_p[tap].astype(f32)
    for k in range(FF // D):
        par[UPB + k : UPB + k + 1, :] = upb_p[:, k * D : (k + 1) * D].astype(f32)

    barrier = pltpu.get_barrier_semaphore()
    for r in range(sections):

        @when(rank != r)
        def _(r=r):
            pl.semaphore_signal(barrier, inc=1, device_id=at(r), device_id_type=pl.DeviceIdType.MESH)

    if sections > 1:
        pl.semaphore_wait(barrier, sections - 1)

    pall[pl.ds(0, 16), :] = jnp.zeros((16, 3 * D), bf16)
    for sp in (sp1, sp2):
        sp[0, pl.ds(0, CH), :] = jnp.zeros((CH, D), bf16)
    small[...] = jnp.zeros(small.shape, f32)
    gqb[pl.ds(CH, CARRY), :] = jnp.zeros((CARRY, 3 * D), f32)

    def filter_spectra(seg):
        k1[seg] = dot(pair[...], sp1[seg]).astype(bf16)
        k2[seg] = dot(pair[...], sp2[seg]).astype(bf16)

    loads[4].wait()
    back[...] = back_table(pair, CH)
    for copy in fill[:2]:
        copy.wait()
    filter_spectra(0)

    @when(jnp.logical_not(first))
    def _():
        for copy in fill[2:]:
            copy.wait()

        def run(seg, carry):
            filter_spectra(seg)
            return carry

        lax.fori_loop(1, pieces, run, 0)

    def out_parts(seg, src, dst, sems, to_self):
        found = []
        for j in range(CH // sub):
            row = seg * CH + j * sub
            r, off = row // share, row % share
            found.append((r, off, j * sub, src.at[pl.ds(j * sub, sub)], sems.at[0, seg * (CH // sub) + j], off // sub))
        return found

    def put(src, dst, k):
        return local(src, dst, osem.at[k])

    def tile_steps(into, act, out):
        def begin(k):
            tile2[k % 2] = into(k)

        steps = [functools.partial(begin, 0)]
        for k in range(tiles):
            if k + 1 < tiles:
                steps.append(functools.partial(begin, k + 1))
            steps.append(functools.partial(act, k))
            if k >= 1:
                steps.append(functools.partial(out, k - 1))
        return steps + [functools.partial(out, tiles - 1)]

    def conv_stages(seg, sp, k, part, after, conj):
        per = CH // 16
        units = mix_units(k, sp, part, [(0, seg)], conj, True)

        def to(p):
            cols = slice(256 * p, 256 * p + 256)
            sp[seg, :, cols] = dot(pair[:, CH:], leadlow[:, cols]).astype(bf16)

        def mix(p):
            for unit in units[per * p : per * (p + 1)]:
                unit()

        def back_to(p):
            cols = slice(256 * p, 256 * p + 256)
            after(cols, dot(back[...], part[:, cols]))

        return [to, mix, back_to]

    def clear_parts():
        part1[...] = jnp.zeros(part1.shape, bf16)
        part2[...] = jnp.zeros(part2.shape, bf16)

    def forward_chunk(seg, carry):
        here = rows_at(seg, CH)
        base = pl.multiple_of(seg * CH, CH)
        hb = inf.at[seg]
        slot = 0
        later = seg > 0

        def before(copy):
            @when(later)
            def _():
                copy.wait()

        puts = [
            put(ab, aS.at[here], 0), put(sp1.at[seg], s1S.at[seg], 1), put(sp2.at[seg], s2S.at[seg], 2),
            put(leadlow, ybS.at[here], 3), put(nb, nS.at[here], 4), put(hid, eS.at[here], 5),
        ]

        @when(first)
        def _():
            own_chunk(tokens, inf, seg, fsem).wait()

        @when(jnp.logical_not(first))
        def _():
            relay(outb.at[slot], inf, seg, fsem, rank).wait_recv()

        before(puts[0])

        def ln1(r):
            unit, _ = normalize(hb[pl.ds(r, 32), :].astype(f32))
            ab[pl.ds(r, 32), :] = (unit * par[GAIN : GAIN + 1, :] + par[SHIFT : SHIFT + 1, :]).astype(bf16)

        for_rows(CH, 32, ln1, 8)
        puts[0].start()

        @when(seg == 0)
        def _():
            loads[0].wait()

        for b in range(3):
            cols = slice(b * D, (b + 1) * D)
            value = dot(ab[...], winb[:, cols]) + par[INB + b : INB + b + 1, :]
            pall[pl.ds(pl.multiple_of(base + 16, 16), CH), cols] = value.astype(bf16)

        before(puts[3])

        def short(r):
            got = [branch(base + r, b)[0] for b in range(3)]
            gate2[pl.ds(r, 32), :] = got[2]
            s = got[0] * got[1]
            lead[pl.ds(r, 32), :] = s
            leadlow[pl.ds(r, 32), :] = s.astype(bf16)

        ahead = first & (seg < pieces - 1)

        @when(ahead)
        def _():
            @when(seg == 0)
            def _():
                for copy in fill[2:]:
                    copy.wait()

            for_rows(CH, 32, short, 8)
            filter_spectra(seg + 1)

        @when(jnp.logical_not(ahead))
        def _():
            for_rows(CH, 32, short, 8)

        def second(cols, value):
            y = value + par[SKIP : SKIP + 1, cols] * lead[:, cols]
            y1all[seg, :, cols] = y.astype(bf16)
            trail = y * gate2[:, cols]
            lead[:, cols] = trail
            leadlow[:, cols] = trail.astype(bf16)

        def third(cols, value):
            leadlow[:, cols] = (value + par[SKIP + 1 : SKIP + 2, cols] * lead[:, cols]).astype(bf16)

        run_skewed(conv_stages(seg, sp1, k1, part1, second, False) + conv_stages(seg, sp2, k2, part2, third, False), D // 256)
        puts[1].start()
        puts[2].start()
        puts[3].start()

        @when(seg == 0)
        def _():
            loads[1].wait()

        wide[...] = dot(leadlow[...], woutb[...])
        before(puts[4])

        def ln2(r):
            rows = pl.ds(r, 32)
            m = hb[rows, :].astype(f32) + (wide[rows, :] + par[OUTB : OUTB + 1, :])
            mall[seg, rows, :] = m.astype(bf16)
            unit, _ = normalize(m)
            nb[rows, :] = (unit * par[GAIN + 1 : GAIN + 2, :] + par[SHIFT + 1 : SHIFT + 2, :]).astype(bf16)
            mid[rows, :] = m + par[DOWNB : DOWNB + 1, :]

        for_rows(CH, 32, ln2, 8)
        puts[4].start()

        @when(seg == 0)
        def _():
            loads[2].wait()
            loads[3].wait()

        before(puts[5])

        def up(k):
            return dot(nb[...], wupb[:, k * FT : (k + 1) * FT])

        def act(k):
            spans = pieces_of(k * FT, FT, D)
            bias = [par[UPB + row : UPB + row + 1, col : col + size] for row, col, _, size in spans]
            bias = bias[0] if len(bias) == 1 else jnp.concatenate(bias, axis=1)
            e, d = gelu_pair(tile2[k % 2] + bias)
            hid[:, k * FT : (k + 1) * FT] = e.astype(bf16)
            dall[seg, :, k * FT : (k + 1) * FT] = d.astype(bf16)

        def down(k):
            mid[...] += dot(hid[:, k * FT : (k + 1) * FT], wdownb[k * FT : (k + 1) * FT, :])

        for s in range(pieces):

            @when(seg == s)
            def _(s=s):
                terms = [(s + 1 - j, j) for j in range(s + 1)]
                units = []
                if s + 1 < pieces:
                    units = mix_units(k1, sp1, part1, terms, False, False) + mix_units(k2, sp2, part2, terms, False, False)
                run_beside(tile_steps(up, act, down), units)

        puts[5].start()

        @when(later)
        def _():
            finish_out(seg - 1, slot)

        outb[slot] = mid[...].astype(bf16)

        @when(jnp.logical_not(final))
        def _():
            relay(outb.at[slot], inf, seg, fsem, rank + 1).start()

        @when(final)
        def _():
            for r, off, inner, src, sem, k in out_parts(seg, outb.at[slot], stream, ssem, None):

                @when(r != rank)
                def _():
                    remote(src, stream.at[pl.ds(pl.multiple_of(off, sub), sub)], sem, ssem.at[1, k], r).start()

                @when(r == rank)
                def _():
                    local(src, stream.at[pl.ds(pl.multiple_of(off, sub), sub)], sem).start()

        return carry

    def finish_out(seg, slot):
        @when(jnp.logical_not(final))
        def _():
            relay(outb.at[slot], inf, seg, fsem, rank + 1).wait_send()

        @when(final)
        def _():
            for r, off, inner, src, sem, k in out_parts(seg, outb.at[slot], stream, ssem, None):

                @when(r != rank)
                def _():
                    remote(src, stream.at[pl.ds(pl.multiple_of(off, sub), sub)], sem, ssem.at[1, k], r).wait_send()

                @when(r == rank)
                def _():
                    local(src, stream.at[pl.ds(pl.multiple_of(off, sub), sub)], sem).wait()

    def branch(start, b):
        rows = pall[pl.ds(pl.multiple_of(start, 16), 48), b * D : (b + 1) * D].astype(f32)
        late = [rows[16 - i : 48 - i] for i in range(3)]
        t = [par[TAP + 3 * i + b : TAP + 3 * i + b + 1, :] for i in range(3)]
        return t[0] * late[0] + t[1] * late[1] + t[2] * late[2], late

    clear_parts()
    lax.fori_loop(0, pieces, forward_chunk, 0)
    last = pieces - 1
    here = rows_at(last, CH)
    for copy in (
        put(ab, aS.at[here], 0), put(sp1.at[last], s1S.at[last], 1), put(sp2.at[last], s2S.at[last], 2),
        put(leadlow, ybS.at[here], 3), put(nb, nS.at[here], 4), put(hid, eS.at[here], 5),
    ):
        copy.wait()
    for k in range(last):
        put(sp1.at[k], s1S.at[k], 1).wait()
        put(sp2.at[k], s2S.at[k], 2).wait()
    finish_out(last, 0)

    def add_small(k, x, cols=slice(None)):
        small[k, :, cols] += fold_rows(x)

    def backward_chunk(i, carry):
        seg = pieces - 1 - i
        here = rows_at(seg, CH)
        base = pl.multiple_of(seg * CH, CH)
        gdb, hb = inb.at[seg], inf.at[seg]
        slot = 0

        def before(copy):
            @when(i > 0)
            def _():
                copy.wait()

        puts = [
            put(gdb, gdS.at[here], 6), put(hid, guS.at[here], 7), put(nb, goS.at[here], 8), put(gpb, gpS.at[here], 9),
            put(sp2.at[seg], g2S.at[seg], 10), put(sp1.at[seg], g1S.at[seg], 11),
        ]

        @when(final)
        def _():
            own_chunk(cots, inb, seg, bsem).wait()

        @when(jnp.logical_not(final))
        def _():
            relay(outb.at[slot], inb, seg, bsem, rank).wait_recv()

        before(puts[0])
        puts[0].start()
        before(puts[1])

        def down(k):
            return dot_nt(gdb[...], wdownb[k * FT : (k + 1) * FT, :])

        def act(k):
            cols = slice(k * FT, (k + 1) * FT)
            gu = (dall[seg, :, cols].astype(f32) * tile2[k % 2]).astype(bf16)
            hid[:, cols] = gu
            total = fold_rows(gu.astype(f32))
            for row, col, off, size in pieces_of(k * FT, FT, D):
                small[UPB + row, :, col : col + size] += total[:, off : off + size]

        def up(k):
            part = dot_nt(hid[:, k * FT : (k + 1) * FT], wupb[:, k * FT : (k + 1) * FT])
            if k == 0:
                gnb[...] = part
            else:
                gnb[...] += part

        for s in range(pieces):

            @when(seg == s)
            def _(s=s):
                terms = [(j - s, j) for j in range(s + 1, pieces)]
                units = []
                if terms:
                    units = mix_units(k2, sp2, part2, terms, True, False) + mix_units(k1, sp1, part1, terms, True, False)
                run_beside(tile_steps(down, act, up), units)

        puts[1].start()
        before(puts[2])

        def ln2(r):
            rows = pl.ds(r, 32)
            unit, scale = normalize(mall[seg, rows, :].astype(f32))
            z = gnb[rows, :]
            gd = gdb[rows, :].astype(f32)
            gm = gd + norm_back(z, par[GAIN + 1 : GAIN + 2, :], unit, scale)
            mid[rows, :] = gm
            go = gm.astype(bf16)
            nb[rows, :] = go
            add_small(GAIN + 1, z * unit)
            add_small(SHIFT + 1, z)
            add_small(OUTB, go.astype(f32))
            add_small(DOWNB, gd)

        for_rows(CH, 32, ln2, 8)
        puts[2].start()
        gy = dot_nt(nb[...], woutb[...])
        lead[...] = gy
        leadlow[...] = gy.astype(bf16)
        sp2[seg] = dot(pair[:, CH:], leadlow[...]).astype(bf16)
        puts[4].start()
        for unit in mix_units(k2, sp2, part2, [(0, seg)], True, True):
            unit()
        wide[...] = dot(back[...], part2[...])

        def keep(r, b, grad, late):
            gqb[pl.ds(r, 32), b * D : (b + 1) * D] = grad
            for tap in range(3):
                add_small(TAP + 3 * tap + b, grad * late[tap])

        def second(r):
            rows = pl.ds(r, 32)
            gate, late = branch(base + r, 2)
            y1 = y1all[seg, rows, :].astype(f32)
            gy2 = lead[rows, :]
            gs2 = wide[rows, :] + par[SKIP + 1 : SKIP + 2, :] * gy2
            gy1 = gs2 * gate
            gate2[rows, :] = gy1
            leadlow[rows, :] = gy1.astype(bf16)
            add_small(SKIP + 1, gy2 * (y1 * gate))
            keep(r, 2, gs2 * y1, late)

        for_rows(CH, 32, second, 8)
        sp1[seg] = dot(pair[:, CH:], leadlow[...]).astype(bf16)
        puts[5].start()
        for unit in mix_units(k1, sp1, part1, [(0, seg)], True, True):
            unit()
        wide[...] = dot(back[...], part1[...])

        def lower(r):
            rows = pl.ds(r, 32)
            carrier, late_carrier = branch(base + r, 0)
            gate, late_gate = branch(base + r, 1)
            gy1 = gate2[rows, :]
            gs1 = wide[rows, :] + par[SKIP : SKIP + 1, :] * gy1
            add_small(SKIP, gy1 * (carrier * gate))
            keep(r, 0, gs1 * gate, late_carrier)
            keep(r, 1, gs1 * carrier, late_gate)

        for_rows(CH, 32, lower, 8)
        before(puts[3])

        def short(r):
            for b in range(3):
                cols = slice(b * D, (b + 1) * D)
                rows = gqb[pl.ds(r, 32 + CARRY), cols]
                t = [par[TAP + 3 * tap + b : TAP + 3 * tap + b + 1, :] for tap in range(3)]
                gp = (t[0] * rows[:32] + t[1] * rows[1:33] + t[2] * rows[2:34]).astype(bf16)
                gpb[pl.ds(r, 32), cols] = gp
                add_small(INB + b, gp.astype(f32))

        for_rows(CH, 32, short, 8)
        puts[3].start()
        gqb[pl.ds(CH, CARRY), :] = gqb[pl.ds(0, CARRY), :]
        gnb[...] = dot_nt(gpb[...], winb[...])

        @when(i > 0)
        def _():
            finish_grad(i - 1, slot)

        def ln1(r):
            rows = pl.ds(r, 32)
            unit, scale = normalize(hb[rows, :].astype(f32))
            z = gnb[rows, :]
            gh = mid[rows, :] + norm_back(z, par[GAIN : GAIN + 1, :], unit, scale)
            outfb[slot, rows, :] = gh
            outb[slot, rows, :] = gh.astype(bf16)
            add_small(GAIN, z * unit)
            add_small(SHIFT, z)

        for_rows(CH, 32, ln1, 8)

        @when(jnp.logical_not(first))
        def _():
            relay(outb.at[slot], inb, seg, bsem, rank - 1).start()

        @when(first)
        def _():
            for r, off, inner, src, sem, k in out_parts(seg, outb.at[slot], gtok, gsem, None):
                whole = outfb.at[slot, pl.ds(inner, sub)]

                @when(r != rank)
                def _():
                    remote(src, inf.at[seg, pl.ds(inner, sub)], sem, gsem.at[1, k], r).start()

                @when(r == rank)
                def _():
                    local(whole, gtok.at[pl.ds(pl.multiple_of(off, sub), sub)], sem).start()

        return carry

    def finish_grad(i, slot):
        seg = pieces - 1 - i

        @when(jnp.logical_not(first))
        def _():
            relay(outb.at[slot], inb, seg, bsem, rank - 1).wait_send()

        @when(first)
        def _():
            for r, off, inner, src, sem, k in out_parts(seg, outb.at[slot], gtok, gsem, None):
                whole = outfb.at[slot, pl.ds(inner, sub)]

                @when(r != rank)
                def _():
                    remote(src, inf.at[seg, pl.ds(inner, sub)], sem, gsem.at[1, k], r).wait_send()

                @when(r == rank)
                def _():
                    local(whole, gtok.at[pl.ds(pl.multiple_of(off, sub), sub)], sem).wait()

    clear_parts()
    lax.fori_loop(0, pieces, backward_chunk, 0)
    here = rows_at(0, CH)
    ends = [
        put(inb.at[0], gdS.at[here], 6), put(hid, guS.at[here], 7), put(nb, goS.at[here], 8), put(gpb, gpS.at[here], 9),
        put(sp2.at[0], g2S.at[0], 10), put(sp1.at[0], g1S.at[0], 11),
    ]
    for copy in ends:
        copy.wait()
    for k in range(last):
        ends[4].wait()
        ends[5].wait()
    total = put(small, smallO, 12)
    total.start()
    finish_grad(last, 0)
    parts = share // sub

    @when(jnp.logical_not(final))
    def _():
        for k in range(parts):
            remote(outb.at[0, pl.ds(0, sub)], stream.at[pl.ds(k * sub, sub)], ssem.at[0, 0], ssem.at[1, k], rank).wait_recv()

    @when(jnp.logical_not(first))
    def _():
        for k in range(parts):
            row = rank * share + k * sub
            landed = inf.at[row // CH, pl.ds(pl.multiple_of(row % CH, sub), sub)]
            remote(outb.at[0, pl.ds(0, sub)], landed, gsem.at[0, 0], gsem.at[1, k], rank).wait_recv()
            outfb[0, pl.ds(0, sub), :] = landed[...].astype(f32)
            copy = local(outfb.at[0, pl.ds(0, sub)], gtok.at[pl.ds(k * sub, sub)], gsem.at[0, k])
            copy.start()
            copy.wait()

    total.wait()


def pass_call(params, tokens, cots, filt, win, wout, wup, wdown, pair, sections):
    T, D = tokens.shape
    FF = wup.shape[1]
    pieces = T // CH
    share = T // sections
    sub = min(CH, share)
    spec3 = (pieces, 2 * CH, D)
    small = (UPB + FF // D, 8, D)
    shapes = [
        ((share, D), bf16), ((share, D), f32),
        ((T, D), bf16), ((T, D), bf16), ((T, D), bf16), ((T, FF), bf16), (spec3, bf16), (spec3, bf16),
        ((T, D), bf16), ((T, FF), bf16), ((T, D), bf16), ((T, 3 * D), bf16), (spec3, bf16), (spec3, bf16),
        (small, f32),
    ]
    V, S = pltpu.VMEM, pltpu.SemaphoreType.DMA
    chunk, chunks = (CH, D), (pieces, CH, D)
    scratch = [
        V(chunks, bf16), V(chunks, bf16),
        V(win.shape, bf16), V(wout.shape, bf16), V(wup.shape, bf16), V(wdown.shape, bf16),
        V((CH, 2 * CH), bf16), V((2 * CH, 2 * CH), bf16),
        V(spec3, bf16), V(spec3, bf16), V(spec3, bf16), V(spec3, bf16),
        V((16 + T, 3 * D), bf16), V(chunks, bf16), V(chunks, bf16), V((pieces, CH, FF), bf16),
        V(chunk, bf16), V(chunk, f32), V(chunk, bf16), V((2 * CH, D), bf16), V((2 * CH, D), bf16), V(chunk, f32), V(chunk, f32),
        V(chunk, f32),
        V(chunk, bf16), V((2, CH, FT), f32), V((CH, FF), bf16), V((1,) + chunk, bf16), V((1,) + chunk, f32),
        V(chunk, f32), V((CH + CARRY, 3 * D), f32), V((CH, 3 * D), bf16), V(small, f32), V((UPB + FF // D, D), f32),
        S((7 + 2 * pieces,)), S((13,)), S((2, pieces)), S((2, pieces)), S((2, T // sub)), S((2, T // sub)),
    ]
    return pl.pallas_call(
        functools.partial(pass_kernel, sections, pieces),
        out_shape=[jax.ShapeDtypeStruct(*s) for s in shapes],
        in_specs=[VM] * 8 + [ANY] * 8,
        out_specs=[ANY] * len(shapes),
        scratch_shapes=scratch,
        compiler_params=pltpu.CompilerParams(vmem_limit_bytes=63 * 1024 * 1024, collective_id=1, has_side_effects=True),
        name="layer_pass",
    )(*params, tokens, cots, filt, win, wout, wup, wdown, pair)


def filter_kernel(pieces, s, g, back, turned, out, q):
    for d in range(pieces):
        mix_spectra(s, g, q.at[d], [(j - d, j) for j in range(d, pieces)], True)
    for d in range(pieces):
        rows = dot(back[...], q[d])
        if d + 1 < pieces:
            rows += dot(turned[...], q[d + 1])
        out[pl.ds(d * CH, CH), :] = rows.astype(bf16)


def filter_call(s, g, pair):
    pieces, _, D = s.shape
    turned, back = ((pair[:, k : k + CH].astype(f32) / CH).astype(bf16).T for k in (0, CH))
    return pl.pallas_call(
        functools.partial(filter_kernel, pieces),
        out_shape=jax.ShapeDtypeStruct((pieces * CH, D), bf16),
        in_specs=[VM] * 4,
        out_specs=VM,
        scratch_shapes=[pltpu.VMEM(s.shape, bf16)],
        compiler_params=pltpu.CompilerParams(vmem_limit_bytes=VMEM_LIMIT),
        name="filter_grad",
    )(s, g, back, turned)


def exchange_plan(groups, D):
    blocks = [("product", 0, g) for g in range(groups)] + [("filter", 0, 0)]
    blocks += [("product", 1, g) for g in range(groups)] + [("filter", 1, 0)]
    blocks += [("product", 2, g) for g in range(groups)]
    half = D // 2
    sent, flows = [], []
    for b in range(len(blocks)):
        spans = [(0, [(0, half, False)]), (half, [(half, half - 128, False), (D - 128, 128, True)])]
        if b == len(blocks) - 1:
            spans = [spans[1], (0, [(0, half - 128, False)]), (half - 128, [(half - 128, 128, False)])]
        for low, parts in spans:
            wide = sum(part[1] for part in parts)
            sent.append((b, low, wide, list(range(len(flows), len(flows) + len(parts)))))
            flows += [(b,) + part for part in parts]
    return blocks, sent, flows


def exchange_kernel(
    pieces, small_in, pair_h, gdS, eS, nS, guS, ybS, goS, aS, gpS, s1S, g1S, s2S, g2S,
    downT, upO, outO, inO, filtO, smallO,
    x, r1, r2, rr, rl, rrz, rlz, r2z, gb, lb, lt, sb, qb, pair, back, turned, ob, mine, got,
    lsem, osem, csem, ysem, rsem, fsem, msem,
):
    D = lb.shape[2]
    half = D // 2
    me = lax.axis_index("dp")
    c, y, z = me % 2, (me // 2) % 2, me // 4
    Z = r2.shape[1]
    groups = lt.shape[2]
    blocks, sent, flows = exchange_plan(groups, D)
    at = lambda i: {"dp": i}
    core_id, y_id = me + 1 - 2 * c, me + 2 - 4 * y
    mates = (core_id, y_id, me + 4 - 8 * (z % 2), me + 8 - 16 * (z // 2))
    inner = (z == 1) | (z == 2)

    def remote(src, dst, send, recv, mate):
        return pltpu.make_async_remote_copy(
            src_ref=src, dst_ref=dst, send_sem=send, recv_sem=recv, device_id=at(mate),
            device_id_type=pl.DeviceIdType.MESH,
        )

    def load(src, dst, k):
        return pltpu.make_async_copy(src, dst, lsem.at[k])

    rights = ((eS,), (guS,), (goS, gpS))
    lefts = ((gdS,), (nS,), (ybS, aS))
    turned_at = ((0,), (1,), (0, 2))

    def right_loads(m):
        found, off = [], 0
        for k, src in enumerate(rights[m]):
            wide = src.shape[1]
            found.append(load(src, gb.at[m % 2, :, pl.ds(off, wide)], 4 * m + k))
            off += wide
        return found

    def left_loads(m):
        return [load(src, lb.at[k], 4 * m + 2 + k) for k, src in enumerate(lefts[m])]

    def spectra(f):
        src = ((s1S, g1S), (s2S, g2S))[f]
        return [load(src[k], sb.at[k], 12 + 2 * f + k) for k in range(2)]

    def turn(m):
        for k, spot in enumerate(turned_at[m]):

            def part(i, carry, k=k, spot=spot):
                rows = pl.multiple_of(i * 128, 128)
                piece = jnp.transpose(lb[k, pl.ds(rows, 128), :])
                lt[spot, :, :, :, pl.ds(rows, 128)] = piece.reshape(lt.shape[1:4] + (128,))
                return carry

            lax.fori_loop(0, lb.shape[1] // 128, part, 0)

    def product(m, g, low, wide, slot):
        def part(i, carry):
            k = jnp.where(i == 0, 0, 2) if m == 2 else m
            left = lt[k, :, g].reshape(16 * lt.shape[1], lt.shape[4])
            cols = pl.ds(pl.multiple_of(i * D + low, 128), wide)
            value = dot(left, gb[m % 2, :, cols]).astype(bf16)
            x[slot, :, :, :, pl.ds(pl.multiple_of(i * 16, 16), 16), :wide] = value.reshape(x.shape[1:4] + (16, wide))
            return carry

        lax.fori_loop(0, 4, part, 0)

    def mix(d):
        mix_spectra(sb.at[0], sb.at[1], qb.at[d], [(j - d, j) for j in range(d, pieces)], True)

    def filters(low, slot):
        cols = slice(low, low + half)

        def part(d, carry):
            rows = dot(back[...], qb[d, :, cols]) + dot(turned[...], qb[d + 1, :, cols])
            x[slot, d] = rows.astype(bf16).reshape(x.shape[2:])
            return carry

        lax.fori_loop(0, pieces, part, 0)

    def core_copy(i):
        b, low, wide, _ = sent[i]
        return remote(
            x.at[i % x.shape[0], :, :, 1 - c, :, pl.ds(0, wide)], r1.at[b, :, :, :, pl.ds(low, wide)],
            csem.at[0, i], csem.at[1, i], core_id,
        )

    def add(p, q):
        return (p.astype(f32) + q.astype(f32)).astype(bf16)

    def by_rows(refs, step):
        lead = refs[0].shape[:-2]

        def run(i, carry):
            tile = pl.ds(pl.multiple_of(i * 16, 16), 16)
            for y_at in range(lead[0]) if lead else (None,):
                step(tile, [ref.at[tile] if y_at is None else ref.at[y_at, tile] for ref in refs], y_at)
            return carry

        lax.fori_loop(0, refs[0].shape[-2] // 16, run, 0)

    def add_into(dst, src):
        def step(tile, views, y_at):
            views[0][...] = add(views[0][...], views[1][...])

        by_rows([dst, src], step)

    def after_core(i):
        b, low, wide, mine_flows = sent[i]
        core_copy(i).wait()
        cols = slice(low, low + wide)

        def part(k, carry):
            for j in range(2):
                r1[b, k, j, :, cols] = add(r1[b, k, j, :, cols], x[i % x.shape[0], k, j, c, :, :wide])
            return carry

        lax.fori_loop(0, Z, part, 0)
        for u in mine_flows:
            if not flows[u][3]:
                y_copy(u).start()

    def y_copy(u):
        b, low, wide, z_first = flows[u]
        cols = pl.ds(low, wide)
        if z_first:
            return remote(r1.at[b, z, 1 - y, :, cols], r2z.at[b], ysem.at[0, u], ysem.at[1, u], y_id)
        return remote(r1.at[b, :, 1 - y, :, cols], r2.at[b, :, :, cols], ysem.at[0, u], ysem.at[1, u], y_id)

    def after_y(u):
        b, low, wide, _ = flows[u]
        cols = slice(low, low + wide)
        y_copy(u).wait()

        def part(k, carry):
            r2[b, k, :, cols] = add(r2[b, k, :, cols], r1[b, k, y, :, cols])
            return carry

        lax.fori_loop(0, Z, part, 0)

    def own(u, d):
        b, low, wide, z_first = flows[u]
        cols = pl.ds(low, wide)
        return r1.at[b, d, :, :, cols] if z_first else r2.at[b, d, :, cols]

    def right_at(u, d):
        b, low, wide, z_first = flows[u]
        return rrz.at[b, d - 1] if z_first else rr.at[b, d - 1, :, pl.ds(low, wide)]

    def left_at(u, d):
        b, low, wide, z_first = flows[u]
        return rlz.at[b, d] if z_first else rl.at[b, d, :, pl.ds(low, wide)]

    def right_copy(u, d, src):
        return remote(src, right_at(u, d), rsem.at[0, u, d - 1], rsem.at[1, u, d - 1], me + 4)

    def left_copy(u, d, src):
        return remote(src, left_at(u, d), fsem.at[0, u, d], fsem.at[1, u, d], me - 4)

    def hop(u, h):
        @pl.when(z == h)
        def _():
            for d in range(Z - 1, h, -1):
                src = own(u, d)
                if h > 0:
                    right_copy(u, d, src).wait_recv()
                    src = right_at(u, d)
                    add_into(src, own(u, d))
                right_copy(u, d, src).start()

        @pl.when(z == Z - 1 - h)
        def _():
            for d in range(Z - 1 - h):
                src = own(u, d)
                if h > 0:
                    left_copy(u, d, src).wait_recv()
                    src = left_at(u, d)
                    add_into(src, own(u, d))
                left_copy(u, d, src).start()

    def gather(u, store):
        for p in range(Z):

            @pl.when(z == p)
            def _(p=p):
                parts = [own(u, p)]
                if p > 0:
                    right_copy(u, p, own(u, p)).wait_recv()
                    parts.append(right_at(u, p))
                if p < Z - 1:
                    left_copy(u, p, own(u, p)).wait_recv()
                    parts.append(left_at(u, p))

                def step(tile, views, y_at):
                    total = views[0][...].astype(f32)
                    for view in views[1:]:
                        total += view[...].astype(f32)
                    store(p, tile, y_at, total)

                by_rows(parts, step)
                for d in range(p + 1, Z):
                    right_copy(u, d, own(u, d)).wait_send()
                for d in range(p):
                    left_copy(u, d, own(u, d)).wait_send()

    def turn_to_y(u):
        def store(p, tile, y_at, total):
            own(u, p).at[y_at, tile][...] = total.astype(bf16)

        gather(u, store)
        y_copy(u).start()

    def out_copies(i):
        b, low, wide, _ = sent[i]
        kind, a, g = blocks[b]
        slot = i % 2
        if kind == "filter":
            src = ob.at[slot, :, pl.ds(0, wide)]
            return [pltpu.make_async_copy(src, filtO.at[a, :, pl.ds(low, wide)], osem.at[4 * slot])]
        found = []
        rows = pl.ds(g * 16, 16)
        for k in range(4):
            if a < 2:
                dst = (downT, upO)[a].at[rows, pl.ds(k * D + low, wide)]
            elif k == 0:
                dst = outO.at[rows, pl.ds(low, wide)]
            else:
                dst = inO.at[rows, pl.ds((k - 1) * D + low, wide)]
            src = ob.at[slot, pl.ds(16 * k, 16), pl.ds(0, wide)]
            found.append(pltpu.make_async_copy(src, dst, osem.at[4 * slot + k]))
        return found

    def finish(i):
        b, low, _, mine_flows = sent[i]
        slot = i % 2
        if i >= 2:
            for copy in out_copies(i - 2):
                copy.wait()
        for u in mine_flows:
            _, first, wide, z_first = flows[u]
            cols = slice(first - low, first - low + wide)
            if z_first:
                y_copy(u).wait()
                ob[slot, :, cols] = r1[b, z, y, :, first : first + wide].astype(f32) + r2z[b].astype(f32)
            else:

                def store(p, tile, y_at, total, cols=cols):
                    ob[slot, tile, cols] = total

                gather(u, store)
        for copy in out_copies(i):
            copy.start()

    def mini_copy(k):
        return remote(mine.at[k], got.at[k], msem.at[0, k], msem.at[1, k], mates[k])

    tables_in = [load(pair_h, pair, 16)]
    early = [
        [load(eS.at[:, pl.ds(k * D + low, half)], gb.at[0, :, pl.ds(k * D + low, half)], 18 + 4 * (low > 0) + k) for k in range(4)]
        for low in (0, half)
    ]
    for copy in left_loads(0) + early[0] + early[1]:
        copy.start()
    barrier = pltpu.get_barrier_semaphore()
    for mate in mates:
        pl.semaphore_signal(barrier, inc=1, device_id=at(mate), device_id_type=pl.DeviceIdType.MESH)

    @pl.when(inner)
    def _():
        other = me + 12 - 8 * z
        pl.semaphore_signal(barrier, inc=1, device_id=at(other), device_id_type=pl.DeviceIdType.MESH)

    @pl.when(inner)
    def _():
        pl.semaphore_wait(barrier, len(mates) + 1)

    @pl.when(jnp.logical_not(inner))
    def _():
        pl.semaphore_wait(barrier, len(mates))

    mine[0] = jnp.sum(small_in[...], axis=1)
    qb[pieces] = jnp.zeros(qb.shape[1:], bf16)

    def compute(i):
        b, low, wide, _ = sent[i]
        kind, a, g = blocks[b]
        slot = i % x.shape[0]
        if kind == "product":
            if g == 0 and low == 0:
                if a == 0:
                    for copy in left_loads(0):
                        copy.wait()
                    turn(0)
                for copy in early[0] if a == 0 else right_loads(a):
                    copy.wait()
                if a == 1:
                    for copy in left_loads(a + 1) + right_loads(a + 1):
                        copy.start()
            if a == 0 and g == 0 and low > 0:
                for copy in early[1]:
                    copy.wait()
                for copy in tables_in + spectra(0) + left_loads(1) + right_loads(1):
                    copy.start()
            product(a, g, low, wide, slot)
            core_copy(i).start()
            if a < 2:
                step = 2 * g + (low > 0)
                if step == 2:
                    for copy in spectra(a):
                        copy.wait()
                if 2 <= step < 2 + pieces:
                    mix(step - 2)
        else:
            if a == 0 and low == 0:
                for copy in tables_in:
                    copy.wait()
                back[...] = back_table(pair, CH)
                turned[...] = back_table(pair, 0)
            filters(low, slot)
            core_copy(i).start()
            if low == 0:
                if a == 0:
                    for copy in spectra(1):
                        copy.start()
                for copy in left_loads(a + 1):
                    copy.wait()
                turn(a + 1)

    n = len(sent)
    by_y = lambda i: [u for u in sent[i][3] if not flows[u][3]]
    by_z = lambda i: [u for u in sent[i][3] if flows[u][3]]
    CORE, Y_DONE, HOP1, HOP2, DONE = 1, 3, 6, 9, 12
    for i in range(n + DONE):
        if i < n:
            compute(i)
        if 0 <= i - CORE < n:
            after_core(i - CORE)
            for u in by_z(i - CORE):
                hop(u, 0)
        if 0 <= i - Y_DONE < n:
            for u in by_z(i - Y_DONE):
                hop(u, 1)
            for u in by_y(i - Y_DONE):
                after_y(u)
                hop(u, 0)
        if 0 <= i - HOP1 < n:
            for u in by_z(i - HOP1):
                hop(u, 2)
            for u in by_y(i - HOP1):
                hop(u, 1)
        if 0 <= i - HOP2 < n:
            for u in by_z(i - HOP2):
                turn_to_y(u)
            for u in by_y(i - HOP2):
                hop(u, 2)
        if 0 <= i - DONE < n:
            finish(i - DONE)
        if i == 2:
            mini_copy(0).start()
        if i in (8, 14, 20, 26):
            k = (i - 8) // 6
            mini_copy(k).wait()
            total = mine[k] + got[k]
            if k < 3:
                mine[k + 1] = total
                mini_copy(k + 1).start()
            else:
                smallO[...] = total
    for i in (n - 2, n - 1):
        for copy in out_copies(i):
            copy.wait()


def exchange_call(small, pair, gdS, eS, nS, guS, ybS, goS, aS, gpS, s1S, g1S, s2S, g2S, ranks):
    T, D = aS.shape
    FF = eS.shape[1]
    pieces = T // CH
    per = D // ranks
    groups = per // 16
    blocks, sent, flows = exchange_plan(groups, D)
    n_blocks, n_sent, n_flows = len(blocks), len(sent), len(flows)
    Z, Y, rows = 4, 2, T // ranks
    V, S = pltpu.VMEM, pltpu.SemaphoreType.DMA
    shard = (rows, D)
    scratch = [
        V((3, Z, Y, 2, rows, D // 2), bf16),
        V((n_blocks, Z, Y) + shard, bf16),
        V((n_blocks, Z) + shard, bf16),
        V((n_blocks, Z - 1) + shard, bf16),
        V((n_blocks, Z - 1) + shard, bf16),
        V((n_blocks, Z - 1, Y, rows, 128), bf16),
        V((n_blocks, Z - 1, Y, rows, 128), bf16),
        V((n_blocks, rows, 128), bf16),
        V((2, T, FF), bf16),
        V((2, T, D), bf16),
        V((3, ranks, groups, 16, T), bf16),
        V((2,) + s1S.shape, bf16),
        V((pieces + 1, 2 * CH, D), bf16),
        V((2 * CH, 2 * CH), bf16),
        V((CH, 2 * CH), bf16),
        V((CH, 2 * CH), bf16),
        V((2, rows, D // 2), f32),
        V((4, small.shape[0], D), f32),
        V((4, small.shape[0], D), f32),
        S((26,)), S((8,)), S((2, n_sent)), S((2, n_flows)), S((2, n_flows, Z - 1)), S((2, n_flows, Z - 1)), S((2, 4)),
    ]
    out_shape = [
        jax.ShapeDtypeStruct(s, f32)
        for s in ((per, FF), (per, FF), (per, D), (per, 3 * D), (2, rows, D), (small.shape[0], D))
    ]
    return pl.pallas_call(
        functools.partial(exchange_kernel, pieces),
        out_shape=out_shape,
        in_specs=[VM] + [ANY] * 13,
        out_specs=[ANY] * 5 + [VM],
        scratch_shapes=scratch,
        compiler_params=pltpu.CompilerParams(vmem_limit_bytes=VMEM_LIMIT, collective_id=0, has_side_effects=True),
        cost_estimate=pl.CostEstimate(flops=2 * T * 12 * D * D, bytes_accessed=40 << 20, transcendentals=0),
        name="exchange",
    )(small, pair, gdS, eS, nS, guS, ybS, goS, aS, gpS, s1S, g1S, s2S, g2S)


def finish_kernel(ranks, stream, token_grad, inn, taps, out, up, down, small, *refs):
    outs, (gains, shifts, in_bias, taps_g, skips, out_bias, down_bias, up_bias) = refs[:7], refs[7:15]
    held, sem = refs[15:22], refs[22]
    given = (stream, token_grad, inn, taps, out, up, down)
    loads = [pltpu.make_async_copy(src, dst, sem.at[0, k]) for k, (src, dst) in enumerate(zip(given, held))]
    stores = [pltpu.make_async_copy(src, dst, sem.at[1, k]) for k, (src, dst) in enumerate(zip(held, outs))]
    for copy in loads:
        copy.start()
    D = small.shape[1]
    spot = lax.axis_index("dp")
    per, wide = gains.shape[1], up_bias.shape[1]
    turned = pltpu.roll(small[:UPB, :], lax.rem(D - spot * per, D), 1)
    for row, dst in ((GAIN, gains), (SHIFT, shifts), (SKIP, skips), (OUTB, out_bias), (DOWNB, down_bias)):
        dst[...] = turned[row : row + dst.shape[0], :per]
    for b in range(3):
        in_bias[b] = turned[INB + b : INB + b + 1, :per]
        for tap in range(3):
            taps_g[tap, b] = turned[TAP + 3 * tap + b : TAP + 3 * tap + b + 1, :per]
    row = small[pl.ds(UPB + spot * wide // D, 1), :]
    row = jnp.broadcast_to(row, (8, D))
    up_bias[...] = pltpu.roll(row, lax.rem(D - lax.rem(spot * wide, D), D), 1)[:1, :wide]
    for load, store in zip(loads, stores):
        load.wait()
        store.start()
    for store in stores:
        store.wait()


def finish_call(stream, token_grad, inn, taps, out, up, down, small, ranks):
    D = small.shape[1]
    given = (stream, token_grad, inn, taps, out, up, down)
    shapes = [jax.ShapeDtypeStruct(x.shape, x.dtype) for x in given]
    per = D // ranks
    for shape in ((2, per), (2, per), (3, 1, per), (3, 3, 1, per), (2, per), (1, per), (1, per), (1, up.shape[1] // ranks)):
        shapes.append(jax.ShapeDtypeStruct(shape, f32))
    return pl.pallas_call(
        functools.partial(finish_kernel, ranks),
        out_shape=shapes,
        in_specs=[ANY] * 7 + [VM],
        out_specs=[ANY] * 7 + [VM] * 8,
        scratch_shapes=[pltpu.VMEM(x.shape, x.dtype) for x in given] + [pltpu.SemaphoreType.DMA((2, 7))],
        compiler_params=pltpu.CompilerParams(vmem_limit_bytes=VMEM_LIMIT),
        name="place_results",
    )(*given, small)


def dot_rows(x, y):
    return lax.dot_general(x, y, (((0,), (0,)), ((), ())), preferred_element_type=f32).astype(bf16)


def body(
    tokens, cotangent, norm_gains, norm_shifts, in_weight, in_bias, short_taps, long_filter, skip_gains,
    out_weight, out_bias, up_weight, up_bias, down_weight, down_bias,
):
    count = lax.axis_size("section")
    ranks = lax.axis_size("dp")
    tok, cot = tokens[0], cotangent[0]
    T, D = tok.shape
    FF = up_weight.shape[2]
    pieces = T // CH
    pair = table()
    params = (
        norm_gains[0], norm_shifts[0], in_bias[0], short_taps[0], skip_gains[0], out_bias, down_bias, up_bias,
    )
    win, wout, wup, wdown, filt = in_weight[0], out_weight[0], up_weight[0], down_weight[0], long_filter[0]

    (stream, token_grad, aS, ybS, nS, eS, s1S, s2S, gdS, guS, goS, gpS, g1S, g2S, small) = pass_call(
        params, tok, cot, filt, win, wout, wup, wdown, pair, count
    )
    if ranks == 16 and D % (16 * ranks) == 0 and T == 64 * ranks and FF == 4 * D and pieces == 4:
        downT, up, out, inn, taps, small = exchange_call(
            small, pair, gdS, eS, nS, guS, ybS, goS, aS, gpS, s1S, g1S, s2S, g2S, ranks
        )
        stream, token_grad, inn, taps, out, up, downT, *smalls, up_bias_grad = finish_call(
            stream, token_grad, inn, taps, out, up, downT, small, ranks
        )
        gains, shifts, in_b, taps_g, skips, out_b, down_b = smalls
        in_b, taps_g = in_b.transpose(1, 0, 2), taps_g.transpose(2, 0, 1, 3)
    else:
        slab = jnp.concatenate([dot_rows(gdS, eS), dot_rows(nS, guS), dot_rows(ybS, goS), dot_rows(aS, gpS)], axis=1)
        taps = jnp.concatenate([filter_call(s1S, g1S, pair), filter_call(s2S, g2S, pair)], axis=1)
        small = jnp.sum(small, axis=1)
        per = D // ranks
        mini = jnp.concatenate(
            [small[:UPB].reshape(UPB, ranks, per).transpose(1, 0, 2).reshape(ranks, -1), small[UPB:].reshape(ranks, -1)], axis=1
        )
        scatter = lambda x: lax.psum_scatter(x, "dp", scatter_dimension=0, tiled=True).astype(f32)
        slab, taps, mini = scatter(slab), scatter(taps), scatter(mini)[0]
        head = mini[: UPB * per].reshape(UPB, per)
        up_bias_grad = mini[UPB * per :]
        taps = taps.reshape(-1, 2, D).transpose(1, 0, 2)
        downT, up, out, inn = (slab[:, i:j] for i, j in ((0, FF), (FF, 2 * FF), (2 * FF, 2 * FF + D), (2 * FF + D, None)))
        gains, shifts, skips = (head[k : k + 2] for k in (GAIN, SHIFT, SKIP))
        in_b, taps_g = head[INB : INB + 3][None], head[TAP : TAP + 9].reshape(1, 3, 3, per)
        out_b, down_b = head[OUTB][None], head[DOWNB][None]
    return (
        stream[None], token_grad[None], gains[None], shifts[None], inn[None], in_b, taps_g, taps[None], skips[None],
        out[None], out_b, up[None], up_bias_grad.reshape(1, -1), downT.T[None], down_b,
    )


def solution(mesh):
    whole = P("dp", None, None)
    split = lambda n: P("section", *([None] * n))
    return jax.shard_map(
        body,
        mesh=mesh,
        in_specs=(
            whole, whole, split(2), split(2), split(2), split(2), split(3), split(3), split(2), split(2), split(1),
            split(2), split(1), split(2), split(1),
        ),
        out_specs=(
            P("dp", "section", None),
            P("dp", "section", None),
            P("section", None, "dp"),
            P("section", None, "dp"),
            P("section", "dp", None),
            P("section", None, "dp"),
            P("section", None, None, "dp"),
            P("section", None, "dp", None),
            P("section", None, "dp"),
            P("section", "dp", None),
            P("section", "dp"),
            P("section", "dp", None),
            P("section", "dp"),
            P("section", None, "dp"),
            P("section", "dp"),
        ),
        check_vma=False,
    )
```
